32 devices in a mesh: dp: 8 (over z, core), fs: 4 (over y, x).
Axes of the slice: x: 2, y: 2, z: 4, core: 2. Of those that a mesh axis runs over, the one named last changes fastest.
Arguments:
- tokens: bfloat16 [4096, 1024], P(('dp', 'fs')), may hold values from -6 to 6
- attend_weight: bfloat16 [3, 1024, 1024], P(None, 'dp', 'fs'), may hold values from -0.1875 to 0.1875
- attend_bias: bfloat16 [2, 16, 64], P(None, 'fs', 'dp'), may hold values from -3 to 3
- output_weight: bfloat16 [1024, 1024], P('fs', 'dp'), may hold values from -1 to 1
- expand_weight: bfloat16 [1024, 4096], P('dp', 'fs'), may hold values from -0.1875 to 0.1875
- expand_bias: bfloat16 [4, 1024], P('fs', 'dp'), may hold values from -3 to 3
- contract_weight: bfloat16 [4096, 1024], P('fs', 'dp'), may hold values from -0.09375 to 0.09375
- layer_vectors: bfloat16 [6, 1024], P(None, ('dp', 'fs')), may hold values from -2 to 2
- sequence_lengths: int32 [64], replicated, may hold values from 16 to 128, as said below
- sequence_owner: int32 [64], replicated, may hold values from 0 to 31, as said below
- output_grad: bfloat16 [4096, 1024], P(('dp', 'fs')), may hold values from -6 to 6
Outputs:
- layer_output: bfloat16 [4096, 1024], P(('dp', 'fs'))
- tokens_grad: float32 [4096, 1024], P(('dp', 'fs'))
- attend_weight_grad: float32 [3, 1024, 1024], P(None, 'dp', 'fs')
- attend_bias_grad: float32 [2, 16, 64], P(None, 'fs', 'dp')
- output_weight_grad: float32 [1024, 1024], P('fs', 'dp')
- expand_weight_grad: float32 [1024, 4096], P('dp', 'fs')
- expand_bias_grad: float32 [4, 1024], P('fs', 'dp')
- contract_weight_grad: float32 [4096, 1024], P('fs', 'dp')
- layer_vectors_grad: float32 [6, 1024], P(None, ('dp', 'fs'))
The draws below stay inside these ranges and needn't reach their ends.
Inputs may be any that keep to these rules, and one draw needn't show every extreme that they name: `sequence_lengths`: the sequences that sequence_owner gives one block hold 128 tokens at most together and 64 at least; one sequence holds exactly 128 and one exactly 16. `sequence_owner`: every block gets one to three sequences; some block gets exactly one.
All inputs are finite; a program needn't handle non-finite values.
Results may differ from the reference program's by a relative error of at most 0.02.
Values may be sent and summed in bfloat16 or wider, within the bound.
No kernel may reach another device: no remote copies, remote signals or barrier semaphores. Data moves between devices by JAX's collectives and lax.ppermute only.
A program may use at most 128 MiB of HBM per device.

```python
import math
from functools import partial
import jax
import jax.numpy as jnp
from jax import lax

HEADS = 16
HEAD = 64
D = 1024
FF = 4096
TOK_DEV = 128
SHORTEST = 16
TOKENS = 4096
N_DP = 8
N_FS = 4


def deal_sequences(key):
    blocks = N_DP * N_FS
    pairs = blocks // 2
    key_count, key_load, key_weight, key_place, key_order = jax.random.split(key, 5)
    first = jax.random.randint(key_count, (pairs,), 1, 4, dtype=jnp.int32)
    first = first.at[0].set(1)
    loads = jax.random.randint(key_load, (pairs, 2), TOK_DEV // 2, TOK_DEV + 1, dtype=jnp.int32)
    loads = loads.at[0, 0].set(TOK_DEV)
    shares = jax.random.randint(key_weight, (pairs, 4), 1, 9, dtype=jnp.int32)
    shares = shares.at[0, 3].set(0)
    entry = jnp.arange(4, dtype=jnp.int32)
    side = (entry[None, :] >= first[:, None]).astype(jnp.int32)
    seq_count = jnp.where(side == 0, first[:, None], 4 - first[:, None])
    load_here = jnp.where(side == 0, loads[:, 0:1], loads[:, 1:2])
    same_side = side[:, :, None] == side[:, None, :]
    earlier = (entry[:, None] > entry[None, :])[None]
    before = jnp.sum(jnp.where(same_side & earlier, shares[:, None, :], 0), axis=2)
    total_share = jnp.sum(jnp.where(same_side, shares[:, None, :], 0), axis=2)
    extra = load_here - seq_count * SHORTEST
    lengths = SHORTEST + extra * (before + shares) // total_share - extra * before // total_share
    home = 2 * jnp.arange(pairs, dtype=jnp.int32)[:, None] + side
    place = jax.random.permutation(key_place, blocks).astype(jnp.int32)
    owners = place[home.reshape(-1)]
    order = jax.random.permutation(key_order, 2 * blocks)
    return (lengths.reshape(-1).astype(jnp.int32)[order], owners[order])


def draw_sequence_lengths(key, part):
    lengths, owners = deal_sequences(key)
    return lengths


def draw_sequence_owner(key, part):
    lengths, owners = deal_sequences(key)
    return owners


def draw_layer_vectors(key, part):
    key = jax.random.fold_in(key, 3)
    noise = jax.random.normal(key, (6, D), jnp.float32)
    centre = jnp.array([0.0, 1.0, 0.0, 0.0, 1.0, 0.0], jnp.float32)[:, None]
    scale_rows = jnp.where(centre > 0.5, 0.15, 0.5)
    return jnp.clip(centre + scale_rows * noise, -2.0, 2.0).astype(jnp.bfloat16)


def levels(stream_key, shape, shards, low, high):
    def one(position, parts):
        steps = jax.random.uniform(jax.random.fold_in(jax.random.fold_in(stream_key, 6), position), (parts,), jnp.float32, low / len(shards), high / len(shards))
        return jnp.repeat(jnp.exp(steps), shape[position] // parts).reshape((-1,) + (1,) * (len(shape) - position - 1))

    level = one(*shards[0])
    for cut in shards[1:]:
        level = level * one(*cut)
    return level


def bell_draw(stream_key, shape, scale, reach, cuts=(), kind=jnp.bfloat16):
    entries = jax.random.normal(stream_key, shape, jnp.float32) * scale
    if len(cuts) > 0:
        entries = levels(stream_key, shape, cuts, -0.22, 0.18) * entries
    return jnp.clip(entries, min=-reach, max=reach).astype(kind)


def setup_inputs(seed: int = 0) -> dict:
    key_list = jax.random.split(jax.random.key(seed), 12)
    return {
        "tokens": bell_draw(key_list[0], (TOKENS, D), 1.0, 6.0, ((0, 32),)),
        "attend_weight": bell_draw(key_list[1], (3, D, D), D ** -0.5, 0.1875, ((1, 8), (2, 4))),
        "attend_bias": bell_draw(key_list[2], (2, HEADS, HEAD), 0.5, 3.0, ((1, 4), (2, 8))),
        "output_weight": bell_draw(key_list[3], (D, D), (D // 32) ** -0.5, 1.0, ((0, 4), (1, 8))),
        "expand_weight": bell_draw(key_list[4], (D, FF), D ** -0.5, 0.1875, ((0, 8), (1, 4))),
        "expand_bias": bell_draw(key_list[5], (N_FS, FF // N_FS), 0.5, 3.0, ((0, 4), (1, 8))),
        "contract_weight": bell_draw(key_list[6], (FF, D), FF ** -0.5, 0.09375, ((0, 4), (1, 8))),
        "layer_vectors": draw_layer_vectors(jax.random.fold_in(key_list[11], 71), 0),
        "sequence_lengths": draw_sequence_lengths(jax.random.fold_in(key_list[11], 71), 0),
        "sequence_owner": draw_sequence_owner(jax.random.fold_in(key_list[11], 71), 0),
        "output_grad": bell_draw(key_list[10], (TOKENS, D), 1.0, 6.0, ((0, 32),)),
    }


HIGHEST = lax.Precision.HIGHEST
masked_score = -1e+30
norm_eps = 1e-12

@jax.custom_vjp
def low(v):
    return lax.optimization_barrier(v.astype(jnp.bfloat16)).astype(jnp.float32)

@jax.custom_vjp
def low_back(v):
    return v

def low_keep(v):
    return (low(v), None)

def low_pass(kept, grad):
    return (grad,)

def back_keep(v):
    return (v, None)

def back_low(kept, grad):
    return (low(grad),)
low.defvjp(low_keep, low_pass)
low_back.defvjp(back_keep, back_low)

def block_segments(lengths, owners, block_index, slot_count):
    seq_count = lengths.shape[0]
    number = jnp.arange(seq_count, dtype=jnp.int32)
    rank_score = jnp.where(owners == block_index, seq_count - number, 0).astype(jnp.int32)
    chosen_score, chosen = lax.top_k(rank_score, 3)
    present = chosen_score > 0
    seq_sizes = jnp.where(present, lengths[chosen], 0).astype(jnp.int32)
    seq_ends = jnp.cumsum(seq_sizes).astype(jnp.int32)
    starts = seq_ends - seq_sizes
    slot_index = jnp.arange(slot_count, dtype=jnp.int32)[:, None]
    inside = (slot_index >= starts[None, :]) & (slot_index < seq_ends[None, :])
    marked = jnp.where(inside, chosen[None, :].astype(jnp.int32) + 1, 0)
    return (lax.optimization_barrier(jnp.sum(marked, axis=1)) - 1).astype(jnp.int32)

def normalize(in_rows, gain_row, shift_row):
    centred = in_rows - lax.optimization_barrier(jnp.mean(in_rows, axis=1, keepdims=True))
    inverse = lax.rsqrt(lax.optimization_barrier(jnp.mean(centred * centred, axis=1, keepdims=True)) + norm_eps)
    return centred * inverse * gain_row + shift_row

def attend_block(pieces):
    queries, key_rows, values, segment = pieces
    raw_scores = jnp.einsum('rhe,che->hrc', queries, key_rows, precision=HIGHEST)
    scores = low_back(raw_scores) * HEAD ** (-0.5)
    allowed = (segment[:, None] == segment[None, :]) & (segment[None, :] >= 0)
    scores = jnp.where(allowed[None], scores, masked_score)
    highest = lax.optimization_barrier(jnp.max(scores, axis=2, keepdims=True))
    weights = jnp.exp(scores - highest)
    probabilities = low(weights / lax.optimization_barrier(jnp.sum(weights, axis=2, keepdims=True)))
    return jnp.einsum('hrc,che->rhe', probabilities, values, precision=HIGHEST)

def layer_group(params, pieces):
    attend_weight, attend_bias, output_weight, expand_weight, expand_bias, contract_weight, layer_vectors = params
    in_rows, segment = pieces
    groups = segment.shape[0]
    projected = jnp.einsum('nd,tdc->tnc', in_rows, attend_weight, precision=HIGHEST)
    biases = attend_bias.reshape(2, -1)
    head_shape = (groups, TOK_DEV, HEADS, HEAD)
    queries = low(low_back(projected[0] + biases[0])).reshape(head_shape)
    key_rows = low(low_back(projected[1])).reshape(head_shape)
    values = low(low_back(projected[2] + biases[1])).reshape(head_shape)
    mixed_heads = lax.map(jax.checkpoint(attend_block), (queries, key_rows, values, segment))
    mixed_rows = low(low_back(mixed_heads.reshape(in_rows.shape[0], -1)))
    branch = low_back(jnp.dot(mixed_rows, output_weight, precision=HIGHEST) + layer_vectors[0])
    middle = normalize(in_rows + branch, layer_vectors[1], layer_vectors[2])
    hidden_in = low_back(jnp.dot(low(middle), expand_weight, precision=HIGHEST) + expand_bias.reshape(-1))
    hidden = low(jax.nn.gelu(hidden_in, approximate=False))
    result = low_back(jnp.dot(hidden, contract_weight, precision=HIGHEST) + layer_vectors[3])
    live_rows = (segment.reshape(-1) >= 0).astype(in_rows.dtype)
    return normalize(middle + result, layer_vectors[4], layer_vectors[5]) * live_rows[:, None]

def reference(tokens, attend_weight, attend_bias, output_weight, expand_weight, expand_bias, contract_weight, layer_vectors, sequence_lengths, sequence_owner, output_grad):
    blocks = N_DP * N_FS
    per_group = math.gcd(blocks, 32)
    segment = lax.map(lambda block_index: block_segments(sequence_lengths, sequence_owner, block_index, TOK_DEV), jnp.arange(blocks, dtype=jnp.int32))
    segment = segment.reshape(blocks // per_group, per_group, TOK_DEV)
    params = tuple((member.astype(jnp.float32) for member in (attend_weight, attend_bias, output_weight, expand_weight, expand_bias, contract_weight, layer_vectors)))

    def forward(in_rows, *weights):
        grouped = in_rows.reshape(blocks // per_group, per_group * TOK_DEV, in_rows.shape[1])
        outputs = lax.map(jax.checkpoint(partial(layer_group, weights)), (grouped, segment))
        return outputs.reshape(in_rows.shape)
    layer_output, pullback = jax.vjp(forward, tokens.astype(jnp.float32), *params)
    grads = pullback(output_grad.astype(jnp.float32))
    return (layer_output.astype(jnp.bfloat16), grads[0], grads[1], grads[2], grads[3], grads[4], grads[5], grads[6], grads[7])
```

```python
import jax
import jax.numpy as jnp
from jax import lax
from jax.sharding import PartitionSpec as P

masked_score = -1e30
norm_eps = 1e-12
root_half = 0.7071067811865476
inverse_root_tau = 0.3989422804014327


def block_segments(lengths, owners, block_index, slot_count):
    seq_count = lengths.shape[0]
    number = jnp.arange(seq_count, dtype=jnp.int32)
    rank_score = jnp.where(owners == block_index, seq_count - number, 0)
    chosen_score, chosen = lax.top_k(rank_score, 3)
    present = chosen_score > 0
    seq_sizes = jnp.where(present, lengths[chosen], 0)
    seq_ends = jnp.cumsum(seq_sizes)
    starts = seq_ends - seq_sizes
    slot_index = jnp.arange(slot_count, dtype=jnp.int32)[:, None]
    inside = (slot_index >= starts[None, :]) & (slot_index < seq_ends[None, :])
    marked = jnp.where(inside, chosen[None, :] + 1, 0)
    return jnp.sum(marked, axis=1) - 1


def normalize(in_rows, gain_row, shift_row):
    centred = in_rows - jnp.mean(in_rows, axis=1, keepdims=True)
    inverse = lax.rsqrt(jnp.mean(centred * centred, axis=1, keepdims=True) + norm_eps)
    unit_rows = centred * inverse
    return (unit_rows * gain_row + shift_row, unit_rows, inverse)


def normalize_back(upstream, gain_row, unit_rows, inverse):
    scaled = upstream * gain_row
    centred = scaled - jnp.mean(scaled, axis=1, keepdims=True)
    downstream = inverse * (
        centred - unit_rows * jnp.mean(scaled * unit_rows, axis=1, keepdims=True)
    )
    return (downstream, jnp.sum(upstream * unit_rows, axis=0), jnp.sum(upstream, axis=0))


def gelu_parts(value):
    normal_cdf = 0.5 * (1.0 + lax.erf(value * root_half))
    density = jnp.exp(-0.5 * value * value) * inverse_root_tau
    return (value * normal_cdf, normal_cdf + value * density)


def score_table(queries, key_rows, segment):
    raw_scores = jnp.einsum(
        "brhe,bche->bhrc", queries, key_rows, preferred_element_type=jnp.float32
    )
    allowed = (segment[:, :, None] == segment[:, None, :]) & (segment[:, None, :] >= 0)
    return jnp.where(allowed[:, None], raw_scores * queries.shape[-1] ** (-0.5), masked_score)


def attend(queries, key_rows, values, segment):
    scores = score_table(queries, key_rows, segment)
    highest = jnp.max(scores, axis=3, keepdims=True)
    weights = jnp.exp(scores - highest)
    totals = jnp.sum(weights, axis=3, keepdims=True)
    probabilities = (weights / totals).astype(jnp.bfloat16)
    mixed_heads = jnp.einsum(
        "bhrc,bche->brhe", probabilities, values, preferred_element_type=jnp.float32
    )
    return (mixed_heads.astype(jnp.bfloat16), highest + jnp.log(totals))


def attend_back(queries, key_rows, values, segment, log_totals, grad_mixed):
    scores = score_table(queries, key_rows, segment)
    probabilities = jnp.exp(scores - log_totals)
    grad_values = jnp.einsum(
        "bhrc,brhe->bche",
        probabilities.astype(jnp.bfloat16),
        grad_mixed,
        preferred_element_type=jnp.float32,
    )
    grad_probs = jnp.einsum(
        "brhe,bche->bhrc", grad_mixed, values, preferred_element_type=jnp.float32
    )
    grad_scores = probabilities * (
        grad_probs - jnp.sum(grad_probs * probabilities, axis=3, keepdims=True)
    )
    grad_raw = (grad_scores * queries.shape[-1] ** (-0.5)).astype(jnp.bfloat16)
    grad_queries = jnp.einsum(
        "bhrc,bche->brhe", grad_raw, key_rows, preferred_element_type=jnp.float32
    )
    grad_keys = jnp.einsum("bhrc,brhe->bche", grad_raw, queries, preferred_element_type=jnp.float32)
    return (grad_queries, grad_keys, grad_values)


def swap(part, axis_name, distance):
    count = lax.axis_size(axis_name)
    return lax.ppermute(part, axis_name, [(i, i ^ distance) for i in range(count)])


def xor_order(table, axis, index):
    count = table.shape[axis]
    step = 1
    while step < count:
        split = table.shape[:axis] + (count // (2 * step), 2, step) + table.shape[axis + 1 :]
        flipped = jnp.flip(table.reshape(split), axis + 1).reshape(table.shape)
        table = jnp.where((index // step) % 2 == 1, flipped, table)
        step *= 2
    return table


def gather_fs(part):
    return [part] + [swap(part, "fs", j) for j in range(1, lax.axis_size("fs"))]


def gather_dp(part):
    own_lane = [part] + [swap(part, "dp", j) for j in range(2, lax.axis_size("dp"), 2)]
    return own_lane + [swap(piece, "dp", 1) for piece in own_lane]


def to_slots(rows, index):
    count = lax.axis_size("dp")
    table = rows.reshape(rows.shape[0], count, -1)
    table = xor_order(table, 1, index)
    table = table.reshape(rows.shape[0], count // 2, 2, -1)
    return jnp.swapaxes(table, 1, 2).reshape(rows.shape)


def from_slots(rows, index):
    count = lax.axis_size("dp")
    table = rows.reshape(rows.shape[0], 2, count // 2, -1)
    table = jnp.swapaxes(table, 1, 2).reshape(rows.shape[0], count, -1)
    return xor_order(table, 1, index).reshape(rows.shape)


def reduce_rows(total, local_rows):
    parts = total.reshape(-1, local_rows, total.shape[1])
    result = parts[0]
    for j in range(1, lax.axis_size("fs")):
        result = result + swap(parts[j].astype(jnp.bfloat16), "fs", j).astype(jnp.float32)
    return result


def reduce_dp(total, kind):
    half = total.shape[0] // 2
    lanes = lax.axis_size("dp") // 2
    mine = total[:half] + swap(total[half:].astype(kind), "dp", 1).astype(jnp.float32)
    pieces = mine.reshape((lanes, half // lanes) + total.shape[1:])
    result = pieces[0]
    for j in range(1, lanes):
        result = result + swap(pieces[j].astype(kind), "dp", 2 * j).astype(jnp.float32)
    return result


def on_device(
    tokens,
    attend_weight,
    attend_bias,
    output_weight,
    expand_weight,
    expand_bias,
    contract_weight,
    layer_vectors,
    sequence_lengths,
    sequence_owner,
    output_grad,
):
    local_rows, width = tokens.shape
    n_fs = lax.axis_size("fs")
    n_dp = lax.axis_size("dp")
    fs_index = lax.axis_index("fs")
    dp_index = lax.axis_index("dp")
    group_first = dp_index * n_fs
    own_block = group_first + fs_index
    block_list = group_first + (fs_index ^ jnp.arange(n_fs, dtype=jnp.int32))
    segment = jax.vmap(
        lambda block_index: block_segments(
            sequence_lengths, sequence_owner, block_index, local_rows
        )
    )(block_list)
    live_rows = (segment[0] >= 0).astype(jnp.float32)[:, None]

    own_rows = to_slots(tokens, dp_index)
    inputs = jnp.concatenate(gather_fs(own_rows), axis=0)
    full_attend = jnp.concatenate(gather_dp(attend_weight), axis=1)
    full_output = jnp.concatenate(gather_dp(output_weight), axis=1)

    vector_part = jnp.stack(gather_fs(layer_vectors), axis=1)
    vector_part = xor_order(vector_part, 1, fs_index)
    bias_shape = attend_bias.shape
    small = jnp.concatenate(
        [vector_part.reshape(-1), attend_bias.reshape(-1), expand_bias.reshape(-1)]
    )
    small_all = jnp.stack(gather_dp(small)).astype(jnp.float32)
    vector_size = vector_part.size
    bias_size = attend_bias.size
    vector_rows = jnp.swapaxes(
        small_all[:, :vector_size].reshape(n_dp, layer_vectors.shape[0], -1), 0, 1
    ).reshape(layer_vectors.shape[0], width)
    slots_first = jnp.swapaxes(small_all.reshape(2, n_dp // 2, -1), 0, 1).reshape(n_dp, -1)
    ordered = xor_order(slots_first, 0, dp_index)
    bias_rows = jnp.moveaxis(
        ordered[:, vector_size : vector_size + bias_size].reshape((n_dp,) + bias_shape), 0, 2
    ).reshape(2, -1)
    expand_row = ordered[:, vector_size + bias_size :].reshape(-1)

    full_expand = jnp.concatenate(gather_dp(expand_weight), axis=0)
    full_contract = jnp.concatenate(gather_dp(contract_weight), axis=1)

    many_rows = inputs.shape[0]
    heads = bias_shape[1]
    head_shape = (n_fs, local_rows, heads, bias_shape[2] * n_dp)
    projected = jnp.einsum("nd,tdc->tnc", inputs, full_attend, preferred_element_type=jnp.float32)
    queries = (projected[0] + bias_rows[0]).astype(jnp.bfloat16).reshape(head_shape)
    key_rows = projected[1].astype(jnp.bfloat16).reshape(head_shape)
    values = (projected[2] + bias_rows[1]).astype(jnp.bfloat16).reshape(head_shape)
    mixed_heads, log_totals = attend(queries, key_rows, values, segment)
    mixed_rows = mixed_heads.reshape(many_rows, -1)

    branch = (
        reduce_rows(
            jnp.dot(mixed_rows, full_output, preferred_element_type=jnp.float32), local_rows
        )
        + vector_rows[0]
    )
    middle, unit_first, inverse_first = normalize(
        own_rows.astype(jnp.float32) + branch, vector_rows[1], vector_rows[2]
    )
    middle_all = jnp.concatenate(gather_fs(middle.astype(jnp.bfloat16)), axis=0)
    hidden_in = jnp.dot(middle_all, full_expand, preferred_element_type=jnp.float32) + expand_row
    activated, slope = gelu_parts(hidden_in)
    hidden = activated.astype(jnp.bfloat16)

    result = (
        reduce_rows(
            jnp.dot(hidden, full_contract, preferred_element_type=jnp.float32), local_rows
        )
        + vector_rows[3]
    )
    final, unit_second, inverse_second = normalize(middle + result, vector_rows[4], vector_rows[5])
    layer_output = from_slots((final * live_rows).astype(jnp.bfloat16), dp_index)

    grad_final = to_slots(output_grad, dp_index).astype(jnp.float32) * live_rows
    grad_second, gain_second, shift_second = normalize_back(
        grad_final, vector_rows[4], unit_second, inverse_second
    )
    grad_result = grad_second.astype(jnp.bfloat16)
    bias_result = jnp.sum(grad_result.astype(jnp.float32), axis=0)
    result_all = jnp.concatenate(gather_fs(grad_result), axis=0)
    grad_hidden = jnp.einsum(
        "nd,fd->nf", result_all, full_contract, preferred_element_type=jnp.float32
    )
    grad_inner = (grad_hidden * slope).astype(jnp.bfloat16)
    grad_middle = grad_second + reduce_rows(
        jnp.einsum("nf,df->nd", grad_inner, full_expand, preferred_element_type=jnp.float32),
        local_rows,
    )
    contract_grad = reduce_dp(
        jnp.einsum("nd,nf->df", result_all, hidden, preferred_element_type=jnp.float32),
        jnp.bfloat16,
    ).T
    expand_bias_grad = jnp.sum(grad_inner.astype(jnp.float32), axis=0)
    expand_grad = reduce_dp(
        jnp.einsum("nd,nf->df", middle_all, grad_inner, preferred_element_type=jnp.float32),
        jnp.bfloat16,
    )

    grad_first, gain_first, shift_first = normalize_back(
        grad_middle, vector_rows[1], unit_first, inverse_first
    )
    grad_branch = grad_first.astype(jnp.bfloat16)
    bias_branch = jnp.sum(grad_branch.astype(jnp.float32), axis=0)
    branch_all = jnp.concatenate(gather_fs(grad_branch), axis=0)
    grad_mixed = (
        jnp.einsum("nd,cd->nc", branch_all, full_output, preferred_element_type=jnp.float32)
        .astype(jnp.bfloat16)
        .reshape(head_shape)
    )
    output_grad_part = reduce_dp(
        jnp.einsum("nd,nc->dc", branch_all, mixed_rows, preferred_element_type=jnp.float32),
        jnp.bfloat16,
    ).T
    grad_queries, grad_keys, grad_values = attend_back(
        queries, key_rows, values, segment, log_totals, grad_mixed
    )
    grad_projected = jnp.concatenate(
        [
            part.reshape(many_rows, -1).astype(jnp.bfloat16)
            for part in (grad_queries, grad_keys, grad_values)
        ],
        axis=1,
    )
    weight_rows = jnp.swapaxes(full_attend, 0, 1).reshape(width, -1)
    tokens_grad = from_slots(
        grad_first
        + reduce_rows(
            jnp.einsum(
                "nc,dc->nd", grad_projected, weight_rows, preferred_element_type=jnp.float32
            ),
            local_rows,
        ),
        dp_index,
    )
    attend_grad = reduce_dp(
        jnp.einsum("nd,nc->dc", inputs, grad_projected, preferred_element_type=jnp.float32),
        jnp.bfloat16,
    )
    attend_grad = jnp.swapaxes(attend_grad.reshape(attend_grad.shape[0], 3, -1), 0, 1)

    bias_sums = jnp.sum(grad_projected.astype(jnp.float32), axis=0).reshape(3, -1)
    bias_pair = jnp.stack([bias_sums[0], bias_sums[2]]).reshape(2, heads, n_dp, -1)
    canonical = jnp.concatenate(
        [jnp.moveaxis(bias_pair, 2, 0).reshape(n_dp, -1), expand_bias_grad.reshape(n_dp, -1)],
        axis=1,
    )
    slotted = jnp.swapaxes(
        xor_order(canonical, 0, dp_index).reshape(n_dp // 2, 2, -1), 0, 1
    ).reshape(n_dp, -1)
    vector_grad = jnp.stack(
        [bias_branch, gain_first, shift_first, bias_result, gain_second, shift_second]
    )
    vector_slots = jnp.swapaxes(vector_grad.reshape(6, n_dp, -1), 0, 1).reshape(n_dp, -1)
    small_grad = reduce_dp(jnp.concatenate([vector_slots, slotted], axis=1), jnp.float32)[0]
    vector_sums = small_grad[:vector_size].reshape(6, n_fs, -1)
    vector_sums = jnp.swapaxes(xor_order(vector_sums, 1, fs_index), 0, 1)
    vector_own = vector_sums[0]
    for j in range(1, n_fs):
        vector_own = vector_own + swap(vector_sums[j], "fs", j)
    attend_bias_grad = small_grad[vector_size : vector_size + bias_size].reshape(bias_shape)
    expand_bias_out = small_grad[vector_size + bias_size :].reshape(expand_bias.shape)
    return (
        layer_output,
        tokens_grad,
        attend_grad,
        attend_bias_grad,
        output_grad_part,
        expand_grad,
        expand_bias_out,
        contract_grad,
        vector_own,
    )


def solution(mesh):
    in_specs = (
        P(("dp", "fs"), None),
        P(None, "dp", "fs"),
        P(None, "fs", "dp"),
        P("fs", "dp"),
        P("dp", "fs"),
        P("fs", "dp"),
        P("fs", "dp"),
        P(None, ("dp", "fs")),
        P(),
        P(),
        P(("dp", "fs"), None),
    )
    out_specs = (
        P(("dp", "fs"), None),
        P(("dp", "fs"), None),
        P(None, "dp", "fs"),
        P(None, "fs", "dp"),
        P("fs", "dp"),
        P("dp", "fs"),
        P("fs", "dp"),
        P("fs", "dp"),
        P(None, ("dp", "fs")),
    )
    return jax.shard_map(
        on_device, mesh=mesh, in_specs=in_specs, out_specs=out_specs, check_vma=False
    )
```

```python
import functools

import jax
import jax.numpy as jnp
from jax import lax
from jax.experimental import pallas as pl
from jax.experimental.pallas import tpu as pltpu
from jax.sharding import PartitionSpec as P

masked_score = -1e30
norm_eps = 1e-12
root_half = 0.7071067811865476
inverse_root_tau = 0.3989422804014327
small_rows = 16
head_size = 64
f32 = jnp.float32
bf16 = jnp.bfloat16


def slot_order(count):
    order = [0]
    while len(order) < count:
        step = count // (2 * len(order))
        order = order + [entry | step for entry in order]
    bits = count.bit_length() - 1
    return [int(format(i, "b").zfill(bits)[::-1], 2) for i in range(count)]


def swap(part, axis_name, distance):
    count = lax.axis_size(axis_name)
    return lax.ppermute(part, axis_name, [(i, i ^ distance) for i in range(count)])


def gather_fs(part):
    return [part] + [swap(part, "fs", j) for j in range(1, lax.axis_size("fs"))]


def gather_dp(part):
    count = lax.axis_size("dp")
    held = {0: part}
    step = count // 2
    while step:
        held.update({entry | step: swap(piece, "dp", step) for entry, piece in list(held.items())})
        step //= 2
    return [held[entry] for entry in slot_order(count)]


def reduce_dp(keep, give, done):
    step = 1
    rounds = []
    while True:
        taken = swap(give, "dp", step)
        step *= 2
        if step == lax.axis_size("dp"):
            return done(keep, taken), rounds
        half = shape_of((keep.shape[0] // 2,) + keep.shape[1:], bf16)
        keep, give = kernel_call(add_kernel, [half, half], keep, taken)
        rounds.append(give)


class Late:
    def __init__(self, source, target, semaphore):
        self.target = target
        self.shape = target.shape
        self.dtype = target.dtype
        self.copy = pltpu.make_async_copy(source, target, semaphore)
        self.copy.start()
        self.waits = True

    def ready(self):
        if self.waits:
            self.copy.wait()
            self.waits = False

    def __getitem__(self, where):
        self.ready()
        return self.target[where]


def kernel_call(body, outs, *args, after=(), flops=0, limit=24):
    moved = sum(a.size * a.dtype.itemsize for a in list(args) + list(outs))
    late = [a.ndim > 1 and a.size * a.dtype.itemsize >= 2**15 for a in args]

    def whole(*refs):
        given, refs = refs[: len(args)], refs[len(args) + len(after) :]
        out_refs, refs = refs[: len(outs)], refs[len(outs) :]
        items = []
        number = 0
        for ref, is_late in zip(given, late):
            if is_late:
                ref = Late(ref, refs[number], refs[-1].at[number])
                number += 1
            items.append(ref)
        body(*items, *out_refs)
        for item in items:
            if isinstance(item, Late):
                item.ready()

    def place(a, is_late):
        if a.ndim == 1:
            return pltpu.SMEM
        return pl.ANY if is_late else pltpu.VMEM

    return pl.pallas_call(
        whole,
        out_shape=outs,
        in_specs=[pl.BlockSpec(memory_space=place(a, b)) for a, b in zip(args, late)]
        + [pl.BlockSpec(memory_space=pl.ANY) for _ in after],
        out_specs=[pl.BlockSpec(memory_space=pltpu.VMEM) for _ in outs],
        scratch_shapes=[pltpu.VMEM(a.shape, a.dtype) for a, b in zip(args, late) if b]
        + [pltpu.SemaphoreType.DMA((max(1, sum(late)),))],
        compiler_params=pltpu.CompilerParams(vmem_limit_bytes=limit * 2**20),
        cost_estimate=pl.CostEstimate(flops=flops, bytes_accessed=moved, transcendentals=0),
    )(*args, *after)


def shape_of(shape, kind):
    return jax.ShapeDtypeStruct(shape, kind)


def dot(left, right):
    return jnp.dot(left, right, preferred_element_type=f32)


def dot_nt(left, right):
    return lax.dot_general(left, right, (((1,), (1,)), ((), ())), preferred_element_type=f32)


def dot_tn(left, right):
    return lax.dot_general(left, right, (((0,), (0,)), ((), ())), preferred_element_type=f32)


def flip_blocks(blocks, index):
    step = 1
    while step < len(blocks):
        chosen = (index // step) % 2 == 1
        blocks = [jnp.where(chosen, blocks[i ^ step], blocks[i]) for i in range(len(blocks))]
        step *= 2
    return blocks


def split_columns(rows, count):
    size = rows.shape[1] // count
    return [rows[:, i * size : (i + 1) * size] for i in range(count)]


def to_slots(rows, index, count):
    blocks = flip_blocks(split_columns(rows, count), index)
    return jnp.concatenate([blocks[entry] for entry in slot_order(count)], axis=1)


def from_slots(rows, index, count):
    slots = split_columns(rows, count)
    order = slot_order(count)
    blocks = [slots[order.index(i)] for i in range(count)]
    return jnp.concatenate(flip_blocks(blocks, index), axis=1)


def row_mean(rows):
    return jnp.mean(rows, axis=1, keepdims=True)


def normalize(rows):
    centred = rows - row_mean(rows)
    inverse = lax.rsqrt(row_mean(centred * centred) + norm_eps)
    return (centred * inverse, inverse)


def normalize_back(upstream, gain, unit, inverse):
    scaled = upstream * gain
    return inverse * (scaled - row_mean(scaled) - unit * row_mean(scaled * unit))


def column_sum(rows):
    return jnp.sum(rows, axis=0, keepdims=True)


def stacked(refs):
    return jnp.concatenate([ref[...] for ref in refs], axis=0)


def beside(refs):
    return jnp.concatenate([ref[...] for ref in refs], axis=1)


def sum_blocks(refs):
    total = refs[0][...]
    for ref in refs[1:]:
        total = total + ref[...].astype(f32)
    return total


def store_blocks(refs, total):
    size = refs[0].shape[0]
    for i, ref in enumerate(refs):
        ref[...] = total[i * size : (i + 1) * size].astype(ref.dtype)


def store_columns(refs, place, total):
    size = refs[0].shape[0]
    width = total.shape[1]
    for i, ref in enumerate(refs):
        part = total[i * size : (i + 1) * size].astype(ref.dtype)
        ref[:, place * width : (place + 1) * width] = part


def add_kernel(left, right, keep, give):
    half = keep.shape[0]
    for out, start in ((give, half), (keep, 0)):
        for i in range(half):
            total = left[start + i].astype(f32) + right[start + i].astype(f32)
            out[i] = total.astype(out.dtype)


def last_kernel(left, right, out):
    out[...] = left[0].astype(f32) + right[0].astype(f32)


def block_shapes(count, rows, width):
    return [shape_of((rows, width), f32)] + [shape_of((rows, width), bf16)] * (count - 1)


def one_hot(target, width):
    column = lax.broadcasted_iota(jnp.int32, (target.shape[0], width), 1)
    return jnp.where(column == target, 1.0, 0.0).astype(bf16)


def entries(count):
    return lax.broadcasted_iota(jnp.int32, (count, 1), 0)


def pack_kernel(n_dp, place, tokens, weight, bias, vectors, expand_bias, x_out, out):
    x_out[...] = to_slots(tokens[...].astype(f32), place[0], n_dp).astype(bf16)
    rows, width = weight.shape[1:]
    for t in range(3):
        out[t * rows : (t + 1) * rows, :] = weight[t]
    count, lanes = vectors.shape
    lead = one_hot(entries(lanes) + place[1] * lanes, width)
    table = dot(vectors[...], lead)
    pads = small_rows - count - 2
    out[3 * rows :, :] = jnp.concatenate(
        [
            dot(bias[...], one_hot(entries(bias.shape[1]), width)),
            table,
            dot(expand_bias[...], one_hot(entries(expand_bias.shape[1]), width)),
            jnp.zeros((pads, width), f32),
        ],
        axis=0,
    ).astype(bf16)


def head_masks(width):
    lane = lax.broadcasted_iota(jnp.int32, (1, width), 1)
    return [lane // head_size == h for h in range(width // head_size)]


def attend_kernel(n_fs, n_dp, bias_shape, expand_share, place, *refs):
    w_refs, refs = refs[:n_dp], refs[n_dp:]
    x_refs, refs = refs[:n_fs], refs[n_fs:]
    seg_row, seg_col, q_out, k_out, v_out, o_out, p_out, small, expand_out = refs
    width = w_refs[0].shape[1]
    rows = (w_refs[0].shape[0] - small_rows) // 3
    order = slot_order(n_dp)
    lows = [ref[3 * rows :, :] for ref in w_refs]
    small[...] = jnp.concatenate([low[:, :rows] for low in lows], axis=1)
    taken = min(128, width)
    _, heads, share = bias_shape
    biases = []
    for t in range(2):
        offset = entries(taken) - t * heads * share
        valid = (offset >= 0) & (offset < heads * share)
        total = jnp.zeros((small_rows, width), f32)
        for s in range(n_dp):
            target = (offset // share) * head_size + (place[0] ^ order[s]) * share + offset % share
            total = total + dot(
                lows[s][:, :taken], one_hot(jnp.where(valid, target, -1), width)
            )
        biases.append(total[0:1])
    total = jnp.zeros((small_rows, expand_out.shape[1]), f32)
    for s in range(n_dp):
        offset = entries(taken)
        target = jnp.where(offset < expand_share, offset + (place[0] ^ order[s]) * expand_share, -1)
        total = total + dot(lows[s][:, :taken], one_hot(target, expand_out.shape[1]))
    expand_out[...] = total[small_rows // 2 - 1 : small_rows // 2]
    x = stacked(x_refs)
    parts = []
    for t in range(3):
        weight = jnp.concatenate([ref[t * rows : (t + 1) * rows, :] for ref in w_refs], axis=0)
        part = dot(x, weight)
        if t != 1:
            part = part + biases[t // 2]
        parts.append(part.astype(bf16))
    q_out[...], k_out[...], v_out[...] = parts
    size = x_refs[0].shape[0]
    group = min(128, width)
    masks = head_masks(group)
    zero = jnp.zeros((), bf16)
    number = 0
    for b in range(n_fs):
        low, high = b * size, (b + 1) * size
        columns = seg_row[b : b + 1, :]
        allowed = (seg_col[low:high, :] == columns) & (columns >= 0)
        for g in range(0, width, group):
            q, k, v = (part[low:high, g : g + group] for part in parts)
            mixed = jnp.zeros((size, group), f32)
            for mask in masks:
                scores = dot_nt(q, jnp.where(mask, k, zero)) * head_size**-0.5
                scores = jnp.where(allowed, scores, masked_score)
                weights = jnp.exp(scores - jnp.max(scores, axis=1, keepdims=True))
                chances = weights / jnp.sum(weights, axis=1, keepdims=True)
                p_out[number] = chances
                number += 1
                mixed = mixed + dot(chances.astype(bf16), jnp.where(mask, v, zero))
            o_out[low:high, g : g + group] = mixed.astype(bf16)


def project_kernel(n_dp, *refs):
    w_refs, refs = refs[:n_dp], refs[n_dp:]
    o, small, outs = refs[0], refs[1], refs[2:]
    total = dot(o[...], beside(w_refs))
    size = outs[0].shape[0] - small_rows
    for i, out in enumerate(outs):
        out[:size, :] = total[i * size : (i + 1) * size].astype(out.dtype)
        out[size:, :] = small[...].astype(out.dtype)


def first_norm_kernel(n_fs, *refs):
    parts, (x, vectors, mid, mid_low, unit_out, inverse_out) = refs[:n_fs], refs[n_fs:]
    total = sum_blocks(parts)
    size = x.shape[0]
    small = total[size + 1 : size + 1 + vectors.shape[0]]
    vectors[...] = small
    rows = x[...].astype(f32) + (total[:size] + small[0:1, :])
    unit, inverse = normalize(rows)
    middle = unit * small[1:2, :] + small[2:3, :]
    mid[...] = middle
    mid_low[...] = middle.astype(bf16)
    unit_out[...] = unit
    inverse_out[...] = inverse


def feed_kernel(n_fs, n_dp, *refs):
    mids, refs = refs[:n_fs], refs[n_fs:]
    w1, refs = refs[:n_dp], refs[n_dp:]
    w2, refs = refs[:n_dp], refs[n_dp:]
    bias, hid_out, slope_out, outs = refs[0], refs[1], refs[2], refs[3:]
    rows = stacked(mids)
    expand = stacked(w1)
    chunk = min(256, hid_out.shape[1])
    for c in range(0, hid_out.shape[1], chunk):
        value = dot(rows, expand[:, c : c + chunk]) + bias[:, c : c + chunk]
        cdf = 0.5 * (1.0 + lax.erf(value * root_half))
        density = jnp.exp(-0.5 * value * value) * inverse_root_tau
        hid_out[:, c : c + chunk] = (value * cdf).astype(bf16)
        slope_out[:, c : c + chunk] = cdf + value * density
    for c in range(0, n_dp, 2):
        store_columns(outs, c // 2, dot(hid_out[...], beside(w2[c : c + 2])))


def second_norm_kernel(n_fs, n_dp, index, *refs):
    parts, refs = refs[:n_fs], refs[n_fs:]
    mid, vectors, grad, live, layer_out, dh, dh_low, sums = refs
    rows = mid[...] + (sum_blocks(parts) + vectors[3:4, :])
    unit, inverse = normalize(rows)
    alive = live[...]
    final = (unit * vectors[4:5, :] + vectors[5:6, :]) * alive
    layer_out[...] = from_slots(final, index[0], n_dp).astype(bf16)
    upstream = to_slots(grad[...].astype(f32), index[0], n_dp) * alive
    down = normalize_back(upstream, vectors[4:5, :], unit, inverse)
    low = down.astype(bf16)
    dh[...] = down
    dh_low[...] = low
    sums[0:1, :] = column_sum(low.astype(f32))
    sums[1:2, :] = column_sum(upstream * unit)
    sums[2:3, :] = column_sum(upstream)


def feed_back_kernel(n_fs, n_dp, *refs):
    grads, refs = refs[:n_fs], refs[n_fs:]
    w2, refs = refs[:n_dp], refs[n_dp:]
    w1, refs = refs[:n_dp], refs[n_dp:]
    slope, du_out, bias_out, outs = refs[0], refs[1], refs[2], refs[3:]
    rows = stacked(grads)
    contract = beside(w2)
    chunk = min(256, du_out.shape[1])
    for c in range(0, du_out.shape[1], chunk):
        du = dot_nt(rows, contract[c : c + chunk]) * slope[:, c : c + chunk]
        du = du.astype(bf16)
        du_out[:, c : c + chunk] = du
        bias_out[:, c : c + chunk] = column_sum(du.astype(f32))
    for c in range(0, n_dp, 2):
        store_columns(outs, c // 2, dot_nt(du_out[...], stacked(w1[c : c + 2])))


def store_halves(keep, give, slot, value):
    half = keep.shape[0]
    target = keep if slot < half else give
    target[slot % half] = value.astype(target.dtype)


def contract_grad_kernel(n_fs, n_dp, hid, *refs):
    grads, (keep, give) = refs[:n_fs], refs[n_fs:]
    left = hid[...].T
    right = stacked(grads)
    size = right.shape[1] // n_dp
    for s in range(0, n_dp, 2):
        pair = dot(left, right[:, s * size : (s + 2) * size])
        store_halves(keep, give, s, pair[:, :size])
        store_halves(keep, give, s + 1, pair[:, size:])


def expand_grad_kernel(n_fs, n_dp, du, *refs):
    mids, (keep, give) = refs[:n_fs], refs[n_fs:]
    left = stacked(mids).T
    size = left.shape[0] // n_dp
    for s in range(n_dp):
        store_halves(keep, give, s, dot(left[s * size : (s + 1) * size], du[...]))


def first_back_kernel(n_fs, *refs):
    parts, refs = refs[:n_fs], refs[n_fs:]
    dh2, unit, inverse, vectors, second, dh, out = refs
    upstream = dh2[...] + sum_blocks(parts)
    units = unit[...]
    down = normalize_back(upstream, vectors[1:2, :], units, inverse[...])
    low = down.astype(bf16)
    size = dh2.shape[0]
    dh[...] = down
    out[:size, :] = low
    out[size:, :] = jnp.concatenate(
        [
            column_sum(low.astype(f32)),
            column_sum(upstream * units),
            column_sum(upstream),
            second[...],
            jnp.zeros((small_rows - 3 - second.shape[0], upstream.shape[1]), f32),
        ],
        axis=0,
    ).astype(bf16)


def attend_back_kernel(n_fs, n_dp, *refs):
    grads, refs = refs[:n_fs], refs[n_fs:]
    o_refs, refs = refs[:n_dp], refs[n_dp:]
    q_in, k_in, v_in, p_in = refs[:4]
    w_refs, refs = refs[4 : 4 + n_dp], refs[4 + n_dp :]
    dq_out, dk_out, dv_out = refs[:3]
    outs = refs[3:]
    width = q_in.shape[1]
    size = grads[0].shape[0] - small_rows
    group = min(128, width)
    masks = head_masks(group)
    zero = jnp.zeros((), bf16)
    rows = jnp.concatenate([ref[:size, :] for ref in grads], axis=0)
    grad_mixed = dot_nt(rows, beside(o_refs)).astype(bf16)
    number = 0
    for b in range(n_fs):
        low, high = b * size, (b + 1) * size
        for g in range(0, width, group):
            q, k, v = (part[low:high, g : g + group] for part in (q_in, k_in, v_in))
            do = grad_mixed[low:high, g : g + group]
            dq = jnp.zeros((size, group), f32)
            dk = jnp.zeros((size, group), f32)
            dv = jnp.zeros((size, group), f32)
            for mask in masks:
                chances = p_in[number]
                number += 1
                masked_do = jnp.where(mask, do, zero)
                dp = dot_nt(masked_do, v)
                ds = chances * (dp - jnp.sum(dp * chances, axis=1, keepdims=True))
                ds = (ds * head_size**-0.5).astype(bf16)
                dv = dv + dot_tn(chances.astype(bf16), masked_do)
                dq = dq + dot(ds, jnp.where(mask, k, zero))
                dk = dk + dot_tn(ds, jnp.where(mask, q, zero))
            dq_out[low:high, g : g + group] = dq.astype(bf16)
            dk_out[low:high, g : g + group] = dk.astype(bf16)
            dv_out[low:high, g : g + group] = dv.astype(bf16)
    share = (w_refs[0].shape[0] - small_rows) // 3
    for c in range(0, n_dp, 2):
        total = 0.0
        for t, part in enumerate((dq_out, dk_out, dv_out)):
            weight = jnp.concatenate(
                [ref[t * share : (t + 1) * share, :] for ref in w_refs[c : c + 2]], axis=0
            )
            total = total + dot_nt(part[...], weight)
        store_columns(outs, c // 2, total)


def attend_grad_kernel(n_fs, n_dp, bias_shape, place, *refs):
    xs, refs = refs[:n_fs], refs[n_fs:]
    grads, refs = refs[:n_fs], refs[n_fs:]
    mixed, dq, dk, dv, expand_sums, keep, give = refs
    size = xs[0].shape[0]
    half = keep.shape[0]
    width = keep.shape[2]
    branch = [ref[:size, :] for ref in grads]
    inputs = [ref[...] for ref in xs]
    for t, (rows, value) in enumerate(((inputs, dq), (inputs, dk), (inputs, dv), (branch, mixed))):
        left = jnp.concatenate(rows, axis=0).T
        share = left.shape[0] // n_dp
        result = dot(left, value[...]).astype(bf16)
        for s in range(n_dp):
            target = keep if s < half else give
            target[s % half, t * share : (t + 1) * share, :] = result[s * share : (s + 1) * share]
    vectors = jnp.zeros((small_rows, xs[0].shape[1]), f32)
    for ref in grads:
        vectors = vectors + ref[size:, :].astype(f32)
    vectors = vectors.astype(bf16)
    _, heads, part = bias_shape
    sums = [column_sum(ref[...].astype(f32)).astype(bf16) for ref in (dq, dv)]
    padding = jnp.zeros((small_rows - 1, width), bf16)
    sums = [jnp.concatenate([row, padding], axis=0) for row in sums]
    expand = expand_sums[...].astype(bf16)
    expand_part = expand.shape[1] // n_dp
    expand = jnp.concatenate(
        [expand, jnp.zeros((small_rows - 1, expand.shape[1]), bf16)], axis=0
    )
    order = slot_order(n_dp)
    for s in range(n_dp):
        owner = place[0] ^ order[s]
        column = entries(width)
        inside = (column % head_size) // part == owner
        first = 0.0
        for t in range(2):
            target = (t * heads + column // head_size) * part + column % part
            first = first + dot(sums[t], one_hot(jnp.where(inside, target, -1), width))
        column = entries(expand.shape[1])
        target = jnp.where(column // expand_part == owner, column % expand_part, -1)
        last = dot(expand, one_hot(target, width))
        middle = dot(vectors[:, s * share : (s + 1) * share], one_hot(entries(share), width))
        target = keep if s < half else give
        target[s % half, 4 * share :, :] = jnp.concatenate(
            [first[0:1], middle[0:6], last[0:1], jnp.zeros((small_rows - 8, width), f32)], axis=0
        ).astype(bf16)


def joint_kernel(left, right, attend_out, output_out, small):
    total = left[0].astype(f32) + right[0].astype(f32)
    rows = attend_out.shape[1]
    for t in range(3):
        attend_out[t] = total[t * rows : (t + 1) * rows]
    output_out[...] = total[3 * rows : 4 * rows].T
    small[...] = total[4 * rows :]


def tokens_grad_kernel(n_fs, n_dp, index, *refs):
    parts, (dh, out) = refs[:n_fs], refs[n_fs:]
    out[...] = from_slots(dh[...] + sum_blocks(parts), index[0], n_dp)


def block_segments(lengths, owners, block_index, slot_count):
    seq_count = lengths.shape[0]
    number = jnp.arange(seq_count, dtype=jnp.int32)
    rank_score = jnp.where(owners == block_index, seq_count - number, 0)
    chosen_score, chosen = lax.top_k(rank_score, 3)
    present = chosen_score > 0
    seq_sizes = jnp.where(present, lengths[chosen], 0)
    seq_ends = jnp.cumsum(seq_sizes)
    starts = seq_ends - seq_sizes
    slot_index = jnp.arange(slot_count, dtype=jnp.int32)[:, None]
    inside = (slot_index >= starts[None, :]) & (slot_index < seq_ends[None, :])
    marked = jnp.where(inside, chosen[None, :] + 1, 0)
    return jnp.sum(marked, axis=1) - 1


def on_device(
    tokens,
    attend_weight,
    attend_bias,
    output_weight,
    expand_weight,
    expand_bias,
    contract_weight,
    layer_vectors,
    sequence_lengths,
    sequence_owner,
    output_grad,
):
    size, width = tokens.shape
    n_fs = lax.axis_size("fs")
    n_dp = lax.axis_size("dp")
    fs_index = lax.axis_index("fs")
    dp_index = lax.axis_index("dp")
    place = jnp.stack([dp_index, fs_index]).astype(jnp.int32)
    fs_order = fs_index ^ jnp.arange(n_fs, dtype=jnp.int32)
    many = n_fs * size
    share = width // n_dp
    heads_width = attend_weight.shape[2]
    hidden_width = expand_weight.shape[1]
    n_vectors, lanes = layer_vectors.shape
    bias_shape = attend_bias.shape

    def send_back(parts):
        return [parts[0]] + [swap(parts[j], "fs", j) for j in range(1, n_fs)]

    own_rows, attend_part = kernel_call(
        functools.partial(pack_kernel, n_dp),
        [
            shape_of((size, width), bf16),
            shape_of((3 * share + small_rows, heads_width), bf16),
        ],
        place,
        tokens,
        attend_weight,
        attend_bias.reshape(1, -1),
        layer_vectors,
        expand_bias.reshape(1, -1),
    )
    attend_parts = gather_dp(attend_part)
    inputs = gather_fs(own_rows)
    output_parts = gather_dp(output_weight)
    expand_parts = gather_dp(expand_weight)
    contract_parts = gather_dp(contract_weight)
    block_list = dp_index * n_fs + fs_order
    segment = jax.vmap(
        lambda block_index: block_segments(sequence_lengths, sequence_owner, block_index, size)
    )(block_list)
    live = (segment[0] >= 0).astype(f32)[:, None]
    seg_col = segment.reshape(many, 1)

    half_shape = shape_of((many, heads_width), bf16)
    n_scores = n_fs * heads_width // head_size
    queries, key_rows, values, mixed, chances, small, expand_row = kernel_call(
        functools.partial(attend_kernel, n_fs, n_dp, bias_shape, expand_bias.size),
        [half_shape] * 4
        + [
            shape_of((n_scores, size, size), f32),
            shape_of((small_rows, width), bf16),
            shape_of((1, hidden_width), f32),
        ],
        place,
        *attend_parts,
        *inputs,
        segment,
        seg_col,
        flops=2 * many * width * heads_width * 3,
    )
    branch_parts = kernel_call(
        functools.partial(project_kernel, n_dp),
        block_shapes(n_fs, size + small_rows, width),
        *output_parts,
        mixed,
        small,
        flops=2 * many * width * heads_width,
    )
    vectors, middle, middle_low, unit_first, inverse_first = kernel_call(
        functools.partial(first_norm_kernel, n_fs),
        [
            shape_of((n_vectors, width), f32),
            shape_of((size, width), f32),
            shape_of((size, width), bf16),
            shape_of((size, width), f32),
            shape_of((size, 1), f32),
        ],
        *send_back(branch_parts),
        own_rows,
        limit=12,
    )
    middles = gather_fs(middle_low)
    hidden, slope, *result_parts = kernel_call(
        functools.partial(feed_kernel, n_fs, n_dp),
        [shape_of((many, hidden_width), bf16), shape_of((many, hidden_width), f32)]
        + block_shapes(n_fs, size, width),
        *middles,
        *expand_parts,
        *contract_parts,
        expand_row,
        flops=4 * many * width * hidden_width,
    )
    layer_output, dh2, dffn, sums_second = kernel_call(
        functools.partial(second_norm_kernel, n_fs, n_dp),
        [
            shape_of((size, width), bf16),
            shape_of((size, width), f32),
            shape_of((size, width), bf16),
            shape_of((3, width), f32),
        ],
        place,
        *send_back(result_parts),
        middle,
        vectors,
        output_grad,
        live,
        limit=12,
    )
    dffns = gather_fs(dffn)
    du, expand_sums, *middle_parts = kernel_call(
        functools.partial(feed_back_kernel, n_fs, n_dp),
        [shape_of((many, hidden_width), bf16), shape_of((1, hidden_width), f32)]
        + block_shapes(n_fs, size, width),
        *dffns,
        *contract_parts,
        *expand_parts,
        slope,
        flops=4 * many * width * hidden_width,
    )
    contract_keep, contract_give = kernel_call(
        functools.partial(contract_grad_kernel, n_fs, n_dp),
        [shape_of((n_dp // 2, hidden_width, share), bf16)] * 2,
        hidden,
        *dffns,
        flops=2 * many * width * hidden_width,
    )
    expand_keep, expand_give = kernel_call(
        functools.partial(expand_grad_kernel, n_fs, n_dp),
        [shape_of((n_dp // 2, share, hidden_width), bf16)] * 2,
        du,
        *middles,
        flops=2 * many * width * hidden_width,
    )

    def last_sum(shape):
        return lambda keep, taken: kernel_call(
            last_kernel, [shape_of(shape, f32)], keep, taken, limit=12
        )[0]

    contract_grad, contract_rounds = reduce_dp(
        contract_keep, contract_give, last_sum(contract_weight.shape)
    )
    expand_grad, expand_rounds = reduce_dp(
        expand_keep, expand_give, last_sum(expand_weight.shape)
    )
    dh1, dbranch = kernel_call(
        functools.partial(first_back_kernel, n_fs),
        [shape_of((size, width), f32), shape_of((size + small_rows, width), bf16)],
        *send_back(middle_parts),
        dh2,
        unit_first,
        inverse_first,
        vectors,
        sums_second,
        after=(contract_keep, expand_keep),
        limit=12,
    )
    branches = gather_fs(dbranch)
    dq, dk, dv, *input_parts = kernel_call(
        functools.partial(attend_back_kernel, n_fs, n_dp),
        [half_shape] * 3 + block_shapes(n_fs, size, width),
        *branches,
        *output_parts,
        queries,
        key_rows,
        values,
        chances,
        *attend_parts,
        after=(contract_rounds[0], expand_rounds[0]),
        flops=2 * many * width * heads_width * 4,
    )
    attend_keep, attend_give = kernel_call(
        functools.partial(attend_grad_kernel, n_fs, n_dp, bias_shape),
        [shape_of((n_dp // 2, 4 * share + small_rows, heads_width), bf16)] * 2,
        place,
        *inputs,
        *branches,
        mixed,
        dq,
        dk,
        dv,
        expand_sums,
        flops=2 * many * width * heads_width * 4,
    )
    (attend_grad, output_weight_grad, small_sums), _ = reduce_dp(
        attend_keep,
        attend_give,
        lambda keep, taken: kernel_call(
            joint_kernel,
            [
                shape_of(attend_weight.shape, f32),
                shape_of(output_weight.shape, f32),
                shape_of((small_rows, heads_width), f32),
            ],
            keep,
            taken,
            limit=12,
        ),
    )
    attend_bias_grad = small_sums[0, : attend_bias.size].reshape(bias_shape)
    expand_bias_grad = small_sums[n_vectors + 1, : expand_bias.size].reshape(expand_bias.shape)
    vector_grad = lax.dynamic_slice(small_sums, (1, fs_index * lanes), (n_vectors, lanes))

    (tokens_grad,) = kernel_call(
        functools.partial(tokens_grad_kernel, n_fs, n_dp),
        [shape_of((size, width), f32)],
        place,
        *send_back(input_parts),
        dh1,
        limit=12,
    )
    return (
        layer_output,
        tokens_grad,
        attend_grad,
        attend_bias_grad,
        output_weight_grad,
        expand_grad,
        expand_bias_grad,
        contract_grad,
        vector_grad,
    )


def solution(mesh):
    in_specs = (
        P(("dp", "fs"), None),
        P(None, "dp", "fs"),
        P(None, "fs", "dp"),
        P("fs", "dp"),
        P("dp", "fs"),
        P("fs", "dp"),
        P("fs", "dp"),
        P(None, ("dp", "fs")),
        P(),
        P(),
        P(("dp", "fs"), None),
    )
    out_specs = (
        P(("dp", "fs"), None),
        P(("dp", "fs"), None),
        P(None, "dp", "fs"),
        P(None, "fs", "dp"),
        P("fs", "dp"),
        P("dp", "fs"),
        P("fs", "dp"),
        P("fs", "dp"),
        P(None, ("dp", "fs")),
    )
    return jax.shard_map(
        on_device, mesh=mesh, in_specs=in_specs, out_specs=out_specs, check_vma=False
    )
```

```python
import functools

import jax
import jax.numpy as jnp
from jax import lax
from jax.experimental import pallas as pl
from jax.experimental.pallas import tpu as pltpu
from jax.sharding import PartitionSpec as P

masked_score = -1e30
norm_eps = 1e-12
root_half = 0.7071067811865476
inverse_root_tau = 0.3989422804014327
small_rows = 16
head_size = 64
f32 = jnp.float32
bf16 = jnp.bfloat16


def slot_order(count):
    order = [0]
    while len(order) < count:
        step = count // (2 * len(order))
        order = order + [entry | step for entry in order]
    bits = count.bit_length() - 1
    return [int(format(i, "b").zfill(bits)[::-1], 2) for i in range(count)]


def swap(part, axis_name, distance):
    count = lax.axis_size(axis_name)
    return lax.ppermute(part, axis_name, [(i, i ^ distance) for i in range(count)])


def gather_fs(part):
    return [part] + [swap(part, "fs", j) for j in range(1, lax.axis_size("fs"))]


def after(part, *earlier):
    return lax.optimization_barrier((part,) + earlier)[0]


def gather_lane(part, *earlier):
    held = {0: part}
    step = lax.axis_size("dp") // 2
    while step > 1:
        for entry, piece in list(held.items()):
            if entry and earlier:
                piece = after(piece, *earlier)
            held[entry | step] = swap(piece, "dp", step)
        step //= 2
    return held


def gather_cores(held, *earlier):
    both = dict(held)
    for entry, piece in held.items():
        if earlier:
            piece = after(piece, *earlier)
        both[entry | 1] = swap(piece, "dp", 1)
    return [both[entry] for entry in slot_order(len(both))]


def reduce_dp(keep, give, done):
    step = 1
    rounds = []
    while True:
        taken = swap(give, "dp", step)
        step *= 2
        if step == lax.axis_size("dp"):
            return done(Hot(keep), Hot(taken)), rounds
        half = Hot(shape_of((keep.shape[0] // 2,) + keep.shape[1:], bf16))
        keep, give = kernel_call(add_kernel, [half, half], Hot(keep), Hot(taken))
        rounds.append(give)


def reduce_direct(keep, give, *earlier):
    taken = swap(give, "dp", 1)
    lanes = keep.shape[0]
    parts = kernel_call(
        split_kernel,
        hot([shape_of(keep.shape[1:], f32)] + [shape_of(keep.shape[1:], bf16)] * (lanes - 1)),
        Hot(after(keep, *earlier)),
        Hot(taken),
    )
    order = slot_order(lanes)
    return [parts[0]] + [swap(parts[i], "dp", 2 * order[i]) for i in range(1, lanes)]


class Late:
    def __init__(self, source, target, semaphore):
        self.target = target
        self.shape = target.shape
        self.dtype = target.dtype
        self.copy = pltpu.make_async_copy(source, target, semaphore)
        self.copy.start()
        self.waits = True

    def ready(self):
        if self.waits:
            self.copy.wait()
            self.waits = False

    def __getitem__(self, where):
        self.ready()
        return self.target[where]


class Leaving:
    def __init__(self, source, target, semaphore):
        self.source = source
        self.shape = source.shape
        self.dtype = source.dtype
        self.copy = pltpu.make_async_copy(source, target, semaphore)
        self.sent = False

    def send(self):
        if not self.sent:
            self.copy.start()
            self.sent = True

    def __getitem__(self, where):
        return self.source[where]

    def __setitem__(self, where, value):
        self.source[where] = value


class Hot:
    def __init__(self, array):
        self.array = array


def hot(arrays):
    return [Hot(array) for array in arrays]


def kernel_call(body, outs, *args, extra=1.5, weight=0):
    def far(a):
        if isinstance(a, Hot):
            return False
        return a.ndim > 1

    def bare(a):
        return a.array if isinstance(a, Hot) else a

    late = [far(a) for a in args]
    leaving = [far(a) for a in outs]
    args = [bare(a) for a in args]
    outs = [bare(a) for a in outs]
    far_args = [a for a, b in zip(args, late) if b]
    far_outs = [a for a, b in zip(outs, leaving) if b]

    own = sum(a.size * a.dtype.itemsize for a in far_args + far_outs)
    limit = own + int(extra * 2**20) * max(1, lax.axis_size("fs") // 4)

    def whole(*refs):
        given, refs = refs[: len(args)], refs[len(args) :]
        out_refs, refs = refs[: len(outs)], refs[len(outs) :]
        items = []
        number = 0
        for ref, is_far in zip(given, late):
            if is_far:
                ref = Late(ref, refs[number], refs[-1].at[number])
                number += 1
            items.append(ref)
        targets = []
        for ref, is_far in zip(out_refs, leaving):
            if is_far:
                ref = Leaving(refs[number], ref, refs[-1].at[number])
                number += 1
            targets.append(ref)
        body(*items, *targets)
        for target in targets:
            if isinstance(target, Leaving):
                target.send()
        for item in items:
            if isinstance(item, Late):
                item.ready()
        for target in targets:
            if isinstance(target, Leaving):
                target.copy.wait()

    def place(a, is_far):
        if a.ndim == 1:
            return pltpu.SMEM
        return pltpu.HBM if is_far else pltpu.VMEM

    return pl.pallas_call(
        whole,
        out_shape=outs,
        in_specs=[pl.BlockSpec(memory_space=place(a, b)) for a, b in zip(args, late)],
        out_specs=[pl.BlockSpec(memory_space=place(a, b)) for a, b in zip(outs, leaving)],
        scratch_shapes=[pltpu.VMEM(a.shape, a.dtype) for a in far_args + far_outs]
        + [pltpu.SemaphoreType.DMA((max(1, len(far_args + far_outs)),))],
        compiler_params=pltpu.CompilerParams(vmem_limit_bytes=limit),
        cost_estimate=pl.CostEstimate(flops=weight, bytes_accessed=0, transcendentals=0),
    )(*args)


def send(ref):
    if isinstance(ref, Leaving):
        ref.send()


def shape_of(shape, kind):
    return jax.ShapeDtypeStruct(shape, kind)


def dot(left, right):
    return jnp.dot(left, right, preferred_element_type=f32)


def dot_nt(left, right):
    return lax.dot_general(left, right, (((1,), (1,)), ((), ())), preferred_element_type=f32)


def dot_tn(left, right):
    return lax.dot_general(left, right, (((0,), (0,)), ((), ())), preferred_element_type=f32)


def flip_blocks(blocks, index):
    step = 1
    while step < len(blocks):
        chosen = (index // step) % 2 == 1
        blocks = [jnp.where(chosen, blocks[i ^ step], blocks[i]) for i in range(len(blocks))]
        step *= 2
    return blocks


def split_columns(rows, count):
    size = rows.shape[1] // count
    return [rows[:, i * size : (i + 1) * size] for i in range(count)]


def to_slots(rows, index, count):
    blocks = flip_blocks(split_columns(rows, count), index)
    return jnp.concatenate([blocks[entry] for entry in slot_order(count)], axis=1)


def from_slots(rows, index, count):
    slots = split_columns(rows, count)
    order = slot_order(count)
    blocks = [slots[order.index(i)] for i in range(count)]
    return jnp.concatenate(flip_blocks(blocks, index), axis=1)


def row_mean(rows):
    return jnp.mean(rows, axis=1, keepdims=True)


def normalize(rows):
    centred = rows - row_mean(rows)
    inverse = lax.rsqrt(row_mean(centred * centred) + norm_eps)
    return (centred * inverse, inverse)


def normalize_back(upstream, gain, unit, inverse):
    scaled = upstream * gain
    return inverse * (scaled - row_mean(scaled) - unit * row_mean(scaled * unit))


def column_sum(rows):
    return jnp.sum(rows, axis=0, keepdims=True)


def stacked(refs):
    return jnp.concatenate([ref[...] for ref in refs], axis=0)


def beside(refs):
    return jnp.concatenate([ref[...] for ref in refs], axis=1)


def sum_blocks(refs):
    total = refs[0][...]
    for ref in refs[1:]:
        total = total + ref[...].astype(f32)
    return total


def store_blocks(refs, total):
    size = refs[0].shape[0]
    for i, ref in enumerate(refs):
        ref[...] = total[i * size : (i + 1) * size].astype(ref.dtype)


def store_columns(refs, place, total):
    size = refs[0].shape[0]
    width = total.shape[1]
    for i, ref in enumerate(refs):
        part = total[i * size : (i + 1) * size].astype(ref.dtype)
        ref[:, place * width : (place + 1) * width] = part


def add_kernel(left, right, keep, give):
    half = keep.shape[0]
    for out, start in ((give, half), (keep, 0)):
        for i in range(half):
            total = left[start + i].astype(f32) + right[start + i].astype(f32)
            out[i] = total.astype(out.dtype)


def split_kernel(left, right, *outs):
    for i, out in enumerate(outs):
        out[...] = (left[i].astype(f32) + right[i].astype(f32)).astype(out.dtype)


def last_kernel(left, right, out):
    out[...] = left[0].astype(f32) + right[0].astype(f32)


def block_shapes(count, rows, width):
    return hot([shape_of((rows, width), f32)] + [shape_of((rows, width), bf16)] * (count - 1))


def one_hot(target, width):
    column = lax.broadcasted_iota(jnp.int32, (target.shape[0], width), 1)
    return jnp.where(column == target, 1.0, 0.0).astype(bf16)


def entries(count):
    return lax.broadcasted_iota(jnp.int32, (count, 1), 0)


def pack_kernel(n_dp, place, weight, mixing, bias, vectors, expand_bias, tokens, out, x_out):
    rows, width = weight.shape[1:]
    for t in range(3):
        out[t * rows : (t + 1) * rows, :] = weight[t]
    out[3 * rows : 4 * rows, :] = mixing[...].T
    count, lanes = vectors.shape
    _, heads, part = bias.shape
    pads = small_rows // 2 - 2 * heads
    table = [
        dot(vectors[...], one_hot(entries(lanes) + place[1] * lanes, width)),
        dot(expand_bias[...], one_hot(entries(expand_bias.shape[1]), width)),
        jnp.zeros((small_rows // 2 - count - 1, width), f32),
    ]
    table = table + [dot(bias[t], one_hot(entries(part), width)) for t in range(2)]
    table = table + [jnp.zeros((pads, width), f32)]
    table = [rows for rows in table if rows.shape[0]]
    out[4 * rows :, :] = jnp.concatenate(table, axis=0).astype(bf16)
    send(out)
    x_out[...] = to_slots(tokens[...].astype(f32), place[0], n_dp).astype(bf16)


def pair_kernel(expand, contract, out):
    rows = expand.shape[0]
    out[:rows, :] = expand[...]
    out[rows:, :] = contract[...].T


def group_part(refs, t, count):
    rows = refs[0].shape[0] // count
    return jnp.concatenate([ref[t * rows : (t + 1) * rows, :] for ref in refs], axis=0)


def head_masks(width):
    lane = lax.broadcasted_iota(jnp.int32, (1, width), 1)
    return [lane // head_size == h for h in range(width // head_size)]


def attend_kernel(n_fs, n_dp, bias_shape, expand_share, place, *refs):
    w_refs, refs = refs[:n_dp], refs[n_dp:]
    x_refs, refs = refs[:n_fs], refs[n_fs:]
    allowed, q_out, k_out, v_out, o_out, p_out, expand_out = refs[:7]
    x_all, w_all, m_all = refs[7:10]
    outs = refs[10:]
    width = w_refs[0].shape[1]
    rows = (w_refs[0].shape[0] - small_rows) // 4
    order = slot_order(n_dp)
    size = x_refs[0].shape[0]
    for b, ref in enumerate(x_refs):
        x_all[b * size : (b + 1) * size, :] = ref[...]
    send(x_all)
    x = x_all[...]
    for t, ref in enumerate((w_all, w_all, w_all, m_all)):
        for s in range(n_dp):
            value = w_refs[s][t * rows : (t + 1) * rows, :]
            if t < 3:
                w_all[t, s * rows : (s + 1) * rows, :] = value
            else:
                m_all[s * rows : (s + 1) * rows, :] = value
    send(w_all)
    send(m_all)
    lows = [ref[4 * rows :, :] for ref in w_refs]
    _, heads, share = bias_shape
    taken = min(128, width)
    total = jnp.zeros((small_rows, width), f32)
    column = lax.broadcasted_iota(jnp.int32, (taken, width), 1)
    lane = entries(taken)
    for s in range(n_dp):
        target = jnp.where(lane < share, (place[0] ^ order[s]) * share + lane, -1)
        chosen = jnp.where(column % head_size == target, 1.0, 0.0).astype(bf16)
        total = total + dot(lows[s][:, :taken], chosen)
    row = entries(small_rows) - small_rows // 2
    head = lax.broadcasted_iota(jnp.int32, (small_rows, width), 1) // head_size
    biases = [column_sum(jnp.where(row == t * heads + head, total, 0.0)) for t in range(2)]
    if expand_share == rows:
        line = jnp.concatenate([low[6:7, :rows] for low in lows], axis=1).astype(f32)
        expand_out[...] = from_slots(line, place[0], n_dp)
    else:
        total = jnp.zeros((small_rows, expand_out.shape[1]), f32)
        for s in range(n_dp):
            owner = place[0] ^ order[s]
            target = jnp.where(lane < expand_share, lane + owner * expand_share, -1)
            total = total + dot(lows[s][:, :taken], one_hot(target, expand_out.shape[1]))
        expand_out[...] = total[6:7]
    parts = []
    for t, ref in enumerate((q_out, k_out, v_out)):
        part = dot(x, w_all[t])
        if t != 1:
            part = part + biases[t // 2]
        ref[...] = part.astype(bf16)
        send(ref)
    group = min(128, width)
    masks = head_masks(group)
    zero = jnp.zeros((), bf16)
    number = 0
    for b in range(n_fs):
        low, high = b * size, (b + 1) * size
        seen = allowed[b] > 0.0
        for g in range(0, width, group):
            q, k, v = (part[low:high, g : g + group] for part in (q_out, k_out, v_out))
            mixed = jnp.zeros((size, group), f32)
            for mask in masks:
                scores = dot_nt(jnp.where(mask, k, zero), q) * head_size**-0.5
                scores = jnp.where(seen, scores, masked_score)
                weights = jnp.exp(scores - jnp.max(scores, axis=0, keepdims=True))
                chances = weights * (1.0 / column_sum(weights))
                p_out[number] = chances
                number += 1
                mixed = mixed + dot_tn(chances.astype(bf16), jnp.where(mask, v, zero))
            o_out[low:high, g : g + group] = mixed.astype(bf16)
    send(p_out)
    send(o_out)
    total = dot_nt(o_out[...], m_all[...])
    small = jnp.concatenate([low[:, :rows] for low in lows], axis=1)
    for i, out in enumerate(outs):
        out[:size, :] = total[i * size : (i + 1) * size].astype(out.dtype)
        out[size:, :] = small.astype(out.dtype)


def first_norm_kernel(n_fs, *refs):
    parts, (x, vectors, mid, mid_low, unit_out, inverse_out) = refs[:n_fs], refs[n_fs:]
    total = sum_blocks(parts)
    size = x.shape[0]
    small = total[size : size + vectors.shape[0]]
    vectors[...] = small
    rows = x[...].astype(f32) + (total[:size] + small[0:1, :])
    unit, inverse = normalize(rows)
    middle = unit * small[1:2, :] + small[2:3, :]
    mid[...] = middle
    mid_low[...] = middle.astype(bf16)
    unit_out[...] = unit
    inverse_out[...] = inverse


def feed_kernel(n_fs, n_dp, *refs):
    mids, refs = refs[:n_fs], refs[n_fs:]
    weights, refs = refs[:n_dp], refs[n_dp:]
    bias, w1, w2, mid_all, hid_out, slope_out, outs = *refs[:6], refs[6:]
    size = mids[0].shape[0]
    for b, ref in enumerate(mids):
        mid_all[b * size : (b + 1) * size, :] = ref[...]
    rows = weights[0].shape[0] // 2
    for s, ref in enumerate(weights):
        w1[s * rows : (s + 1) * rows, :] = ref[:rows, :]
        w2[s * rows : (s + 1) * rows, :] = ref[rows:, :]
    send(mid_all)
    send(w1)
    send(w2)
    chunk = min(256, hid_out.shape[1])
    for c in range(0, hid_out.shape[1], chunk):
        value = dot(mid_all[...], w1[:, c : c + chunk]) + bias[:, c : c + chunk]
        cdf = 0.5 * (1.0 + lax.erf(value * root_half))
        density = jnp.exp(-0.5 * value * value) * inverse_root_tau
        hid_out[:, c : c + chunk] = (value * cdf).astype(bf16)
        slope_out[:, c : c + chunk] = (cdf + value * density).astype(bf16)
    send(hid_out)
    send(slope_out)
    chunk = min(256, w2.shape[0])
    for c in range(0, w2.shape[0], chunk):
        store_columns(outs, c // chunk, dot_nt(hid_out[...], w2[c : c + chunk, :]))


def second_norm_kernel(n_fs, n_dp, index, *refs):
    parts, refs = refs[:n_fs], refs[n_fs:]
    mid, vectors, grad, live, layer_out, dh, dh_low, sums = refs
    rows = mid[...] + (sum_blocks(parts) + vectors[3:4, :])
    unit, inverse = normalize(rows)
    alive = live[...]
    final = (unit * vectors[4:5, :] + vectors[5:6, :]) * alive
    layer_out[...] = from_slots(final, index[0], n_dp).astype(bf16)
    upstream = to_slots(grad[...].astype(f32), index[0], n_dp) * alive
    down = normalize_back(upstream, vectors[4:5, :], unit, inverse)
    low = down.astype(bf16)
    dh[...] = down
    dh_low[...] = low
    sums[0:1, :] = column_sum(low.astype(f32))
    sums[1:2, :] = column_sum(upstream * unit)
    sums[2:3, :] = column_sum(upstream)


def feed_back_kernel(n_fs, *refs):
    grads, refs = refs[:n_fs], refs[n_fs:]
    w2, slope, w1, grad_all, du_out, bias_out, outs = *refs[:6], refs[6:]
    size = grads[0].shape[0]
    for b, ref in enumerate(grads):
        grad_all[b * size : (b + 1) * size, :] = ref[...]
    send(grad_all)
    chunk = min(256, du_out.shape[1])
    for c in range(0, du_out.shape[1], chunk):
        du = dot(grad_all[...], w2[:, c : c + chunk]) * slope[:, c : c + chunk].astype(f32)
        du = du.astype(bf16)
        du_out[:, c : c + chunk] = du
        bias_out[:, c : c + chunk] = column_sum(du.astype(f32))
    send(du_out)
    chunk = min(256, w1.shape[0])
    for c in range(0, w1.shape[0], chunk):
        store_columns(outs, c // chunk, dot_nt(du_out[...], w1[c : c + chunk, :]))


def store_halves(keep, give, slot, value):
    half = keep.shape[0]
    target = keep if slot < half else give
    target[slot % half] = value.astype(target.dtype)


def contract_grad_kernel(n_dp, hid, grads, keep, give):
    left = hid[...].T
    size = grads.shape[1] // n_dp
    for s in reversed(range(0, n_dp, 2)):
        pair = dot(left, grads[:, s * size : (s + 2) * size])
        store_halves(keep, give, s, pair[:, :size])
        store_halves(keep, give, s + 1, pair[:, size:])


def expand_grad_kernel(n_dp, du, mids, keep, give):
    left = mids[...].T
    size = left.shape[0] // n_dp
    for s in reversed(range(n_dp)):
        store_halves(keep, give, s, dot(left[s * size : (s + 1) * size], du[...]))


def first_back_kernel(n_fs, *refs):
    parts, refs = refs[:n_fs], refs[n_fs:]
    dh2, unit, inverse, vectors, second, dh, out = refs
    upstream = dh2[...] + sum_blocks(parts)
    units = unit[...]
    down = normalize_back(upstream, vectors[1:2, :], units, inverse[...])
    low = down.astype(bf16)
    size = dh2.shape[0]
    dh[...] = down
    out[:size, :] = low
    out[size:, :] = jnp.concatenate(
        [
            column_sum(low.astype(f32)),
            column_sum(upstream * units),
            column_sum(upstream),
            second[...],
            jnp.zeros((small_rows - 3 - second.shape[0], upstream.shape[1]), f32),
        ],
        axis=0,
    ).astype(bf16)


def attend_back_kernel(n_fs, *refs):
    grads, refs = refs[:n_fs], refs[n_fs:]
    mixing, q_in, k_in, v_in, p_in, dq_out, dk_out, dv_out = refs
    width = q_in.shape[1]
    size = grads[0].shape[0] - small_rows
    group = min(128, width)
    masks = head_masks(group)
    zero = jnp.zeros((), bf16)
    rows = jnp.concatenate([ref[:size, :] for ref in grads], axis=0)
    grad_mixed = dot(rows, mixing[...]).astype(bf16)
    number = 0
    for b in range(n_fs):
        low, high = b * size, (b + 1) * size
        for g in range(0, width, group):
            q, k, v = (part[low:high, g : g + group] for part in (q_in, k_in, v_in))
            do = grad_mixed[low:high, g : g + group]
            dq = jnp.zeros((size, group), f32)
            dk = jnp.zeros((size, group), f32)
            dv = jnp.zeros((size, group), f32)
            for mask in masks:
                chances = p_in[number]
                number += 1
                masked_do = jnp.where(mask, do, zero)
                dp = dot_nt(v, masked_do)
                ds = chances * (dp - column_sum(dp * chances))
                ds = (ds * head_size**-0.5).astype(bf16)
                dv = dv + dot(chances.astype(bf16), masked_do)
                dq = dq + dot_tn(ds, jnp.where(mask, k, zero))
                dk = dk + dot(ds, jnp.where(mask, q, zero))
            dq_out[low:high, g : g + group] = dq.astype(bf16)
            dk_out[low:high, g : g + group] = dk.astype(bf16)
            dv_out[low:high, g : g + group] = dv.astype(bf16)


def input_back_kernel(weights, dq, dk, dv, *outs):
    width = weights.shape[1]
    chunk = min(256, width)
    for c in range(0, width, chunk):
        total = 0.0
        for t, part in enumerate((dq, dk, dv)):
            total = total + dot_nt(part[...], weights[t, c : c + chunk, :])
        store_columns(outs, c // chunk, total)


def attend_grad_kernel(n_fs, n_dp, bias_shape, place, *refs):
    grads, refs = refs[:n_fs], refs[n_fs:]
    x, mixed, dq, dk, dv, expand_sums, keep, give = refs
    size = grads[0].shape[0] - small_rows
    half = keep.shape[0]
    width = keep.shape[2]
    branch = jnp.concatenate([ref[:size, :] for ref in grads], axis=0)
    left = branch.T
    share = left.shape[0] // n_dp
    inputs = x[...].T
    for t, value in ((3, mixed), (0, dq), (1, dk), (2, dv)):
        result = dot(left if t == 3 else inputs, value[...]).astype(bf16)
        for s in range(n_dp):
            target = keep if s < half else give
            target[s % half, t * share : (t + 1) * share, :] = result[s * share : (s + 1) * share]
    vectors = jnp.zeros((small_rows, x.shape[1]), f32)
    for ref in grads:
        vectors = vectors + ref[size:, :].astype(f32)
    _, heads, part = bias_shape
    padding = jnp.zeros((small_rows - 2, width), f32)
    sums = [column_sum(ref[...].astype(f32)) for ref in (dq, dv)]
    sums = jnp.concatenate(sums + [padding], axis=0).astype(bf16)
    expand = expand_sums[...]
    expand_part = expand.shape[1] // n_dp
    if expand_part == share:
        expand = to_slots(expand, place[0], n_dp)
    column = entries(width)
    order = slot_order(n_dp)
    for s in range(n_dp):
        owner = place[0] ^ order[s]
        inside = (column % head_size) // part == owner
        lane = jnp.where(inside, column // head_size * part + column % part, -1)
        low = dot(sums, one_hot(lane, share))
        if expand_part == share:
            line = expand[:, s * share : (s + 1) * share]
        else:
            spot = entries(expand.shape[1])
            spot = jnp.where(spot // expand_part == owner, spot % expand_part, -1)
            rows = jnp.concatenate([expand, jnp.zeros((7, expand.shape[1]), f32)], axis=0)
            line = dot(rows.astype(bf16), one_hot(spot, share))[0:1]
        target = keep if s < half else give
        if share < width:
            target[s % half, 4 * share :, share:] = jnp.zeros((small_rows, width - share), bf16)
        target[s % half, 4 * share :, :share] = jnp.concatenate(
            [vectors[0:6, s * share : (s + 1) * share], line, low[0 : small_rows - 7]], axis=0
        ).astype(bf16)


def joint_kernel(n_parts, place, *refs):
    parts, (attend_out, output_out, bias_out, expand_out, vectors_out) = (
        refs[:n_parts],
        refs[n_parts:],
    )
    total = sum_blocks(parts)
    rows = attend_out.shape[1]
    for t in range(3):
        attend_out[t] = total[t * rows : (t + 1) * rows]
    send(attend_out)
    output_out[...] = total[3 * rows : 4 * rows].T
    small = total[4 * rows :]
    _, heads, part = bias_out.shape
    for t in range(2):
        for h in range(heads):
            bias_out[t, h : h + 1, :] = small[7 + t : 8 + t, h * part : (h + 1) * part]
    expand_out[...] = small[6:7, : expand_out.shape[1]]
    count, lanes = vectors_out.shape
    found = jnp.zeros((count, lanes), f32)
    for i in range(rows // lanes):
        found = found + jnp.where(place[1] == i, small[:count, i * lanes : (i + 1) * lanes], 0.0)
    vectors_out[...] = found


def tokens_grad_kernel(n_fs, n_dp, index, *refs):
    parts, (dh, out) = refs[:n_fs], refs[n_fs:]
    out[...] = from_slots(dh[...] + sum_blocks(parts), index[0], n_dp)


def segment_kernel(n_fs, place, lengths, owners, allowed, live):
    size = live.shape[0]
    slot = lax.broadcasted_iota(jnp.int32, (8, size), 1)
    blocks = [place[0] * n_fs + (place[1] ^ i) for i in range(n_fs)]

    def add(s, carry):
        result = []
        for block, (offset, found) in zip(blocks, carry):
            count = jnp.where(owners[s] == block, lengths[s], 0)
            found = jnp.where((slot >= offset) & (slot < offset + count), s, found)
            result.append((offset + count, found))
        return tuple(result)

    start = tuple((jnp.int32(0), jnp.full((8, size), -1, jnp.int32)) for _ in blocks)
    for i, (_, found) in enumerate(lax.fori_loop(0, lengths.shape[0], add, start)):
        along = jnp.broadcast_to(found[0:1].astype(f32), (size, size))
        down = along.T
        allowed[i] = jnp.where((along == down) & (down >= 0.0), 1.0, 0.0)
        if i == 0:
            live[...] = jnp.where(down[:, 0:1] >= 0.0, 1.0, 0.0)


def on_device(
    tokens,
    attend_weight,
    attend_bias,
    output_weight,
    expand_weight,
    expand_bias,
    contract_weight,
    layer_vectors,
    sequence_lengths,
    sequence_owner,
    output_grad,
):
    size, width = tokens.shape
    n_fs = lax.axis_size("fs")
    n_dp = lax.axis_size("dp")
    fs_index = lax.axis_index("fs")
    dp_index = lax.axis_index("dp")
    place = jnp.stack([dp_index, fs_index]).astype(jnp.int32)
    many = n_fs * size
    share = width // n_dp
    heads_width = attend_weight.shape[2]
    hidden_width = expand_weight.shape[1]
    n_vectors, lanes = layer_vectors.shape
    bias_shape = attend_bias.shape

    def send_back(parts):
        return [parts[0]] + [swap(parts[j], "fs", j) for j in range(1, n_fs)]

    attend_part, own_rows = kernel_call(
        functools.partial(pack_kernel, n_dp),
        [
            shape_of((4 * share + small_rows, heads_width), bf16),
            shape_of((size, width), bf16),
        ],
        place,
        attend_weight,
        output_weight,
        attend_bias,
        layer_vectors,
        expand_bias,
        tokens,
        extra=56,
    )
    attend_lane = gather_lane(attend_part)
    inputs = gather_fs(own_rows)
    attend_parts = gather_cores(attend_lane)
    (feed_part,) = kernel_call(
        pair_kernel,
        [shape_of((2 * share, hidden_width), bf16)],
        after(expand_weight, attend_part),
        contract_weight,
    )
    feed_lane = gather_lane(after(feed_part, *attend_lane.values()))
    allowed, live = kernel_call(
        functools.partial(segment_kernel, n_fs),
        hot([shape_of((n_fs, size, size), f32), shape_of((size, 1), f32)]),
        place,
        sequence_lengths,
        sequence_owner,
    )

    half_shape = shape_of((many, heads_width), bf16)
    n_scores = n_fs * heads_width // head_size
    (
        queries,
        key_rows,
        values,
        mixed,
        chances,
        expand_row,
        x_all,
        w_all,
        mixing,
        *branch_parts,
    ) = kernel_call(
        functools.partial(attend_kernel, n_fs, n_dp, bias_shape, expand_bias.size),
        [half_shape] * 4
        + [shape_of((n_scores, size, size), f32), Hot(shape_of((1, hidden_width), f32))]
        + [
            shape_of((many, width), bf16),
            shape_of((3, width, heads_width), bf16),
            shape_of((width, heads_width), bf16),
        ]
        + block_shapes(n_fs, size + small_rows, width),
        place,
        *hot(attend_parts),
        *hot(inputs),
        Hot(allowed),
        extra=4,
    )
    vectors, middle, middle_low, unit_first, inverse_first = kernel_call(
        functools.partial(first_norm_kernel, n_fs),
        hot(
            [
                shape_of((n_vectors, width), f32),
                shape_of((size, width), f32),
                shape_of((size, width), bf16),
                shape_of((size, width), f32),
                shape_of((size, 1), f32),
            ]
        ),
        *hot(send_back(branch_parts)),
        Hot(after(own_rows, *list(feed_lane.values())[1:-1])),
    )
    middles = gather_fs(middle_low)
    feed_parts = gather_cores(feed_lane, middles[1])
    wide = shape_of((many, hidden_width), bf16)
    w1, w2, mid_all, hidden, slope, *result_parts = kernel_call(
        functools.partial(feed_kernel, n_fs, n_dp),
        [
            shape_of((width, hidden_width), bf16),
            shape_of((width, hidden_width), bf16),
            shape_of((many, width), bf16),
            wide,
            wide,
        ]
        + block_shapes(n_fs, size, width),
        *hot(middles),
        *hot(feed_parts),
        Hot(expand_row),
        extra=3,
    )
    layer_output, dh2, dffn, sums_second = kernel_call(
        functools.partial(second_norm_kernel, n_fs, n_dp),
        [
            shape_of((size, width), bf16),
            Hot(shape_of((size, width), f32)),
            Hot(shape_of((size, width), bf16)),
            Hot(shape_of((3, width), f32)),
        ],
        place,
        *hot(send_back(result_parts)),
        Hot(middle),
        Hot(vectors),
        output_grad,
        Hot(live),
        extra=3,
    )
    dffns = gather_fs(dffn)
    dffn_all, du, expand_sums, *middle_parts = kernel_call(
        functools.partial(feed_back_kernel, n_fs),
        [shape_of((many, width), bf16), wide, Hot(shape_of((1, hidden_width), f32))]
        + block_shapes(n_fs, size, width),
        *hot(dffns),
        w2,
        slope,
        w1,
        extra=3,
    )
    back_parts = send_back(middle_parts)
    contract_keep, contract_give = kernel_call(
        functools.partial(contract_grad_kernel, n_dp),
        hot([shape_of((n_dp // 2, hidden_width, share), bf16)] * 2),
        hidden,
        dffn_all,
        extra=2,
    )
    expand_keep, expand_give = kernel_call(
        functools.partial(expand_grad_kernel, n_dp),
        hot([shape_of((n_dp // 2, share, hidden_width), bf16)] * 2),
        du,
        mid_all,
        extra=2,
    )

    def last_sum(shape):
        return lambda keep, taken: kernel_call(
            last_kernel, [shape_of(shape, f32)], keep, taken
        )[0]

    contract_grad, contract_rounds = reduce_dp(
        contract_keep, contract_give, last_sum(contract_weight.shape)
    )
    expand_grad, expand_rounds = reduce_dp(
        expand_keep, expand_give, last_sum(expand_weight.shape)
    )
    dh1, dbranch = kernel_call(
        functools.partial(first_back_kernel, n_fs),
        hot([shape_of((size, width), f32), shape_of((size + small_rows, width), bf16)]),
        *hot(back_parts),
        Hot(after(dh2, contract_keep, expand_keep)),
        Hot(unit_first),
        Hot(inverse_first),
        Hot(vectors),
        Hot(sums_second),
        weight=3 * 10**10,
    )
    branches = gather_fs(dbranch)
    dq, dk, dv = kernel_call(
        functools.partial(attend_back_kernel, n_fs),
        hot([half_shape] * 3),
        *hot(branches),
        after(mixing, contract_rounds[-1]),
        queries,
        key_rows,
        values,
        chances,
        extra=2.5,
    )
    attend_keep, attend_give = kernel_call(
        functools.partial(attend_grad_kernel, n_fs, n_dp, bias_shape),
        hot([shape_of((n_dp // 2, 4 * share + small_rows, heads_width), bf16)] * 2),
        place,
        *hot(branches),
        after(x_all, expand_grad, contract_grad),
        mixed,
        Hot(dq),
        Hot(dk),
        Hot(dv),
        Hot(expand_sums),
        extra=3,
    )
    input_parts = kernel_call(
        input_back_kernel,
        block_shapes(n_fs, size, width),
        after(w_all, attend_keep),
        Hot(dq),
        Hot(dk),
        Hot(dv),
    )
    joint = reduce_direct(attend_keep, attend_give, input_parts[0])
    small_outs = [
        shape_of(attend_bias.shape, f32),
        shape_of(expand_bias.shape, f32),
        shape_of(layer_vectors.shape, f32),
    ]
    attend_grad, output_weight_grad, attend_bias_grad, expand_bias_grad, vector_grad = kernel_call(
        functools.partial(joint_kernel, len(joint)),
        [shape_of(attend_weight.shape, f32), shape_of(output_weight.shape, f32)] + hot(small_outs),
        place,
        *hot(joint),
    )
    (tokens_grad,) = kernel_call(
        functools.partial(tokens_grad_kernel, n_fs, n_dp),
        [shape_of((size, width), f32)],
        place,
        *hot(send_back(input_parts)),
        Hot(after(dh1, expand_grad)),
    )
    return (
        layer_output,
        tokens_grad,
        attend_grad,
        attend_bias_grad,
        output_weight_grad,
        expand_grad,
        expand_bias_grad,
        contract_grad,
        vector_grad,
    )


def solution(mesh):
    in_specs = (
        P(("dp", "fs"), None),
        P(None, "dp", "fs"),
        P(None, "fs", "dp"),
        P("fs", "dp"),
        P("dp", "fs"),
        P("fs", "dp"),
        P("fs", "dp"),
        P(None, ("dp", "fs")),
        P(),
        P(),
        P(("dp", "fs"), None),
    )
    out_specs = (
        P(("dp", "fs"), None),
        P(("dp", "fs"), None),
        P(None, "dp", "fs"),
        P(None, "fs", "dp"),
        P("fs", "dp"),
        P("dp", "fs"),
        P("fs", "dp"),
        P("fs", "dp"),
        P(None, ("dp", "fs")),
    )
    return jax.shard_map(
        on_device, mesh=mesh, in_specs=in_specs, out_specs=out_specs, check_vma=False
    )
```

```python
import functools

import jax
import jax.numpy as jnp
from jax import lax
from jax.experimental import pallas as pl
from jax.experimental.pallas import tpu as pltpu
from jax.sharding import PartitionSpec as P

masked_score = -1e30
norm_eps = 1e-12
root_half = 0.7071067811865476
inverse_root_tau = 0.3989422804014327
small_rows = 16
head_size = 64
f32 = jnp.float32
bf16 = jnp.bfloat16


def slot_order(count):
    order = [0]
    while len(order) < count:
        step = count // (2 * len(order))
        order = order + [entry | step for entry in order]
    bits = count.bit_length() - 1
    return [int(format(i, "b").zfill(bits)[::-1], 2) for i in range(count)]


def swap(part, axis_name, distance):
    count = lax.axis_size(axis_name)
    return lax.ppermute(part, axis_name, [(i, i ^ distance) for i in range(count)])


def gather_fs(part):
    return [part] + [swap(part, "fs", j) for j in range(1, lax.axis_size("fs"))]


def after(part, *earlier):
    return lax.optimization_barrier((part,) + earlier)[0]


def gather_lane(part, *earlier):
    held = {0: part}
    steps = []
    step = lax.axis_size("dp") // 2
    while step > 1:
        steps.append(step)
        held[step] = swap(part, "dp", step)
        step //= 2
    direct = list(held.values())[1:] + list(earlier)
    for i, step in enumerate(steps):
        for entry in [e for e in held if e % steps[i - 1] == 0 and e and i]:
            if entry | step not in held:
                held[entry | step] = swap(after(held[entry], *direct), "dp", step)
    return held


def gather_cores(held, *earlier):
    both = dict(held)
    for entry, piece in held.items():
        if earlier:
            piece = after(piece, *earlier)
        both[entry | 1] = swap(piece, "dp", 1)
    return [both[entry] for entry in slot_order(len(both))]


def sum_cores(keep, give):
    taken = swap(give, "dp", 1)
    half = Hot(shape_of((keep.shape[0] // 2,) + keep.shape[1:], bf16))
    return kernel_call(add_kernel, [half, half], Hot(keep), Hot(taken))


def sum_lanes(keep, give, done):
    step = 2
    rounds = []
    while True:
        taken = swap(give, "dp", step)
        step *= 2
        if step == lax.axis_size("dp"):
            return done(Hot(keep), Hot(taken)), rounds
        half = Hot(shape_of((keep.shape[0] // 2,) + keep.shape[1:], bf16))
        keep, give = kernel_call(add_kernel, [half, half], Hot(keep), Hot(taken))
        rounds.append(give)


class Late:
    def __init__(self, source, target, semaphore):
        self.target = target
        self.shape = target.shape
        self.dtype = target.dtype
        self.copy = pltpu.make_async_copy(source, target, semaphore)
        self.copy.start()
        self.waits = True

    def ready(self):
        if self.waits:
            self.copy.wait()
            self.waits = False

    def __getitem__(self, where):
        self.ready()
        return self.target[where]


class Leaving:
    def __init__(self, source, target, semaphore):
        self.source = source
        self.shape = source.shape
        self.dtype = source.dtype
        self.copy = pltpu.make_async_copy(source, target, semaphore)
        self.sent = False

    def send(self):
        if not self.sent:
            self.copy.start()
            self.sent = True

    def __getitem__(self, where):
        return self.source[where]

    def __setitem__(self, where, value):
        self.source[where] = value


class Hot:
    def __init__(self, array):
        self.array = array


def hot(arrays):
    return [Hot(array) for array in arrays]


def kernel_call(body, outs, *args, extra=1.5, aliases=None):
    def far(a):
        if isinstance(a, Hot):
            return False
        return a.ndim > 1

    def bare(a):
        return a.array if isinstance(a, Hot) else a

    late = [far(a) for a in args]
    leaving = [far(a) for a in outs]
    args = [bare(a) for a in args]
    outs = [bare(a) for a in outs]
    far_args = [a for a, b in zip(args, late) if b]
    far_outs = [a for a, b in zip(outs, leaving) if b]

    own = sum(a.size * a.dtype.itemsize for a in far_args + far_outs)
    limit = own + int(extra * 2**20) * max(1, lax.axis_size("fs") // 4)

    def whole(*refs):
        given, refs = refs[: len(args)], refs[len(args) :]
        out_refs, refs = refs[: len(outs)], refs[len(outs) :]
        items = []
        number = 0
        for ref, is_far in zip(given, late):
            if is_far:
                ref = Late(ref, refs[number], refs[-1].at[number])
                number += 1
            items.append(ref)
        targets = []
        for ref, is_far in zip(out_refs, leaving):
            if is_far:
                ref = Leaving(refs[number], ref, refs[-1].at[number])
                number += 1
            targets.append(ref)
        body(*items, *targets)
        for target in targets:
            if isinstance(target, Leaving):
                target.send()
        for item in items:
            if isinstance(item, Late):
                item.ready()
        for target in targets:
            if isinstance(target, Leaving):
                target.copy.wait()

    def place(a, is_far):
        if a.ndim == 1:
            return pltpu.SMEM
        return pltpu.HBM if is_far else pltpu.VMEM

    return pl.pallas_call(
        whole,
        out_shape=outs,
        in_specs=[pl.BlockSpec(memory_space=place(a, b)) for a, b in zip(args, late)],
        out_specs=[pl.BlockSpec(memory_space=place(a, b)) for a, b in zip(outs, leaving)],
        scratch_shapes=[pltpu.VMEM(a.shape, a.dtype) for a in far_args + far_outs]
        + [pltpu.SemaphoreType.DMA((max(1, len(far_args + far_outs)),))],
        compiler_params=pltpu.CompilerParams(vmem_limit_bytes=limit),
        cost_estimate=pl.CostEstimate(flops=0, bytes_accessed=0, transcendentals=0),
        input_output_aliases=aliases or {},
    )(*args)


def send(ref):
    if isinstance(ref, Leaving):
        ref.send()


def shape_of(shape, kind):
    return jax.ShapeDtypeStruct(shape, kind)


def dot(left, right):
    return jnp.dot(left, right, preferred_element_type=f32)


def dot_nt(left, right):
    return lax.dot_general(left, right, (((1,), (1,)), ((), ())), preferred_element_type=f32)


def dot_tn(left, right):
    return lax.dot_general(left, right, (((0,), (0,)), ((), ())), preferred_element_type=f32)


def flip_blocks(blocks, index):
    step = 1
    while step < len(blocks):
        chosen = (index // step) % 2 == 1
        blocks = [jnp.where(chosen, blocks[i ^ step], blocks[i]) for i in range(len(blocks))]
        step *= 2
    return blocks


def split_columns(rows, count):
    size = rows.shape[1] // count
    return [rows[:, i * size : (i + 1) * size] for i in range(count)]


def to_slots(rows, index, count):
    blocks = flip_blocks(split_columns(rows, count), index)
    return jnp.concatenate([blocks[entry] for entry in slot_order(count)], axis=1)


def from_slots(rows, index, count):
    slots = split_columns(rows, count)
    order = slot_order(count)
    blocks = [slots[order.index(i)] for i in range(count)]
    return jnp.concatenate(flip_blocks(blocks, index), axis=1)


def row_mean(rows):
    return jnp.mean(rows, axis=1, keepdims=True)


def normalize(rows):
    centred = rows - row_mean(rows)
    inverse = lax.rsqrt(row_mean(centred * centred) + norm_eps)
    return (centred * inverse, inverse)


def normalize_back(upstream, gain, unit, inverse):
    scaled = upstream * gain
    return inverse * (scaled - row_mean(scaled) - unit * row_mean(scaled * unit))


def column_sum(rows):
    return jnp.sum(rows, axis=0, keepdims=True)


def stacked(refs):
    return jnp.concatenate([ref[...] for ref in refs], axis=0)


def beside(refs):
    return jnp.concatenate([ref[...] for ref in refs], axis=1)


def sum_blocks(refs):
    total = refs[0][...]
    for ref in refs[1:]:
        total = total + ref[...].astype(f32)
    return total


def store_blocks(refs, total):
    size = refs[0].shape[0]
    for i, ref in enumerate(refs):
        ref[...] = total[i * size : (i + 1) * size].astype(ref.dtype)


def store_columns(refs, place, total):
    size = refs[0].shape[0]
    width = total.shape[1]
    for i, ref in enumerate(refs):
        part = total[i * size : (i + 1) * size].astype(ref.dtype)
        ref[:, place * width : (place + 1) * width] = part


def add_kernel(left, right, keep, give):
    half = keep.shape[0]
    for out, start in ((give, half), (keep, 0)):
        for i in range(half):
            total = left[start + i].astype(f32) + right[start + i].astype(f32)
            out[i] = total.astype(out.dtype)


def last_kernel(left, right, out):
    out[...] = left[0].astype(f32) + right[0].astype(f32)


def block_shapes(count, rows, width):
    return hot([shape_of((rows, width), f32)] + [shape_of((rows, width), bf16)] * (count - 1))


def one_hot(target, width):
    column = lax.broadcasted_iota(jnp.int32, (target.shape[0], width), 1)
    return jnp.where(column == target, 1.0, 0.0).astype(bf16)


def entries(count):
    return lax.broadcasted_iota(jnp.int32, (count, 1), 0)


def pack_kernel(weight, mixing, bias, vectors, expand_bias, out):
    place = own_place()
    rows, width = weight.shape[1:]
    for t in range(3):
        out[t * rows : (t + 1) * rows, :] = weight[t]
    out[3 * rows : 4 * rows, :] = mixing[...].T
    count, lanes = vectors.shape
    _, heads, part = bias.shape
    pads = small_rows // 2 - 2 * heads
    table = [
        dot(vectors[...], one_hot(entries(lanes) + place[1] * lanes, width)),
        dot(expand_bias[...], one_hot(entries(expand_bias.shape[1]), width)),
        jnp.zeros((small_rows // 2 - count - 1, width), f32),
    ]
    table = table + [dot(bias[t], one_hot(entries(part), width)) for t in range(2)]
    table = table + [jnp.zeros((pads, width), f32)]
    table = [rows for rows in table if rows.shape[0]]
    out[4 * rows :, :] = jnp.concatenate(table, axis=0).astype(bf16)


def slots_kernel(n_dp, tokens, out):
    out[...] = to_slots(tokens[...].astype(f32), own_place()[0], n_dp).astype(bf16)


def pair_kernel(expand, contract, out):
    rows = expand.shape[0]
    out[:rows, :] = expand[...]
    out[rows:, :] = contract[...].T


def group_part(refs, t, count):
    rows = refs[0].shape[0] // count
    return jnp.concatenate([ref[t * rows : (t + 1) * rows, :] for ref in refs], axis=0)


def own_place():
    return (lax.axis_index("dp"), lax.axis_index("fs"))


def head_masks(width):
    lane = lax.broadcasted_iota(jnp.int32, (1, width), 1)
    return [lane // head_size == h for h in range(width // head_size)]


def attend_kernel(n_fs, n_dp, bias_shape, expand_share, *refs):
    place = own_place()
    w_refs, refs = refs[:n_dp], refs[n_dp:]
    x_refs, refs = refs[:n_fs], refs[n_fs:]
    allowed, q_out, k_out, v_out, o_out, p_out, expand_out = refs[:7]
    x_all, w_all, m_all = refs[7:10]
    outs = refs[10:]
    width = w_refs[0].shape[1]
    rows = (w_refs[0].shape[0] - small_rows) // 4
    order = slot_order(n_dp)
    size = x_refs[0].shape[0]
    for b, ref in enumerate(x_refs):
        x_all[b * size : (b + 1) * size, :] = ref[...]
    send(x_all)
    x = x_all[...]
    for t, ref in enumerate((w_all, w_all, w_all, m_all)):
        for s in range(n_dp):
            value = w_refs[s][t * rows : (t + 1) * rows, :]
            if t < 3:
                w_all[t, s * rows : (s + 1) * rows, :] = value
            else:
                m_all[s * rows : (s + 1) * rows, :] = value
    send(w_all)
    send(m_all)
    lows = [ref[4 * rows :, :] for ref in w_refs]
    _, heads, share = bias_shape
    taken = min(128, width)
    total = jnp.zeros((small_rows, width), f32)
    column = lax.broadcasted_iota(jnp.int32, (taken, width), 1)
    lane = entries(taken)
    for s in range(n_dp):
        target = jnp.where(lane < share, (place[0] ^ order[s]) * share + lane, -1)
        chosen = jnp.where(column % head_size == target, 1.0, 0.0).astype(bf16)
        total = total + dot(lows[s][:, :taken], chosen)
    row = entries(small_rows) - small_rows // 2
    head = lax.broadcasted_iota(jnp.int32, (small_rows, width), 1) // head_size
    biases = [column_sum(jnp.where(row == t * heads + head, total, 0.0)) for t in range(2)]
    if expand_share == rows:
        line = jnp.concatenate([low[6:7, :rows] for low in lows], axis=1).astype(f32)
        expand_out[...] = from_slots(line, place[0], n_dp)
    else:
        total = jnp.zeros((small_rows, expand_out.shape[1]), f32)
        for s in range(n_dp):
            owner = place[0] ^ order[s]
            target = jnp.where(lane < expand_share, lane + owner * expand_share, -1)
            total = total + dot(lows[s][:, :taken], one_hot(target, expand_out.shape[1]))
        expand_out[...] = total[6:7]
    parts = []
    for t, ref in enumerate((q_out, k_out, v_out)):
        part = dot(x, w_all[t])
        if t != 1:
            part = part + biases[t // 2]
        ref[...] = part.astype(bf16)
        send(ref)
    group = min(128, width)
    masks = head_masks(group)
    zero = jnp.zeros((), bf16)
    number = 0
    for b in range(n_fs):
        low, high = b * size, (b + 1) * size
        seen = allowed[b] > 0.0
        for g in range(0, width, group):
            q, k, v = (part[low:high, g : g + group] for part in (q_out, k_out, v_out))
            mixed = jnp.zeros((size, group), f32)
            for mask in masks:
                scores = dot_nt(jnp.where(mask, k, zero), q) * head_size**-0.5
                scores = jnp.where(seen, scores, masked_score)
                weights = jnp.exp(scores - jnp.max(scores, axis=0, keepdims=True))
                chances = weights * (1.0 / column_sum(weights))
                p_out[number] = chances
                number += 1
                mixed = mixed + dot_tn(chances.astype(bf16), jnp.where(mask, v, zero))
            o_out[low:high, g : g + group] = mixed.astype(bf16)
    send(p_out)
    send(o_out)
    total = dot_nt(o_out[...], m_all[...])
    small = jnp.concatenate([low[:, :rows] for low in lows], axis=1)
    for i, out in enumerate(outs):
        out[:size, :] = total[i * size : (i + 1) * size].astype(out.dtype)
        out[size:, :] = small.astype(out.dtype)


def first_norm_kernel(n_fs, *refs):
    parts, (x, vectors, mid, mid_low, unit_out, inverse_out) = refs[:n_fs], refs[n_fs:]
    total = sum_blocks(parts)
    size = x.shape[0]
    small = total[size : size + vectors.shape[0]]
    vectors[...] = small
    rows = x[...].astype(f32) + (total[:size] + small[0:1, :])
    unit, inverse = normalize(rows)
    middle = unit * small[1:2, :] + small[2:3, :]
    mid[...] = middle
    mid_low[...] = middle.astype(bf16)
    unit_out[...] = unit
    inverse_out[...] = inverse


def feed_kernel(n_fs, n_dp, *refs):
    mids, refs = refs[:n_fs], refs[n_fs:]
    weights, refs = refs[:n_dp], refs[n_dp:]
    bias, w1, w2, mid_all, hid_out, inner_out, outs = *refs[:6], refs[6:]
    size = mids[0].shape[0]
    for b, ref in enumerate(mids):
        mid_all[b * size : (b + 1) * size, :] = ref[...]
    rows = weights[0].shape[0] // 2
    for s, ref in enumerate(weights):
        w1[s * rows : (s + 1) * rows, :] = ref[:rows, :]
        w2[s * rows : (s + 1) * rows, :] = ref[rows:, :]
    send(mid_all)
    send(w1)
    send(w2)
    chunk = min(256, hid_out.shape[1])
    for c in range(0, hid_out.shape[1], chunk):
        value = dot(mid_all[...], w1[:, c : c + chunk]) + bias[:, c : c + chunk]
        inner_out[:, c : c + chunk] = value
        cdf = 0.5 * (1.0 + lax.erf(value * root_half))
        hid_out[:, c : c + chunk] = (value * cdf).astype(bf16)
    send(hid_out)
    chunk = min(256, w2.shape[0])
    for c in range(0, w2.shape[0], chunk):
        store_columns(outs, c // chunk, dot_nt(hid_out[...], w2[c : c + chunk, :]))


def second_norm_kernel(n_fs, n_dp, *refs):
    index = own_place()
    parts, refs = refs[:n_fs], refs[n_fs:]
    mid, vectors, grad, live, layer_out, dh, dh_low, sums = refs
    rows = mid[...] + (sum_blocks(parts) + vectors[3:4, :])
    unit, inverse = normalize(rows)
    alive = live[...]
    final = (unit * vectors[4:5, :] + vectors[5:6, :]) * alive
    layer_out[...] = from_slots(final, index[0], n_dp).astype(bf16)
    upstream = to_slots(grad[...].astype(f32), index[0], n_dp) * alive
    down = normalize_back(upstream, vectors[4:5, :], unit, inverse)
    low = down.astype(bf16)
    dh[...] = down
    dh_low[...] = low
    sums[0:1, :] = column_sum(low.astype(f32))
    sums[1:2, :] = column_sum(upstream * unit)
    sums[2:3, :] = column_sum(upstream)


def feed_back_kernel(n_fs, *refs):
    grads, refs = refs[:n_fs], refs[n_fs:]
    w2, slope, w1, du_out, bias_out, outs = *refs[:5], refs[5:]
    rows = stacked(grads)
    chunk = min(256, du_out.shape[1])
    for c in range(0, du_out.shape[1], chunk):
        du = dot(rows, w2[:, c : c + chunk]) * slope[:, c : c + chunk].astype(f32)
        du = du.astype(bf16)
        du_out[:, c : c + chunk] = du
        bias_out[:, c : c + chunk] = column_sum(du.astype(f32))
    send(du_out)
    chunk = min(256, w1.shape[0])
    for c in range(0, w1.shape[0], chunk):
        store_columns(outs, c // chunk, dot_nt(du_out[...], w1[c : c + chunk, :]))


def slot_refs(keep, give):
    half = keep.shape[0]
    return [keep.at[s] for s in range(half)] + [give.at[s] for s in range(half)]


def contract_grad_kernel(n_fs, turned, *refs):
    grads, slots = stacked(refs[:n_fs]), slot_refs(*refs[n_fs:])
    left = turned[...]
    size = slots[0].shape[1]
    for s in reversed(range(0, len(slots), 2)):
        pair = dot(left, grads[:, s * size : (s + 2) * size])
        slots[s][...] = pair[:, :size].astype(bf16)
        slots[s + 1][...] = pair[:, size:].astype(bf16)


def expand_grad_kernel(du, turned, keep, give):
    left = turned[...]
    size = keep.shape[1]
    for s, slot in reversed(list(enumerate(slot_refs(keep, give)))):
        slot[...] = dot(left[s * size : (s + 1) * size], du[...]).astype(bf16)


def first_back_kernel(n_fs, *refs):
    parts, refs = refs[:n_fs], refs[n_fs:]
    dh2, unit, inverse, vectors, second, dh, out = refs
    upstream = dh2[...] + sum_blocks(parts)
    units = unit[...]
    down = normalize_back(upstream, vectors[1:2, :], units, inverse[...])
    low = down.astype(bf16)
    size = dh2.shape[0]
    dh[...] = down
    out[:size, :] = low
    out[size:, :] = jnp.concatenate(
        [
            column_sum(low.astype(f32)),
            column_sum(upstream * units),
            column_sum(upstream),
            second[...],
            jnp.zeros((small_rows - 3 - second.shape[0], upstream.shape[1]), f32),
        ],
        axis=0,
    ).astype(bf16)


def attend_back_kernel(n_fs, *refs):
    grads, refs = refs[:n_fs], refs[n_fs:]
    mixing, q_in, k_in, v_in, p_in, dq_out, dk_out, dv_out = refs
    width = q_in.shape[1]
    size = grads[0].shape[0] - small_rows
    group = min(128, width)
    masks = head_masks(group)
    zero = jnp.zeros((), bf16)
    rows = jnp.concatenate([ref[:size, :] for ref in grads], axis=0)
    grad_mixed = dot(rows, mixing[...]).astype(bf16)
    number = 0
    for b in range(n_fs):
        low, high = b * size, (b + 1) * size
        for g in range(0, width, group):
            q, k, v = (part[low:high, g : g + group] for part in (q_in, k_in, v_in))
            do = grad_mixed[low:high, g : g + group]
            dq = jnp.zeros((size, group), f32)
            dk = jnp.zeros((size, group), f32)
            dv = jnp.zeros((size, group), f32)
            for mask in masks:
                chances = p_in[number]
                number += 1
                masked_do = jnp.where(mask, do, zero)
                dp = dot_nt(v, masked_do)
                ds = chances * (dp - column_sum(dp * chances))
                ds = (ds * head_size**-0.5).astype(bf16)
                dv = dv + dot(chances.astype(bf16), masked_do)
                dq = dq + dot_tn(ds, jnp.where(mask, k, zero))
                dk = dk + dot(ds, jnp.where(mask, q, zero))
            dq_out[low:high, g : g + group] = dq.astype(bf16)
            dk_out[low:high, g : g + group] = dk.astype(bf16)
            dv_out[low:high, g : g + group] = dv.astype(bf16)


def input_back_kernel(weights, dq, dk, dv, *outs):
    width = weights.shape[1]
    chunk = min(256, width)
    for c in range(0, width, chunk):
        total = 0.0
        for t, part in enumerate((dq, dk, dv)):
            total = total + dot_nt(part[...], weights[t, c : c + chunk, :])
        store_columns(outs, c // chunk, total)


def attend_grad_kernel(n_fs, n_dp, bias_shape, *refs):
    place = own_place()
    grads, refs = refs[:n_fs], refs[n_fs:]
    x, mixed, dq, dk, dv, expand_sums = refs[:6]
    slots = slot_refs(*refs[6:])
    size = grads[0].shape[0] - small_rows
    width = slots[0].shape[1]
    branch = jnp.concatenate([ref[:size, :] for ref in grads], axis=0)
    left = branch.T
    share = left.shape[0] // n_dp
    inputs = x[...]
    for t, value in ((3, mixed), (0, dq), (1, dk), (2, dv)):
        result = dot(left if t == 3 else inputs, value[...]).astype(bf16)
        for s in range(n_dp):
            slots[s][t * share : (t + 1) * share, :] = result[s * share : (s + 1) * share]
    vectors = jnp.zeros((small_rows, x.shape[0]), f32)
    for ref in grads:
        vectors = vectors + ref[size:, :].astype(f32)
    _, heads, part = bias_shape
    padding = jnp.zeros((small_rows - 2, width), f32)
    sums = [column_sum(ref[...].astype(f32)) for ref in (dq, dv)]
    sums = jnp.concatenate(sums + [padding], axis=0).astype(bf16)
    expand = expand_sums[...]
    expand_part = expand.shape[1] // n_dp
    if expand_part == share:
        expand = to_slots(expand, place[0], n_dp)
    column = entries(width)
    order = slot_order(n_dp)
    for s in range(n_dp):
        owner = place[0] ^ order[s]
        inside = (column % head_size) // part == owner
        lane = jnp.where(inside, column // head_size * part + column % part, -1)
        low = dot(sums, one_hot(lane, share))
        if expand_part == share:
            line = expand[:, s * share : (s + 1) * share]
        else:
            spot = entries(expand.shape[1])
            spot = jnp.where(spot // expand_part == owner, spot % expand_part, -1)
            rows = jnp.concatenate([expand, jnp.zeros((7, expand.shape[1]), f32)], axis=0)
            line = dot(rows.astype(bf16), one_hot(spot, share))[0:1]
        if share < width:
            slots[s][4 * share :, share:] = jnp.zeros((small_rows, width - share), bf16)
        slots[s][4 * share :, :share] = jnp.concatenate(
            [vectors[0:6, s * share : (s + 1) * share], line, low[0 : small_rows - 7]], axis=0
        ).astype(bf16)


def joint_kernel(left, right, attend_out, output_out, bias_out, expand_out, vectors_out):
    place = own_place()
    total = left[0].astype(f32) + right[0].astype(f32)
    rows = attend_out.shape[1]
    for t in range(3):
        attend_out[t] = total[t * rows : (t + 1) * rows]
    send(attend_out)
    output_out[...] = total[3 * rows : 4 * rows].T
    small = total[4 * rows :]
    _, heads, part = bias_out.shape
    for t in range(2):
        for h in range(heads):
            bias_out[t, h : h + 1, :] = small[7 + t : 8 + t, h * part : (h + 1) * part]
    expand_out[...] = small[6:7, : expand_out.shape[1]]
    count, lanes = vectors_out.shape
    found = jnp.zeros((count, lanes), f32)
    for i in range(rows // lanes):
        found = found + jnp.where(place[1] == i, small[:count, i * lanes : (i + 1) * lanes], 0.0)
    vectors_out[...] = found


def tokens_grad_kernel(n_fs, n_dp, *refs):
    index = own_place()
    parts, (dh, out) = refs[:n_fs], refs[n_fs:]
    out[...] = from_slots(dh[...] + sum_blocks(parts), index[0], n_dp)


def segment_kernel(n_fs, lengths, owners, allowed, live):
    place = own_place()
    size = live.shape[0]
    slot = lax.broadcasted_iota(jnp.int32, (8, size), 1)
    blocks = [place[0] * n_fs + (place[1] ^ i) for i in range(n_fs)]

    def add(s, carry):
        result = []
        for block, (offset, found) in zip(blocks, carry):
            count = jnp.where(owners[s] == block, lengths[s], 0)
            found = jnp.where((slot >= offset) & (slot < offset + count), s, found)
            result.append((offset + count, found))
        return tuple(result)

    start = tuple((jnp.int32(0), jnp.full((8, size), -1, jnp.int32)) for _ in blocks)
    for i, (_, found) in enumerate(lax.fori_loop(0, lengths.shape[0], add, start)):
        along = jnp.broadcast_to(found[0:1].astype(f32), (size, size))
        down = along.T
        allowed[i] = jnp.where((along == down) & (down >= 0.0), 1.0, 0.0)
        if i == 0:
            live[...] = jnp.where(down[:, 0:1] >= 0.0, 1.0, 0.0)


def prepare_kernel(parity, *refs):
    for source in refs[:4]:
        if isinstance(source, Late):
            source.ready()

    @pl.when(own_place()[0] % 2 == parity)
    def _():
        inner, slope = refs[0], refs[-4]
        chunk = min(256, inner.shape[1])
        for c in range(0, inner.shape[1], chunk):
            value = inner[:, c : c + chunk]
            cdf = 0.5 * (1.0 + lax.erf(value * root_half))
            density = jnp.exp(-0.5 * value * value) * inverse_root_tau
            slope[:, c : c + chunk] = (cdf + value * density).astype(bf16)
        for source, target in zip(refs[1:4], refs[-3:]):
            target[...] = source[...].T


def on_device(
    tokens,
    attend_weight,
    attend_bias,
    output_weight,
    expand_weight,
    expand_bias,
    contract_weight,
    layer_vectors,
    sequence_lengths,
    sequence_owner,
    output_grad,
):
    size, width = tokens.shape
    n_fs = lax.axis_size("fs")
    n_dp = lax.axis_size("dp")
    many = n_fs * size
    share = width // n_dp
    heads_width = attend_weight.shape[2]
    hidden_width = expand_weight.shape[1]
    n_vectors, lanes = layer_vectors.shape
    bias_shape = attend_bias.shape

    def send_back(parts):
        return [parts[0]] + [swap(parts[j], "fs", j) for j in range(1, n_fs)]

    (attend_part,) = kernel_call(
        pack_kernel,
        [shape_of((4 * share + small_rows, heads_width), bf16)],
        attend_weight,
        output_weight,
        attend_bias,
        layer_vectors,
        expand_bias,
        extra=56,
    )
    (own_rows,) = kernel_call(
        functools.partial(slots_kernel, n_dp), hot([shape_of((size, width), bf16)]), tokens
    )
    inputs = gather_fs(own_rows)
    allowed, live = kernel_call(
        functools.partial(segment_kernel, n_fs),
        hot([shape_of((n_fs, size, size), f32), shape_of((size, 1), f32)]),
        sequence_lengths,
        sequence_owner,
    )
    attend_lane = gather_lane(attend_part, *inputs[1:], allowed)
    attend_parts = gather_cores(attend_lane)
    (feed_part,) = kernel_call(
        pair_kernel,
        [shape_of((2 * share, hidden_width), bf16)],
        after(expand_weight, attend_part),
        contract_weight,
    )
    feed_lane = gather_lane(after(feed_part, *attend_lane.values()))
    half_shape = shape_of((many, heads_width), bf16)
    n_scores = n_fs * heads_width // head_size
    (
        queries,
        key_rows,
        values,
        mixed,
        chances,
        expand_row,
        x_all,
        w_all,
        mixing,
        *branch_parts,
    ) = kernel_call(
        functools.partial(attend_kernel, n_fs, n_dp, bias_shape, expand_bias.size),
        [half_shape] * 4
        + [shape_of((n_scores, size, size), f32), Hot(shape_of((1, hidden_width), f32))]
        + [
            shape_of((many, width), bf16),
            shape_of((3, width, heads_width), bf16),
            shape_of((width, heads_width), bf16),
        ]
        + block_shapes(n_fs, size + small_rows, width),
        attend_parts[0],
        *hot(attend_parts[1:]),
        *hot(inputs),
        Hot(allowed),
        extra=4,
    )
    vectors, middle, middle_low, unit_first, inverse_first = kernel_call(
        functools.partial(first_norm_kernel, n_fs),
        hot(
            [
                shape_of((n_vectors, width), f32),
                shape_of((size, width), f32),
                shape_of((size, width), bf16),
                shape_of((size, width), f32),
                shape_of((size, 1), f32),
            ]
        ),
        *hot(send_back(branch_parts)),
        Hot(after(own_rows, *list(feed_lane.values())[1:-1])),
    )
    middles = gather_fs(middle_low)
    last = list(feed_lane)[-1]
    feed_parts = gather_cores({**feed_lane, last: after(feed_lane[last], *middles[1:])})
    wide = shape_of((many, hidden_width), bf16)
    w1, w2, mid_all, hidden, inner, *result_parts = kernel_call(
        functools.partial(feed_kernel, n_fs, n_dp),
        [
            shape_of((width, hidden_width), bf16),
            shape_of((width, hidden_width), bf16),
            shape_of((many, width), bf16),
            wide,
            Hot(shape_of((many, hidden_width), f32)),
        ]
        + block_shapes(n_fs, size, width),
        *hot(middles),
        *hot(feed_parts),
        Hot(expand_row),
        extra=3,
    )
    turned = hot(
        [wide, shape_of((hidden_width, many), bf16)] + [shape_of((width, many), bf16)] * 2
    )
    ready = kernel_call(
        functools.partial(prepare_kernel, 0), turned, Hot(inner), hidden, mid_all, x_all
    )
    result_parts = [after(part, ready[0]) for part in result_parts]
    layer_output, dh2, dffn, sums_second = kernel_call(
        functools.partial(second_norm_kernel, n_fs, n_dp),
        [
            shape_of((size, width), bf16),
            Hot(shape_of((size, width), f32)),
            Hot(shape_of((size, width), bf16)),
            Hot(shape_of((3, width), f32)),
        ],
        *hot(send_back(result_parts)),
        Hot(middle),
        Hot(vectors),
        output_grad,
        Hot(live),
        extra=3,
    )
    dffns = gather_fs(dffn)
    slope, hidden_turned, mid_turned, x_turned = kernel_call(
        functools.partial(prepare_kernel, 1),
        turned,
        Hot(inner),
        hidden,
        mid_all,
        x_all,
        *hot([after(ready[0], dffn), *ready[1:]]),
        aliases={4: 0, 5: 1, 6: 2, 7: 3},
    )
    contract_slots = kernel_call(
        functools.partial(contract_grad_kernel, n_fs),
        hot([shape_of((n_dp // 2, hidden_width, share), bf16)] * 2),
        Hot(hidden_turned),
        *hot(dffns),
        extra=2,
    )
    du, expand_sums, *middle_parts = kernel_call(
        functools.partial(feed_back_kernel, n_fs),
        [wide, Hot(shape_of((1, hidden_width), f32))]
        + block_shapes(n_fs, size, width),
        *hot(dffns),
        w2,
        Hot(after(slope, contract_slots[0])),
        w1,
        extra=3,
    )
    back_parts = send_back(middle_parts)
    def last_sum(shape):
        return lambda keep, taken: kernel_call(
            last_kernel, [shape_of(shape, f32)], keep, taken
        )[0]

    contract_pair = sum_cores(*contract_slots)
    contract_grad, contract_rounds = sum_lanes(*contract_pair, last_sum(contract_weight.shape))
    expand_slots = kernel_call(
        expand_grad_kernel,
        hot([shape_of((n_dp // 2, share, hidden_width), bf16)] * 2),
        after(du, contract_pair[1]),
        Hot(mid_turned),
        extra=2,
    )

    expand_pair = sum_cores(*expand_slots)
    expand_grad, expand_rounds = sum_lanes(*expand_pair, last_sum(expand_weight.shape))
    dh1, dbranch = kernel_call(
        functools.partial(first_back_kernel, n_fs),
        hot([shape_of((size, width), f32), shape_of((size + small_rows, width), bf16)]),
        *hot(back_parts),
        Hot(after(dh2, contract_rounds[-1], expand_slots[0])),
        Hot(unit_first),
        Hot(inverse_first),
        Hot(vectors),
        Hot(sums_second),
    )
    branches = gather_fs(dbranch)
    dq, dk, dv = kernel_call(
        functools.partial(attend_back_kernel, n_fs),
        hot([half_shape] * 3),
        *hot(branches),
        after(mixing, expand_pair[1]),
        queries,
        key_rows,
        values,
        chances,
        extra=2.5,
    )
    attend_slots = kernel_call(
        functools.partial(attend_grad_kernel, n_fs, n_dp, bias_shape),
        hot([shape_of((n_dp // 2, 4 * share + small_rows, heads_width), bf16)] * 2),
        *hot(branches),
        Hot(after(x_turned, expand_rounds[-1], contract_grad)),
        mixed,
        Hot(dq),
        Hot(dk),
        Hot(dv),
        Hot(expand_sums),
        extra=3,
    )
    attend_keep, attend_give = sum_cores(*attend_slots)
    input_parts = kernel_call(
        input_back_kernel,
        block_shapes(n_fs, size, width),
        after(w_all, attend_give),
        Hot(dq),
        Hot(dk),
        Hot(dv),
    )
    (tokens_grad,) = kernel_call(
        functools.partial(tokens_grad_kernel, n_fs, n_dp),
        [shape_of((size, width), f32)],
        *hot(send_back(input_parts)),
        Hot(dh1),
    )
    small_outs = [
        shape_of(attend_bias.shape, f32),
        shape_of(expand_bias.shape, f32),
        shape_of(layer_vectors.shape, f32),
    ]
    sums, _ = sum_lanes(
        after(attend_keep, tokens_grad, expand_grad),
        attend_give,
        lambda keep, taken: kernel_call(
            joint_kernel,
            [shape_of(attend_weight.shape, f32), shape_of(output_weight.shape, f32)]
            + hot(small_outs),
            keep,
            taken,
        ),
    )
    attend_grad, output_weight_grad, attend_bias_grad, expand_bias_grad, vector_grad = sums
    return (
        layer_output,
        tokens_grad,
        attend_grad,
        attend_bias_grad,
        output_weight_grad,
        expand_grad,
        expand_bias_grad,
        contract_grad,
        vector_grad,
    )


def solution(mesh):
    in_specs = (
        P(("dp", "fs"), None),
        P(None, "dp", "fs"),
        P(None, "fs", "dp"),
        P("fs", "dp"),
        P("dp", "fs"),
        P("fs", "dp"),
        P("fs", "dp"),
        P(None, ("dp", "fs")),
        P(),
        P(),
        P(("dp", "fs"), None),
    )
    out_specs = (
        P(("dp", "fs"), None),
        P(("dp", "fs"), None),
        P(None, "dp", "fs"),
        P(None, "fs", "dp"),
        P("fs", "dp"),
        P("dp", "fs"),
        P("fs", "dp"),
        P("fs", "dp"),
        P(None, ("dp", "fs")),
    )
    return jax.shard_map(
        on_device, mesh=mesh, in_specs=in_specs, out_specs=out_specs, check_vma=False
    )
```

```python
import functools

import jax
import jax.numpy as jnp
from jax import lax
from jax.experimental import pallas as pl
from jax.experimental.pallas import tpu as pltpu
from jax.sharding import PartitionSpec as P

masked_score = -1e30
norm_eps = 1e-12
root_half = 0.7071067811865476
inverse_root_tau = 0.3989422804014327
small_rows = 16
head_size = 64
f32 = jnp.float32
bf16 = jnp.bfloat16


def slot_order(count):
    order = [0]
    while len(order) < count:
        step = count // (2 * len(order))
        order = order + [entry | step for entry in order]
    bits = count.bit_length() - 1
    return [int(format(i, "b").zfill(bits)[::-1], 2) for i in range(count)]


def swap(part, axis_name, distance):
    count = lax.axis_size(axis_name)
    return lax.ppermute(part, axis_name, [(i, i ^ distance) for i in range(count)])


def gather_fs(part):
    return [part] + [swap(part, "fs", j) for j in range(1, lax.axis_size("fs"))]


def after(part, *earlier):
    return lax.optimization_barrier((part,) + earlier)[0]


def gather_lane(part, *earlier):
    held = {0: part}
    steps = []
    step = lax.axis_size("dp") // 2
    while step > 1:
        steps.append(step)
        held[step] = swap(part, "dp", step)
        step //= 2
    direct = list(held.values())[1:] + list(earlier)
    for i, step in enumerate(steps):
        for entry in [e for e in held if e % steps[i - 1] == 0 and e and i]:
            if entry | step not in held:
                held[entry | step] = swap(after(held[entry], *direct), "dp", step)
    return held


def gather_cores(held, *earlier):
    both = dict(held)
    for entry, piece in held.items():
        if earlier:
            piece = after(piece, *earlier)
        both[entry | 1] = swap(piece, "dp", 1)
    return [both[entry] for entry in slot_order(len(both))]


def sum_cores(keep, give):
    taken = swap(give, "dp", 1)
    half = Hot(shape_of((keep.shape[0] // 2,) + keep.shape[1:], bf16))
    return kernel_call(add_kernel, [half, half], Hot(keep), Hot(taken))


def sum_lanes(keep, give, done):
    step = 2
    rounds = []
    while True:
        taken = swap(give, "dp", step)
        step *= 2
        if step == lax.axis_size("dp"):
            return done(Hot(keep), Hot(taken)), rounds
        half = Hot(shape_of((keep.shape[0] // 2,) + keep.shape[1:], bf16))
        keep, give = kernel_call(add_kernel, [half, half], Hot(keep), Hot(taken))
        rounds.append(give)


class Late:
    def __init__(self, source, target, semaphore):
        self.target = target
        self.shape = target.shape
        self.dtype = target.dtype
        self.copy = pltpu.make_async_copy(source, target, semaphore)
        self.copy.start()
        self.waits = True

    def ready(self):
        if self.waits:
            self.copy.wait()
            self.waits = False

    def __getitem__(self, where):
        self.ready()
        return self.target[where]


class Leaving:
    def __init__(self, source, target, semaphore):
        self.source = source
        self.shape = source.shape
        self.dtype = source.dtype
        self.copy = pltpu.make_async_copy(source, target, semaphore)
        self.sent = False

    def send(self):
        if not self.sent:
            self.copy.start()
            self.sent = True

    def __getitem__(self, where):
        return self.source[where]

    def __setitem__(self, where, value):
        self.source[where] = value


class Hot:
    def __init__(self, array):
        self.array = array


def hot(arrays):
    return [Hot(array) for array in arrays]


def kernel_call(body, outs, *args, extra=1.5, aliases=None):
    def far(a):
        if isinstance(a, Hot):
            return False
        return a.ndim > 1

    def bare(a):
        return a.array if isinstance(a, Hot) else a

    late = [far(a) for a in args]
    leaving = [far(a) for a in outs]
    args = [bare(a) for a in args]
    outs = [bare(a) for a in outs]
    far_args = [a for a, b in zip(args, late) if b]
    far_outs = [a for a, b in zip(outs, leaving) if b]

    own = sum(a.size * a.dtype.itemsize for a in far_args + far_outs)
    limit = own + int(extra * 2**20) * max(1, lax.axis_size("fs") // 4)

    def whole(*refs):
        given, refs = refs[: len(args)], refs[len(args) :]
        out_refs, refs = refs[: len(outs)], refs[len(outs) :]
        items = []
        number = 0
        for ref, is_far in zip(given, late):
            if is_far:
                ref = Late(ref, refs[number], refs[-1].at[number])
                number += 1
            items.append(ref)
        targets = []
        for ref, is_far in zip(out_refs, leaving):
            if is_far:
                ref = Leaving(refs[number], ref, refs[-1].at[number])
                number += 1
            targets.append(ref)
        body(*items, *targets)
        for target in targets:
            if isinstance(target, Leaving):
                target.send()
        for item in items:
            if isinstance(item, Late):
                item.ready()
        for target in targets:
            if isinstance(target, Leaving):
                target.copy.wait()

    def place(a, is_far):
        if a.ndim == 1:
            return pltpu.SMEM
        return pltpu.HBM if is_far else pltpu.VMEM

    return pl.pallas_call(
        whole,
        out_shape=outs,
        in_specs=[pl.BlockSpec(memory_space=place(a, b)) for a, b in zip(args, late)],
        out_specs=[pl.BlockSpec(memory_space=place(a, b)) for a, b in zip(outs, leaving)],
        scratch_shapes=[pltpu.VMEM(a.shape, a.dtype) for a in far_args + far_outs]
        + [pltpu.SemaphoreType.DMA((max(1, len(far_args + far_outs)),))],
        compiler_params=pltpu.CompilerParams(vmem_limit_bytes=limit),
        cost_estimate=pl.CostEstimate(flops=0, bytes_accessed=0, transcendentals=0),
        input_output_aliases=aliases or {},
    )(*args)


def send(ref):
    if isinstance(ref, Leaving):
        ref.send()


def shape_of(shape, kind):
    return jax.ShapeDtypeStruct(shape, kind)


def dot(left, right):
    return jnp.dot(left, right, preferred_element_type=f32)


def dot_nt(left, right):
    return lax.dot_general(left, right, (((1,), (1,)), ((), ())), preferred_element_type=f32)


def dot_tn(left, right):
    return lax.dot_general(left, right, (((0,), (0,)), ((), ())), preferred_element_type=f32)


def flip_blocks(blocks, index):
    step = 1
    while step < len(blocks):
        chosen = (index // step) % 2 == 1
        blocks = [jnp.where(chosen, blocks[i ^ step], blocks[i]) for i in range(len(blocks))]
        step *= 2
    return blocks


def split_columns(rows, count):
    size = rows.shape[1] // count
    return [rows[:, i * size : (i + 1) * size] for i in range(count)]


def to_slots(rows, index, count):
    blocks = flip_blocks(split_columns(rows, count), index)
    return jnp.concatenate([blocks[entry] for entry in slot_order(count)], axis=1)


def from_slots(rows, index, count):
    slots = split_columns(rows, count)
    order = slot_order(count)
    blocks = [slots[order.index(i)] for i in range(count)]
    return jnp.concatenate(flip_blocks(blocks, index), axis=1)


def row_mean(rows):
    return jnp.mean(rows, axis=1, keepdims=True)


def normalize(rows):
    centred = rows - row_mean(rows)
    inverse = lax.rsqrt(row_mean(centred * centred) + norm_eps)
    return (centred * inverse, inverse)


def normalize_back(upstream, gain, unit, inverse):
    scaled = upstream * gain
    return inverse * (scaled - row_mean(scaled) - unit * row_mean(scaled * unit))


def column_sum(rows):
    return jnp.sum(rows, axis=0, keepdims=True)


def stacked(refs):
    return jnp.concatenate([ref[...] for ref in refs], axis=0)


def beside(refs):
    return jnp.concatenate([ref[...] for ref in refs], axis=1)


def sum_blocks(refs):
    total = refs[0][...]
    for ref in refs[1:]:
        total = total + ref[...].astype(f32)
    return total


def store_blocks(refs, total):
    size = refs[0].shape[0]
    for i, ref in enumerate(refs):
        ref[...] = total[i * size : (i + 1) * size].astype(ref.dtype)


def store_columns(refs, place, total):
    size = refs[0].shape[0]
    width = total.shape[1]
    for i, ref in enumerate(refs):
        part = total[i * size : (i + 1) * size].astype(ref.dtype)
        ref[:, place * width : (place + 1) * width] = part


def add_kernel(left, right, keep, give):
    half = keep.shape[0]
    for out, start in ((give, half), (keep, 0)):
        for i in range(half):
            total = left[start + i].astype(f32) + right[start + i].astype(f32)
            out[i] = total.astype(out.dtype)


def last_kernel(left, right, out):
    out[...] = left[0].astype(f32) + right[0].astype(f32)


def block_shapes(count, rows, width):
    return hot([shape_of((rows, width), f32)] + [shape_of((rows, width), bf16)] * (count - 1))


def one_hot(target, width):
    column = lax.broadcasted_iota(jnp.int32, (target.shape[0], width), 1)
    return jnp.where(column == target, 1.0, 0.0).astype(bf16)


def entries(count):
    return lax.broadcasted_iota(jnp.int32, (count, 1), 0)


def pack_kernel(weight, mixing, bias, vectors, expand_bias, out):
    place = own_place()
    rows, width = weight.shape[1:]
    for t in range(3):
        out[t * rows : (t + 1) * rows, :] = weight[t]
    out[3 * rows : 4 * rows, :] = mixing[...].T
    count, lanes = vectors.shape
    _, heads, part = bias.shape
    pads = small_rows // 2 - 2 * heads
    table = [
        dot(vectors[...], one_hot(entries(lanes) + place[1] * lanes, width)),
        dot(expand_bias[...], one_hot(entries(expand_bias.shape[1]), width)),
        jnp.zeros((small_rows // 2 - count - 1, width), f32),
    ]
    table = table + [dot(bias[t], one_hot(entries(part), width)) for t in range(2)]
    table = table + [jnp.zeros((pads, width), f32)]
    table = [rows for rows in table if rows.shape[0]]
    out[4 * rows :, :] = jnp.concatenate(table, axis=0).astype(bf16)


def slots_kernel(n_dp, tokens, out):
    size = tokens.shape[0]
    out[:size, :] = to_slots(tokens[...].astype(f32), own_place()[0], n_dp).astype(bf16)
    out[size:, :] = jnp.zeros((small_rows, out.shape[1]), bf16)


def pair_kernel(expand, contract, out):
    rows = expand.shape[0]
    out[:rows, :] = expand[...]
    out[rows:, :] = contract[...].T


def group_part(refs, t, count):
    rows = refs[0].shape[0] // count
    return jnp.concatenate([ref[t * rows : (t + 1) * rows, :] for ref in refs], axis=0)


def own_place():
    return (lax.axis_index("dp"), lax.axis_index("fs"))


def head_masks(width):
    lane = lax.broadcasted_iota(jnp.int32, (1, width), 1)
    return [lane // head_size == h for h in range(width // head_size)]


def attend_kernel(n_fs, n_dp, bias_shape, expand_share, *refs):
    place = own_place()
    w_refs, refs = refs[:n_dp], refs[n_dp:]
    x_refs, refs = refs[:n_fs], refs[n_fs:]
    allowed, q_out, k_out, v_out, o_out, p_out, expand_out = refs[:7]
    x_all, w_all, m_all = refs[7:10]
    outs = refs[10:]
    width = w_refs[0].shape[1]
    rows = (w_refs[0].shape[0] - small_rows) // 4
    order = slot_order(n_dp)
    size = x_refs[0].shape[0] - small_rows
    for b, ref in enumerate(x_refs):
        x_all[b * size : (b + 1) * size, :] = ref[:size, :]
    send(x_all)
    x = x_all[...]
    for t, ref in enumerate((w_all, w_all, w_all, m_all)):
        for s in range(n_dp):
            value = w_refs[s][t * rows : (t + 1) * rows, :]
            if t < 3:
                w_all[t, s * rows : (s + 1) * rows, :] = value
            else:
                m_all[s * rows : (s + 1) * rows, :] = value
    send(w_all)
    send(m_all)
    lows = [ref[4 * rows :, :] for ref in w_refs]
    _, heads, share = bias_shape
    taken = min(128, width)
    total = jnp.zeros((small_rows, width), f32)
    column = lax.broadcasted_iota(jnp.int32, (taken, width), 1)
    lane = entries(taken)
    for s in range(n_dp):
        target = jnp.where(lane < share, (place[0] ^ order[s]) * share + lane, -1)
        chosen = jnp.where(column % head_size == target, 1.0, 0.0).astype(bf16)
        total = total + dot(lows[s][:, :taken], chosen)
    row = entries(small_rows) - small_rows // 2
    head = lax.broadcasted_iota(jnp.int32, (small_rows, width), 1) // head_size
    biases = [column_sum(jnp.where(row == t * heads + head, total, 0.0)) for t in range(2)]
    if expand_share == rows:
        line = jnp.concatenate([low[6:7, :rows] for low in lows], axis=1).astype(f32)
        expand_out[...] = from_slots(line, place[0], n_dp)
    else:
        total = jnp.zeros((small_rows, expand_out.shape[1]), f32)
        for s in range(n_dp):
            owner = place[0] ^ order[s]
            target = jnp.where(lane < expand_share, lane + owner * expand_share, -1)
            total = total + dot(lows[s][:, :taken], one_hot(target, expand_out.shape[1]))
        expand_out[...] = total[6:7]
    parts = []
    for t, ref in enumerate((q_out, k_out, v_out)):
        part = dot(x, w_all[t])
        if t != 1:
            part = part + biases[t // 2]
        ref[...] = part.astype(bf16)
        send(ref)
    group = min(128, width)
    masks = head_masks(group)
    zero = jnp.zeros((), bf16)
    number = 0
    for b in range(n_fs):
        low, high = b * size, (b + 1) * size
        seen = allowed[b] > 0.0
        for g in range(0, width, group):
            q, k, v = (part[low:high, g : g + group] for part in (q_out, k_out, v_out))
            mixed = jnp.zeros((size, group), f32)
            for mask in masks:
                scores = dot_nt(jnp.where(mask, k, zero), q) * head_size**-0.5
                scores = jnp.where(seen, scores, masked_score)
                weights = jnp.exp(scores - jnp.max(scores, axis=0, keepdims=True))
                chances = weights * (1.0 / column_sum(weights))
                p_out[number] = chances
                number += 1
                mixed = mixed + dot_tn(chances.astype(bf16), jnp.where(mask, v, zero))
            o_out[low:high, g : g + group] = mixed.astype(bf16)
    send(p_out)
    send(o_out)
    total = dot_nt(o_out[...], m_all[...])
    small = jnp.concatenate([low[:, :rows] for low in lows], axis=1)
    for i, out in enumerate(outs):
        out[:size, :] = total[i * size : (i + 1) * size].astype(out.dtype)
        out[size:, :] = small.astype(out.dtype)


def first_norm_kernel(n_fs, *refs):
    parts, (x, vectors, mid, mid_low, unit_out, inverse_out) = refs[:n_fs], refs[n_fs:]
    total = sum_blocks(parts)
    size = x.shape[0] - small_rows
    small = total[size : size + vectors.shape[0]]
    vectors[...] = small
    rows = x[:size, :].astype(f32) + (total[:size] + small[0:1, :])
    unit, inverse = normalize(rows)
    middle = unit * small[1:2, :] + small[2:3, :]
    mid[...] = middle
    mid_low[...] = middle.astype(bf16)
    unit_out[...] = unit
    inverse_out[...] = inverse


def feed_kernel(n_fs, n_dp, *refs):
    mids, refs = refs[:n_fs], refs[n_fs:]
    weights, refs = refs[:n_dp], refs[n_dp:]
    bias, w1, w2, mid_all, hid_out, inner_out, outs = *refs[:6], refs[6:]
    size = mids[0].shape[0]
    for b, ref in enumerate(mids):
        mid_all[b * size : (b + 1) * size, :] = ref[...]
    rows = weights[0].shape[0] // 2
    for s, ref in enumerate(weights):
        w1[s * rows : (s + 1) * rows, :] = ref[:rows, :]
        w2[s * rows : (s + 1) * rows, :] = ref[rows:, :]
    send(mid_all)
    send(w1)
    send(w2)
    chunk = min(256, hid_out.shape[1])
    for c in range(0, hid_out.shape[1], chunk):
        value = dot(mid_all[...], w1[:, c : c + chunk]) + bias[:, c : c + chunk]
        inner_out[:, c : c + chunk] = value
        cdf = 0.5 * (1.0 + lax.erf(value * root_half))
        hid_out[:, c : c + chunk] = (value * cdf).astype(bf16)
    send(hid_out)
    chunk = min(256, w2.shape[0])
    for c in range(0, w2.shape[0], chunk):
        store_columns(outs, c // chunk, dot_nt(hid_out[...], w2[c : c + chunk, :]))


def second_norm_kernel(n_fs, n_dp, *refs):
    index = own_place()
    parts, refs = refs[:n_fs], refs[n_fs:]
    mid, vectors, grad, live, layer_out, dh, dh_low, sums = refs
    rows = mid[...] + (sum_blocks(parts) + vectors[3:4, :])
    unit, inverse = normalize(rows)
    alive = live[...]
    final = (unit * vectors[4:5, :] + vectors[5:6, :]) * alive
    layer_out[...] = from_slots(final, index[0], n_dp).astype(bf16)
    upstream = to_slots(grad[...].astype(f32), index[0], n_dp) * alive
    down = normalize_back(upstream, vectors[4:5, :], unit, inverse)
    low = down.astype(bf16)
    dh[...] = down
    dh_low[...] = low
    sums[0:1, :] = column_sum(low.astype(f32))
    sums[1:2, :] = column_sum(upstream * unit)
    sums[2:3, :] = column_sum(upstream)


def feed_back_kernel(n_fs, *refs):
    grads, refs = refs[:n_fs], refs[n_fs:]
    w2, slope, w1, du_out, bias_out, outs = *refs[:5], refs[5:]
    rows = stacked(grads)
    chunk = min(256, du_out.shape[1])
    for c in range(0, du_out.shape[1], chunk):
        du = dot(rows, w2[:, c : c + chunk]) * slope[:, c : c + chunk].astype(f32)
        du = du.astype(bf16)
        du_out[:, c : c + chunk] = du
        bias_out[:, c : c + chunk] = column_sum(du.astype(f32))
    send(du_out)
    chunk = min(256, w1.shape[0])
    for c in range(0, w1.shape[0], chunk):
        store_columns(outs, c // chunk, dot_nt(du_out[...], w1[c : c + chunk, :]))


def slot_refs(keep, give):
    half = keep.shape[0]
    return [keep.at[s] for s in range(half)] + [give.at[s] for s in range(half)]


def contract_grad_kernel(n_fs, turned, *refs):
    grads, slots = stacked(refs[:n_fs]), slot_refs(*refs[n_fs:])
    left = turned[...]
    size = slots[0].shape[1]
    for s in reversed(range(0, len(slots), 2)):
        pair = dot(left, grads[:, s * size : (s + 2) * size])
        slots[s][...] = pair[:, :size].astype(bf16)
        slots[s + 1][...] = pair[:, size:].astype(bf16)


def expand_grad_kernel(du, turned, keep, give):
    left = turned[...]
    size = keep.shape[1]
    for s, slot in reversed(list(enumerate(slot_refs(keep, give)))):
        slot[...] = dot(left[s * size : (s + 1) * size], du[...]).astype(bf16)


def first_back_kernel(n_fs, *refs):
    parts, refs = refs[:n_fs], refs[n_fs:]
    dh2, unit, inverse, vectors, second, dh, out = refs
    upstream = dh2[...] + sum_blocks(parts)
    units = unit[...]
    down = normalize_back(upstream, vectors[1:2, :], units, inverse[...])
    low = down.astype(bf16)
    size = dh2.shape[0]
    dh[...] = down
    out[:size, :] = low
    out[size:, :] = jnp.concatenate(
        [
            column_sum(low.astype(f32)),
            column_sum(upstream * units),
            column_sum(upstream),
            second[...],
            jnp.zeros((small_rows - 3 - second.shape[0], upstream.shape[1]), f32),
        ],
        axis=0,
    ).astype(bf16)


def attend_back_kernel(n_fs, *refs):
    grads, refs = refs[:n_fs], refs[n_fs:]
    mixing, q_in, k_in, v_in, p_in, dq_out, dk_out, dv_out = refs
    width = q_in.shape[1]
    size = grads[0].shape[0] - small_rows
    group = min(128, width)
    masks = head_masks(group)
    zero = jnp.zeros((), bf16)
    rows = jnp.concatenate([ref[:size, :] for ref in grads], axis=0)
    grad_mixed = dot(rows, mixing[...]).astype(bf16)
    number = 0
    for b in range(n_fs):
        low, high = b * size, (b + 1) * size
        for g in range(0, width, group):
            q, k, v = (part[low:high, g : g + group] for part in (q_in, k_in, v_in))
            do = grad_mixed[low:high, g : g + group]
            dq = jnp.zeros((size, group), f32)
            dk = jnp.zeros((size, group), f32)
            dv = jnp.zeros((size, group), f32)
            for mask in masks:
                chances = p_in[number]
                number += 1
                masked_do = jnp.where(mask, do, zero)
                dp = dot_nt(v, masked_do)
                ds = chances * (dp - column_sum(dp * chances))
                ds = (ds * head_size**-0.5).astype(bf16)
                dv = dv + dot(chances.astype(bf16), masked_do)
                dq = dq + dot_tn(ds, jnp.where(mask, k, zero))
                dk = dk + dot(ds, jnp.where(mask, q, zero))
            dq_out[low:high, g : g + group] = dq.astype(bf16)
            dk_out[low:high, g : g + group] = dk.astype(bf16)
            dv_out[low:high, g : g + group] = dv.astype(bf16)


def input_back_kernel(weights, dq, dk, dv, *outs):
    width = weights.shape[1]
    chunk = min(256, width)
    for c in range(0, width, chunk):
        total = 0.0
        for t, part in enumerate((dq, dk, dv)):
            total = total + dot_nt(part[...], weights[t, c : c + chunk, :])
        store_columns(outs, c // chunk, total)


def attend_grad_kernel(n_fs, n_dp, bias_shape, *refs):
    place = own_place()
    grads, refs = refs[:n_fs], refs[n_fs:]
    x, mixed, dq, dk, dv, expand_sums = refs[:6]
    slots = slot_refs(*refs[6:])
    size = grads[0].shape[0] - small_rows
    width = slots[0].shape[1]
    branch = jnp.concatenate([ref[:size, :] for ref in grads], axis=0)
    left = branch.T
    share = left.shape[0] // n_dp
    inputs = x[...]
    for t, value in ((3, mixed), (0, dq), (1, dk), (2, dv)):
        result = dot(left if t == 3 else inputs, value[...]).astype(bf16)
        for s in range(n_dp):
            slots[s][t * share : (t + 1) * share, :] = result[s * share : (s + 1) * share]
    vectors = jnp.zeros((small_rows, x.shape[0]), f32)
    for ref in grads:
        vectors = vectors + ref[size:, :].astype(f32)
    _, heads, part = bias_shape
    padding = jnp.zeros((small_rows - 2, width), f32)
    sums = [column_sum(ref[...].astype(f32)) for ref in (dq, dv)]
    sums = jnp.concatenate(sums + [padding], axis=0).astype(bf16)
    expand = expand_sums[...]
    expand_part = expand.shape[1] // n_dp
    if expand_part == share:
        expand = to_slots(expand, place[0], n_dp)
    column = entries(width)
    order = slot_order(n_dp)
    for s in range(n_dp):
        owner = place[0] ^ order[s]
        inside = (column % head_size) // part == owner
        lane = jnp.where(inside, column // head_size * part + column % part, -1)
        low = dot(sums, one_hot(lane, share))
        if expand_part == share:
            line = expand[:, s * share : (s + 1) * share]
        else:
            spot = entries(expand.shape[1])
            spot = jnp.where(spot // expand_part == owner, spot % expand_part, -1)
            rows = jnp.concatenate([expand, jnp.zeros((7, expand.shape[1]), f32)], axis=0)
            line = dot(rows.astype(bf16), one_hot(spot, share))[0:1]
        if share < width:
            slots[s][4 * share :, share:] = jnp.zeros((small_rows, width - share), bf16)
        slots[s][4 * share :, :share] = jnp.concatenate(
            [vectors[0:6, s * share : (s + 1) * share], line, low[0 : small_rows - 7]], axis=0
        ).astype(bf16)


def joint_kernel(left, right, attend_out, output_out, bias_out, expand_out, vectors_out):
    place = own_place()
    total = left[0].astype(f32) + right[0].astype(f32)
    rows = attend_out.shape[1]
    for t in range(3):
        attend_out[t] = total[t * rows : (t + 1) * rows]
    send(attend_out)
    output_out[...] = total[3 * rows : 4 * rows].T
    small = total[4 * rows :]
    _, heads, part = bias_out.shape
    for t in range(2):
        for h in range(heads):
            bias_out[t, h : h + 1, :] = small[7 + t : 8 + t, h * part : (h + 1) * part]
    expand_out[...] = small[6:7, : expand_out.shape[1]]
    count, lanes = vectors_out.shape
    found = jnp.zeros((count, lanes), f32)
    for i in range(rows // lanes):
        found = found + jnp.where(place[1] == i, small[:count, i * lanes : (i + 1) * lanes], 0.0)
    vectors_out[...] = found


def tokens_grad_kernel(n_fs, n_dp, *refs):
    index = own_place()
    parts, (dh, out) = refs[:n_fs], refs[n_fs:]
    out[...] = from_slots(dh[...] + sum_blocks(parts), index[0], n_dp)


def segment_kernel(n_fs, lengths, owners, allowed, live):
    place = own_place()
    size = live.shape[0]
    slot = lax.broadcasted_iota(jnp.int32, (8, size), 1)
    blocks = [place[0] * n_fs + (place[1] ^ i) for i in range(n_fs)]

    def add(s, carry):
        result = []
        for block, (offset, found) in zip(blocks, carry):
            count = jnp.where(owners[s] == block, lengths[s], 0)
            found = jnp.where((slot >= offset) & (slot < offset + count), s, found)
            result.append((offset + count, found))
        return tuple(result)

    start = tuple((jnp.int32(0), jnp.full((8, size), -1, jnp.int32)) for _ in blocks)
    for i, (_, found) in enumerate(lax.fori_loop(0, lengths.shape[0], add, start)):
        along = jnp.broadcast_to(found[0:1].astype(f32), (size, size))
        down = along.T
        allowed[i] = jnp.where((along == down) & (down >= 0.0), 1.0, 0.0)
        if i == 0:
            live[...] = jnp.where(down[:, 0:1] >= 0.0, 1.0, 0.0)


def prepare_kernel(parity, *refs):
    for source in refs[:4]:
        if isinstance(source, Late):
            source.ready()

    @pl.when(own_place()[0] % 2 == parity)
    def _():
        inner, slope = refs[0], refs[-4]
        chunk = min(256, inner.shape[1])
        for c in range(0, inner.shape[1], chunk):
            value = inner[:, c : c + chunk]
            cdf = 0.5 * (1.0 + lax.erf(value * root_half))
            density = jnp.exp(-0.5 * value * value) * inverse_root_tau
            slope[:, c : c + chunk] = (cdf + value * density).astype(bf16)
        for source, target in zip(refs[1:4], refs[-3:]):
            target[...] = source[...].T


def on_device(
    tokens,
    attend_weight,
    attend_bias,
    output_weight,
    expand_weight,
    expand_bias,
    contract_weight,
    layer_vectors,
    sequence_lengths,
    sequence_owner,
    output_grad,
):
    size, width = tokens.shape
    n_fs = lax.axis_size("fs")
    n_dp = lax.axis_size("dp")
    many = n_fs * size
    share = width // n_dp
    heads_width = attend_weight.shape[2]
    hidden_width = expand_weight.shape[1]
    n_vectors, lanes = layer_vectors.shape
    bias_shape = attend_bias.shape

    def send_back(parts):
        return [parts[0]] + [swap(parts[j], "fs", j) for j in range(1, n_fs)]

    (attend_part,) = kernel_call(
        pack_kernel,
        hot([shape_of((4 * share + small_rows, heads_width), bf16)]),
        attend_weight,
        output_weight,
        attend_bias,
        layer_vectors,
        expand_bias,
        extra=56,
    )
    (own_rows,) = kernel_call(
        functools.partial(slots_kernel, n_dp), hot([shape_of((size + small_rows, width), bf16)]), tokens, extra=52
    )
    inputs = gather_fs(own_rows)
    allowed, live = kernel_call(
        functools.partial(segment_kernel, n_fs),
        hot([shape_of((n_fs, size, size), f32), shape_of((size, 1), f32)]),
        sequence_lengths,
        sequence_owner,
    )
    attend_lane = gather_lane(attend_part)
    attend_parts = gather_cores(attend_lane)
    (feed_part,) = kernel_call(
        pair_kernel,
        [shape_of((2 * share, hidden_width), bf16)],
        after(expand_weight, allowed, *inputs[1:]),
        contract_weight,
    )
    feed_lane = gather_lane(after(feed_part, *attend_lane.values()))
    half_shape = shape_of((many, heads_width), bf16)
    n_scores = n_fs * heads_width // head_size
    (
        queries,
        key_rows,
        values,
        mixed,
        chances,
        expand_row,
        x_all,
        w_all,
        mixing,
        *branch_parts,
    ) = kernel_call(
        functools.partial(attend_kernel, n_fs, n_dp, bias_shape, expand_bias.size),
        [half_shape] * 4
        + [shape_of((n_scores, size, size), f32), Hot(shape_of((1, hidden_width), f32))]
        + [
            shape_of((many, width), bf16),
            shape_of((3, width, heads_width), bf16),
            shape_of((width, heads_width), bf16),
        ]
        + block_shapes(n_fs, size + small_rows, width),
        *hot(attend_parts),
        *hot(inputs),
        Hot(allowed),
        extra=4,
    )
    vectors, middle, middle_low, unit_first, inverse_first = kernel_call(
        functools.partial(first_norm_kernel, n_fs),
        hot(
            [
                shape_of((n_vectors, width), f32),
                shape_of((size, width), f32),
                shape_of((size, width), bf16),
                shape_of((size, width), f32),
                shape_of((size, 1), f32),
            ]
        ),
        *hot(send_back(branch_parts)),
        Hot(after(own_rows, *list(feed_lane.values())[1:-1])),
    )
    middles = gather_fs(middle_low)
    last = list(feed_lane)[-1]
    feed_parts = gather_cores({**feed_lane, last: after(feed_lane[last], *middles[1:])})
    wide = shape_of((many, hidden_width), bf16)
    w1, w2, mid_all, hidden, inner, *result_parts = kernel_call(
        functools.partial(feed_kernel, n_fs, n_dp),
        [
            shape_of((width, hidden_width), bf16),
            shape_of((width, hidden_width), bf16),
            shape_of((many, width), bf16),
            wide,
            Hot(shape_of((many, hidden_width), f32)),
        ]
        + block_shapes(n_fs, size, width),
        *hot(middles),
        *hot(feed_parts),
        Hot(expand_row),
        extra=3,
    )
    turned = hot(
        [wide, shape_of((hidden_width, many), bf16)] + [shape_of((width, many), bf16)] * 2
    )
    ready = kernel_call(
        functools.partial(prepare_kernel, 0), turned, Hot(inner), hidden, mid_all, x_all
    )
    result_parts = [after(part, ready[0]) for part in result_parts]
    layer_output, dh2, dffn, sums_second = kernel_call(
        functools.partial(second_norm_kernel, n_fs, n_dp),
        [
            shape_of((size, width), bf16),
            Hot(shape_of((size, width), f32)),
            Hot(shape_of((size, width), bf16)),
            Hot(shape_of((3, width), f32)),
        ],
        *hot(send_back(result_parts)),
        Hot(middle),
        Hot(vectors),
        output_grad,
        Hot(live),
        extra=3,
    )
    dffns = gather_fs(dffn)
    slope, hidden_turned, mid_turned, x_turned = kernel_call(
        functools.partial(prepare_kernel, 1),
        turned,
        Hot(inner),
        hidden,
        mid_all,
        x_all,
        *hot([after(ready[0], dffn), *ready[1:]]),
        aliases={4: 0, 5: 1, 6: 2, 7: 3},
    )
    contract_slots = kernel_call(
        functools.partial(contract_grad_kernel, n_fs),
        hot([shape_of((n_dp // 2, hidden_width, share), bf16)] * 2),
        Hot(hidden_turned),
        *hot(dffns),
        extra=2,
    )
    du, expand_sums, *middle_parts = kernel_call(
        functools.partial(feed_back_kernel, n_fs),
        [wide, Hot(shape_of((1, hidden_width), f32))]
        + block_shapes(n_fs, size, width),
        *hot(dffns),
        w2,
        Hot(after(slope, contract_slots[0])),
        w1,
        extra=3,
    )
    back_parts = send_back(middle_parts)
    def last_sum(shape):
        return lambda keep, taken: kernel_call(
            last_kernel, [shape_of(shape, f32)], keep, taken
        )[0]

    contract_pair = sum_cores(*contract_slots)
    contract_grad, contract_rounds = sum_lanes(*contract_pair, last_sum(contract_weight.shape))
    expand_slots = kernel_call(
        expand_grad_kernel,
        hot([shape_of((n_dp // 2, share, hidden_width), bf16)] * 2),
        after(du, contract_pair[1]),
        Hot(mid_turned),
        extra=2,
    )

    expand_pair = sum_cores(*expand_slots)
    expand_grad, expand_rounds = sum_lanes(*expand_pair, last_sum(expand_weight.shape))
    dh1, dbranch = kernel_call(
        functools.partial(first_back_kernel, n_fs),
        hot([shape_of((size, width), f32), shape_of((size + small_rows, width), bf16)]),
        *hot(back_parts),
        Hot(after(dh2, contract_rounds[-1], expand_slots[0])),
        Hot(unit_first),
        Hot(inverse_first),
        Hot(vectors),
        Hot(sums_second),
    )
    branches = gather_fs(dbranch)
    dq, dk, dv = kernel_call(
        functools.partial(attend_back_kernel, n_fs),
        hot([half_shape] * 3),
        *hot(branches),
        after(mixing, expand_pair[1]),
        queries,
        key_rows,
        values,
        chances,
        extra=2.5,
    )
    attend_slots = kernel_call(
        functools.partial(attend_grad_kernel, n_fs, n_dp, bias_shape),
        hot([shape_of((n_dp // 2, 4 * share + small_rows, heads_width), bf16)] * 2),
        *hot(branches),
        Hot(after(x_turned, expand_rounds[-1], contract_grad)),
        mixed,
        Hot(dq),
        Hot(dk),
        Hot(dv),
        Hot(expand_sums),
        extra=3,
    )
    attend_keep, attend_give = sum_cores(*attend_slots)
    input_parts = kernel_call(
        input_back_kernel,
        block_shapes(n_fs, size, width),
        after(w_all, attend_give),
        Hot(dq),
        Hot(dk),
        Hot(dv),
    )
    (tokens_grad,) = kernel_call(
        functools.partial(tokens_grad_kernel, n_fs, n_dp),
        [shape_of((size, width), f32)],
        *hot(send_back(input_parts)),
        Hot(dh1),
    )
    small_outs = [
        shape_of(attend_bias.shape, f32),
        shape_of(expand_bias.shape, f32),
        shape_of(layer_vectors.shape, f32),
    ]
    sums, _ = sum_lanes(
        after(attend_keep, tokens_grad, expand_grad),
        attend_give,
        lambda keep, taken: kernel_call(
            joint_kernel,
            [shape_of(attend_weight.shape, f32), shape_of(output_weight.shape, f32)]
            + hot(small_outs),
            keep,
            taken,
        ),
    )
    attend_grad, output_weight_grad, attend_bias_grad, expand_bias_grad, vector_grad = sums
    return (
        layer_output,
        tokens_grad,
        attend_grad,
        attend_bias_grad,
        output_weight_grad,
        expand_grad,
        expand_bias_grad,
        contract_grad,
        vector_grad,
    )


def solution(mesh):
    in_specs = (
        P(("dp", "fs"), None),
        P(None, "dp", "fs"),
        P(None, "fs", "dp"),
        P("fs", "dp"),
        P("dp", "fs"),
        P("fs", "dp"),
        P("fs", "dp"),
        P(None, ("dp", "fs")),
        P(),
        P(),
        P(("dp", "fs"), None),
    )
    out_specs = (
        P(("dp", "fs"), None),
        P(("dp", "fs"), None),
        P(None, "dp", "fs"),
        P(None, "fs", "dp"),
        P("fs", "dp"),
        P("dp", "fs"),
        P("fs", "dp"),
        P("fs", "dp"),
        P(None, ("dp", "fs")),
    )
    return jax.shard_map(
        on_device, mesh=mesh, in_specs=in_specs, out_specs=out_specs, check_vma=False
    )
```

```python
import functools

import jax
import jax.numpy as jnp
from jax import lax
from jax.experimental import pallas as pl
from jax.experimental.pallas import tpu as pltpu
from jax.sharding import PartitionSpec as P

masked_score = -1e30
norm_eps = 1e-12
root_half = 0.7071067811865476
inverse_root_tau = 0.3989422804014327
small_rows = 16
head_size = 64
f32 = jnp.float32
bf16 = jnp.bfloat16


def slot_order(count):
    order = [0]
    while len(order) < count:
        step = count // (2 * len(order))
        order = order + [entry | step for entry in order]
    bits = count.bit_length() - 1
    return [int(format(i, "b").zfill(bits)[::-1], 2) for i in range(count)]


def swap(part, axis_name, distance):
    count = lax.axis_size(axis_name)
    return lax.ppermute(part, axis_name, [(i, i ^ distance) for i in range(count)])


def gather_fs(part):
    return [part] + [swap(part, "fs", j) for j in range(1, lax.axis_size("fs"))]


def after(part, *earlier):
    return lax.optimization_barrier((part,) + earlier)[0]


def gather_lane(part, *earlier):
    held = {0: part}
    steps = []
    step = lax.axis_size("dp") // 2
    while step > 1:
        steps.append(step)
        held[step] = swap(part, "dp", step)
        step //= 2
    direct = list(held.values())[1:] + list(earlier)
    for i, step in enumerate(steps):
        for entry in [e for e in held if e % steps[i - 1] == 0 and e and i]:
            if entry | step not in held:
                held[entry | step] = swap(after(held[entry], *direct), "dp", step)
    return held


def gather_cores(held, *earlier):
    both = dict(held)
    for entry, piece in held.items():
        if earlier:
            piece = after(piece, *earlier)
        both[entry | 1] = swap(piece, "dp", 1)
    return [both[entry] for entry in slot_order(len(both))]


def sum_cores(keep, give):
    taken = swap(give, "dp", 1)
    half = Hot(shape_of((keep.shape[0] // 2,) + keep.shape[1:], bf16))
    return kernel_call(add_kernel, [half, half], Hot(keep), Hot(taken))


def sum_lanes(keep, give, done):
    step = 2
    rounds = []
    while True:
        taken = swap(give, "dp", step)
        step *= 2
        if step == lax.axis_size("dp"):
            return done(Hot(keep), Hot(taken)), rounds
        half = Hot(shape_of((keep.shape[0] // 2,) + keep.shape[1:], bf16))
        keep, give = kernel_call(add_kernel, [half, half], Hot(keep), Hot(taken))
        rounds.append(give)


class Late:
    def __init__(self, source, target, semaphore):
        self.target = target
        self.shape = target.shape
        self.dtype = target.dtype
        self.copy = pltpu.make_async_copy(source, target, semaphore)
        self.copy.start()
        self.waits = True

    def ready(self):
        if self.waits:
            self.copy.wait()
            self.waits = False

    def __getitem__(self, where):
        self.ready()
        return self.target[where]


class Leaving:
    def __init__(self, source, target, semaphore):
        self.source = source
        self.shape = source.shape
        self.dtype = source.dtype
        self.copy = pltpu.make_async_copy(source, target, semaphore)
        self.sent = False

    def send(self):
        if not self.sent:
            self.copy.start()
            self.sent = True

    def __getitem__(self, where):
        return self.source[where]

    def __setitem__(self, where, value):
        self.source[where] = value


class Far:
    def __init__(self, array):
        self.array = array


class Hot:
    def __init__(self, array):
        self.array = array


def hot(arrays):
    return [Hot(array) for array in arrays]


def kernel_call(body, outs, *args, extra=1.5, aliases=None):
    def far(a):
        return isinstance(a, Far)

    def bare(a):
        return a.array if isinstance(a, (Far, Hot)) else a

    late = [far(a) for a in args]
    leaving = [far(a) for a in outs]
    args = [bare(a) for a in args]
    outs = [bare(a) for a in outs]
    far_args = [a for a, b in zip(args, late) if b]
    far_outs = [a for a, b in zip(outs, leaving) if b]

    own = sum(a.size * a.dtype.itemsize for a in far_args + far_outs)
    limit = own + int(extra * 2**20) * max(1, lax.axis_size("fs") // 4)

    def whole(*refs):
        given, refs = refs[: len(args)], refs[len(args) :]
        out_refs, refs = refs[: len(outs)], refs[len(outs) :]
        items = []
        number = 0
        for ref, is_far in zip(given, late):
            if is_far:
                ref = Late(ref, refs[number], refs[-1].at[number])
                number += 1
            items.append(ref)
        targets = []
        for ref, is_far in zip(out_refs, leaving):
            if is_far:
                ref = Leaving(refs[number], ref, refs[-1].at[number])
                number += 1
            targets.append(ref)
        body(*items, *targets)
        for target in targets:
            if isinstance(target, Leaving):
                target.send()
        for item in items:
            if isinstance(item, Late):
                item.ready()
        for target in targets:
            if isinstance(target, Leaving):
                target.copy.wait()

    def place(a, is_far):
        if a.ndim == 1:
            return pltpu.SMEM
        return pltpu.HBM if is_far else pltpu.VMEM

    return pl.pallas_call(
        whole,
        out_shape=outs,
        in_specs=[pl.BlockSpec(memory_space=place(a, b)) for a, b in zip(args, late)],
        out_specs=[pl.BlockSpec(memory_space=place(a, b)) for a, b in zip(outs, leaving)],
        scratch_shapes=[pltpu.VMEM(a.shape, a.dtype) for a in far_args + far_outs]
        + [pltpu.SemaphoreType.DMA((max(1, len(far_args + far_outs)),))],
        compiler_params=pltpu.CompilerParams(vmem_limit_bytes=limit),
        cost_estimate=pl.CostEstimate(flops=0, bytes_accessed=0, transcendentals=0),
        input_output_aliases=aliases or {},
    )(*args)


def send(ref):
    if isinstance(ref, Leaving):
        ref.send()


def shape_of(shape, kind):
    return jax.ShapeDtypeStruct(shape, kind)


def dot(left, right):
    return jnp.dot(left, right, preferred_element_type=f32)


def dot_nt(left, right):
    return lax.dot_general(left, right, (((1,), (1,)), ((), ())), preferred_element_type=f32)


def dot_tn(left, right):
    return lax.dot_general(left, right, (((0,), (0,)), ((), ())), preferred_element_type=f32)


def flip_blocks(blocks, index):
    step = 1
    while step < len(blocks):
        chosen = (index // step) % 2 == 1
        blocks = [jnp.where(chosen, blocks[i ^ step], blocks[i]) for i in range(len(blocks))]
        step *= 2
    return blocks


def split_columns(rows, count):
    size = rows.shape[1] // count
    return [rows[:, i * size : (i + 1) * size] for i in range(count)]


def to_slots(rows, index, count):
    blocks = flip_blocks(split_columns(rows, count), index)
    return jnp.concatenate([blocks[entry] for entry in slot_order(count)], axis=1)


def from_slots(rows, index, count):
    slots = split_columns(rows, count)
    order = slot_order(count)
    blocks = [slots[order.index(i)] for i in range(count)]
    return jnp.concatenate(flip_blocks(blocks, index), axis=1)


def row_mean(rows):
    return jnp.mean(rows, axis=1, keepdims=True)


def normalize(rows):
    centred = rows - row_mean(rows)
    inverse = lax.rsqrt(row_mean(centred * centred) + norm_eps)
    return (centred * inverse, inverse)


def normalize_back(upstream, gain, unit, inverse):
    scaled = upstream * gain
    return inverse * (scaled - row_mean(scaled) - unit * row_mean(scaled * unit))


def column_sum(rows):
    return jnp.sum(rows, axis=0, keepdims=True)


def stacked(refs):
    return jnp.concatenate([ref[...] for ref in refs], axis=0)


def beside(refs):
    return jnp.concatenate([ref[...] for ref in refs], axis=1)


def sum_blocks(refs):
    total = refs[0][...]
    for ref in refs[1:]:
        total = total + ref[...].astype(f32)
    return total


def store_blocks(refs, total):
    size = refs[0].shape[0]
    for i, ref in enumerate(refs):
        ref[...] = total[i * size : (i + 1) * size].astype(ref.dtype)


def store_columns(refs, place, total):
    size = refs[0].shape[0]
    width = total.shape[1]
    for i, ref in enumerate(refs):
        part = total[i * size : (i + 1) * size].astype(ref.dtype)
        ref[:, place * width : (place + 1) * width] = part


def add_kernel(left, right, keep, give):
    half = keep.shape[0]
    for out, start in ((give, half), (keep, 0)):
        for i in range(half):
            total = left[start + i].astype(f32) + right[start + i].astype(f32)
            out[i] = total.astype(out.dtype)


def last_kernel(left, right, out):
    out[...] = left[0].astype(f32) + right[0].astype(f32)


def block_shapes(count, rows, width):
    return hot([shape_of((rows, width), f32)] + [shape_of((rows, width), bf16)] * (count - 1))


def one_hot(target, width):
    column = lax.broadcasted_iota(jnp.int32, (target.shape[0], width), 1)
    return jnp.where(column == target, 1.0, 0.0).astype(bf16)


def entries(count):
    return lax.broadcasted_iota(jnp.int32, (count, 1), 0)


def pack_kernel(weight, mixing, bias, vectors, expand_bias, out):
    place = own_place()
    rows, width = weight.shape[1:]
    for t in range(3):
        out[t * rows : (t + 1) * rows, :] = weight[t]
    out[3 * rows : 4 * rows, :] = mixing[...].T
    count, lanes = vectors.shape
    _, heads, part = bias.shape
    pads = small_rows // 2 - 2 * heads
    table = [
        dot(vectors[...], one_hot(entries(lanes) + place[1] * lanes, width)),
        dot(expand_bias[...], one_hot(entries(expand_bias.shape[1]), width)),
        jnp.zeros((small_rows // 2 - count - 1, width), f32),
    ]
    table = table + [dot(bias[t], one_hot(entries(part), width)) for t in range(2)]
    table = table + [jnp.zeros((pads, width), f32)]
    table = [rows for rows in table if rows.shape[0]]
    out[4 * rows :, :] = jnp.concatenate(table, axis=0).astype(bf16)


def slots_kernel(n_dp, tokens, out):
    size = tokens.shape[0]
    out[:size, :] = to_slots(tokens[...].astype(f32), own_place()[0], n_dp).astype(bf16)
    out[size:, :] = jnp.zeros((small_rows, out.shape[1]), bf16)


def pair_kernel(expand, contract, out):
    rows = expand.shape[0]
    out[:rows, :] = expand[...]
    out[rows:, :] = contract[...].T


def group_part(refs, t, count):
    rows = refs[0].shape[0] // count
    return jnp.concatenate([ref[t * rows : (t + 1) * rows, :] for ref in refs], axis=0)


def own_place():
    return (lax.axis_index("dp"), lax.axis_index("fs"))


def head_masks(width):
    lane = lax.broadcasted_iota(jnp.int32, (1, width), 1)
    return [lane // head_size == h for h in range(width // head_size)]


def attend_kernel(n_fs, n_dp, bias_shape, expand_share, *refs):
    place = own_place()
    w_refs, refs = refs[:n_dp], refs[n_dp:]
    x_refs, refs = refs[:n_fs], refs[n_fs:]
    allowed, q_out, k_out, v_out, o_out, p_out, expand_out = refs[:7]
    x_all, w_all, m_all = refs[7:10]
    outs = refs[10:]
    width = w_refs[0].shape[1]
    rows = (w_refs[0].shape[0] - small_rows) // 4
    order = slot_order(n_dp)
    size = x_refs[0].shape[0] - small_rows
    for b, ref in enumerate(x_refs):
        x_all[b * size : (b + 1) * size, :] = ref[:size, :]
    send(x_all)
    x = x_all[...]
    for t, ref in enumerate((w_all, w_all, w_all, m_all)):
        for s in range(n_dp):
            value = w_refs[s][t * rows : (t + 1) * rows, :]
            if t < 3:
                w_all[t, s * rows : (s + 1) * rows, :] = value
            else:
                m_all[s * rows : (s + 1) * rows, :] = value
    send(w_all)
    send(m_all)
    lows = [ref[4 * rows :, :] for ref in w_refs]
    _, heads, share = bias_shape
    taken = min(128, width)
    total = jnp.zeros((small_rows, width), f32)
    column = lax.broadcasted_iota(jnp.int32, (taken, width), 1)
    lane = entries(taken)
    for s in range(n_dp):
        target = jnp.where(lane < share, (place[0] ^ order[s]) * share + lane, -1)
        chosen = jnp.where(column % head_size == target, 1.0, 0.0).astype(bf16)
        total = total + dot(lows[s][:, :taken], chosen)
    row = entries(small_rows) - small_rows // 2
    head = lax.broadcasted_iota(jnp.int32, (small_rows, width), 1) // head_size
    biases = [column_sum(jnp.where(row == t * heads + head, total, 0.0)) for t in range(2)]
    if expand_share == rows:
        line = jnp.concatenate([low[6:7, :rows] for low in lows], axis=1).astype(f32)
        expand_out[...] = from_slots(line, place[0], n_dp)
    else:
        total = jnp.zeros((small_rows, expand_out.shape[1]), f32)
        for s in range(n_dp):
            owner = place[0] ^ order[s]
            target = jnp.where(lane < expand_share, lane + owner * expand_share, -1)
            total = total + dot(lows[s][:, :taken], one_hot(target, expand_out.shape[1]))
        expand_out[...] = total[6:7]
    parts = []
    for t, ref in enumerate((q_out, k_out, v_out)):
        part = dot(x, w_all[t])
        if t != 1:
            part = part + biases[t // 2]
        ref[...] = part.astype(bf16)
        send(ref)
    group = min(128, width)
    masks = head_masks(group)
    zero = jnp.zeros((), bf16)
    number = 0
    for b in range(n_fs):
        low, high = b * size, (b + 1) * size
        seen = allowed[b] > 0.0
        for g in range(0, width, group):
            q, k, v = (part[low:high, g : g + group] for part in (q_out, k_out, v_out))
            mixed = jnp.zeros((size, group), f32)
            for mask in masks:
                scores = dot_nt(jnp.where(mask, k, zero), q) * head_size**-0.5
                scores = jnp.where(seen, scores, masked_score)
                weights = jnp.exp(scores - jnp.max(scores, axis=0, keepdims=True))
                chances = weights * (1.0 / column_sum(weights))
                p_out[number] = chances
                number += 1
                mixed = mixed + dot_tn(chances.astype(bf16), jnp.where(mask, v, zero))
            o_out[low:high, g : g + group] = mixed.astype(bf16)
    send(p_out)
    send(o_out)
    total = dot_nt(o_out[...], m_all[...])
    small = jnp.concatenate([low[:, :rows] for low in lows], axis=1)
    for i, out in enumerate(outs):
        out[:size, :] = total[i * size : (i + 1) * size].astype(out.dtype)
        out[size:, :] = small.astype(out.dtype)


def first_norm_kernel(n_fs, *refs):
    parts, (x, vectors, mid, mid_low, unit_out, inverse_out) = refs[:n_fs], refs[n_fs:]
    total = sum_blocks(parts)
    size = x.shape[0] - small_rows
    small = total[size : size + vectors.shape[0]]
    vectors[...] = small
    rows = x[:size, :].astype(f32) + (total[:size] + small[0:1, :])
    unit, inverse = normalize(rows)
    middle = unit * small[1:2, :] + small[2:3, :]
    mid[...] = middle
    mid_low[...] = middle.astype(bf16)
    unit_out[...] = unit
    inverse_out[...] = inverse


def feed_kernel(n_fs, n_dp, *refs):
    mids, refs = refs[:n_fs], refs[n_fs:]
    weights, refs = refs[:n_dp], refs[n_dp:]
    bias, w1, w2, mid_all, hid_out, inner_out, outs = *refs[:6], refs[6:]
    size = mids[0].shape[0]
    for b, ref in enumerate(mids):
        mid_all[b * size : (b + 1) * size, :] = ref[...]
    rows = weights[0].shape[0] // 2
    for s, ref in enumerate(weights):
        w1[s * rows : (s + 1) * rows, :] = ref[:rows, :]
        w2[s * rows : (s + 1) * rows, :] = ref[rows:, :]
    send(mid_all)
    send(w1)
    send(w2)
    chunk = min(256, hid_out.shape[1])
    for c in range(0, hid_out.shape[1], chunk):
        value = dot(mid_all[...], w1[:, c : c + chunk]) + bias[:, c : c + chunk]
        inner_out[:, c : c + chunk] = value
        cdf = 0.5 * (1.0 + lax.erf(value * root_half))
        hid_out[:, c : c + chunk] = (value * cdf).astype(bf16)
    send(hid_out)
    chunk = min(256, w2.shape[0])
    for c in range(0, w2.shape[0], chunk):
        store_columns(outs, c // chunk, dot_nt(hid_out[...], w2[c : c + chunk, :]))


def second_norm_kernel(n_fs, n_dp, *refs):
    index = own_place()
    parts, refs = refs[:n_fs], refs[n_fs:]
    mid, vectors, grad, live, layer_out, dh, dh_low, sums = refs
    rows = mid[...] + (sum_blocks(parts) + vectors[3:4, :])
    unit, inverse = normalize(rows)
    alive = live[...]
    final = (unit * vectors[4:5, :] + vectors[5:6, :]) * alive
    layer_out[...] = from_slots(final, index[0], n_dp).astype(bf16)
    upstream = to_slots(grad[...].astype(f32), index[0], n_dp) * alive
    down = normalize_back(upstream, vectors[4:5, :], unit, inverse)
    low = down.astype(bf16)
    dh[...] = down
    dh_low[...] = low
    sums[0:1, :] = column_sum(low.astype(f32))
    sums[1:2, :] = column_sum(upstream * unit)
    sums[2:3, :] = column_sum(upstream)


def feed_back_kernel(n_fs, *refs):
    grads, refs = refs[:n_fs], refs[n_fs:]
    w2, slope, w1, du_out, bias_out, outs = *refs[:5], refs[5:]
    rows = stacked(grads)
    chunk = min(256, du_out.shape[1])
    for c in range(0, du_out.shape[1], chunk):
        du = dot(rows, w2[:, c : c + chunk]) * slope[:, c : c + chunk].astype(f32)
        du = du.astype(bf16)
        du_out[:, c : c + chunk] = du
        bias_out[:, c : c + chunk] = column_sum(du.astype(f32))
    send(du_out)
    chunk = min(256, w1.shape[1])
    for c in range(0, w1.shape[1], chunk):
        store_columns(outs, c // chunk, dot(du_out[...], w1[:, c : c + chunk]))


def slot_refs(keep, give):
    half = keep.shape[0]
    return [keep.at[s] for s in range(half)] + [give.at[s] for s in range(half)]


def contract_grad_kernel(n_fs, turned, *refs):
    grads, slots = stacked(refs[:n_fs]), slot_refs(*refs[n_fs:])
    left = turned[...]
    size = slots[0].shape[1]
    for s in reversed(range(0, len(slots), 2)):
        pair = dot(left, grads[:, s * size : (s + 2) * size])
        slots[s][...] = pair[:, :size].astype(bf16)
        slots[s + 1][...] = pair[:, size:].astype(bf16)


def expand_grad_kernel(du, turned, keep, give):
    left = turned[...]
    size = keep.shape[1]
    for s, slot in reversed(list(enumerate(slot_refs(keep, give)))):
        slot[...] = dot(left[s * size : (s + 1) * size], du[...]).astype(bf16)


def first_back_kernel(n_fs, *refs):
    parts, refs = refs[:n_fs], refs[n_fs:]
    dh2, unit, inverse, vectors, second, dh, out = refs
    upstream = dh2[...] + sum_blocks(parts)
    units = unit[...]
    down = normalize_back(upstream, vectors[1:2, :], units, inverse[...])
    low = down.astype(bf16)
    size = dh2.shape[0]
    dh[...] = down
    out[:size, :] = low
    out[size:, :] = jnp.concatenate(
        [
            column_sum(low.astype(f32)),
            column_sum(upstream * units),
            column_sum(upstream),
            second[...],
            jnp.zeros((small_rows - 3 - second.shape[0], upstream.shape[1]), f32),
        ],
        axis=0,
    ).astype(bf16)


def attend_back_kernel(n_fs, *refs):
    grads, refs = refs[:n_fs], refs[n_fs:]
    mixing, q_in, k_in, v_in, p_in, dq_out, dk_out, dv_out = refs
    width = q_in.shape[1]
    size = grads[0].shape[0] - small_rows
    group = min(128, width)
    masks = head_masks(group)
    zero = jnp.zeros((), bf16)
    rows = jnp.concatenate([ref[:size, :] for ref in grads], axis=0)
    grad_mixed = dot(rows, mixing[...]).astype(bf16)
    number = 0
    for b in range(n_fs):
        low, high = b * size, (b + 1) * size
        for g in range(0, width, group):
            q, k, v = (part[low:high, g : g + group] for part in (q_in, k_in, v_in))
            do = grad_mixed[low:high, g : g + group]
            dq = jnp.zeros((size, group), f32)
            dk = jnp.zeros((size, group), f32)
            dv = jnp.zeros((size, group), f32)
            for mask in masks:
                chances = p_in[number]
                number += 1
                masked_do = jnp.where(mask, do, zero)
                dp = dot_nt(v, masked_do)
                ds = chances * (dp - column_sum(dp * chances))
                ds = (ds * head_size**-0.5).astype(bf16)
                dv = dv + dot(chances.astype(bf16), masked_do)
                dq = dq + dot_tn(ds, jnp.where(mask, k, zero))
                dk = dk + dot(ds, jnp.where(mask, q, zero))
            dq_out[low:high, g : g + group] = dq.astype(bf16)
            dk_out[low:high, g : g + group] = dk.astype(bf16)
            dv_out[low:high, g : g + group] = dv.astype(bf16)


def input_back_kernel(weights, dq, dk, dv, *outs):
    width = weights.shape[1]
    chunk = min(256, width)
    for c in range(0, width, chunk):
        total = 0.0
        for t, part in enumerate((dq, dk, dv)):
            total = total + dot_nt(part[...], weights[t, c : c + chunk, :])
        store_columns(outs, c // chunk, total)


def attend_grad_kernel(n_fs, n_dp, bias_shape, *refs):
    place = own_place()
    grads, refs = refs[:n_fs], refs[n_fs:]
    x, mixed, dq, dk, dv, expand_sums = refs[:6]
    slots = slot_refs(*refs[6:])
    size = grads[0].shape[0] - small_rows
    width = slots[0].shape[1]
    branch = jnp.concatenate([ref[:size, :] for ref in grads], axis=0)
    left = branch.T
    share = left.shape[0] // n_dp
    inputs = x[...]
    for t, value in ((3, mixed), (0, dq), (1, dk), (2, dv)):
        result = dot(left if t == 3 else inputs, value[...]).astype(bf16)
        for s in range(n_dp):
            slots[s][t * share : (t + 1) * share, :] = result[s * share : (s + 1) * share]
    vectors = jnp.zeros((small_rows, x.shape[0]), f32)
    for ref in grads:
        vectors = vectors + ref[size:, :].astype(f32)
    _, heads, part = bias_shape
    padding = jnp.zeros((small_rows - 2, width), f32)
    sums = [column_sum(ref[...].astype(f32)) for ref in (dq, dv)]
    sums = jnp.concatenate(sums + [padding], axis=0).astype(bf16)
    expand = expand_sums[...]
    expand_part = expand.shape[1] // n_dp
    if expand_part == share:
        expand = to_slots(expand, place[0], n_dp)
    column = entries(width)
    order = slot_order(n_dp)
    for s in range(n_dp):
        owner = place[0] ^ order[s]
        inside = (column % head_size) // part == owner
        lane = jnp.where(inside, column // head_size * part + column % part, -1)
        low = dot(sums, one_hot(lane, share))
        if expand_part == share:
            line = expand[:, s * share : (s + 1) * share]
        else:
            spot = entries(expand.shape[1])
            spot = jnp.where(spot // expand_part == owner, spot % expand_part, -1)
            rows = jnp.concatenate([expand, jnp.zeros((7, expand.shape[1]), f32)], axis=0)
            line = dot(rows.astype(bf16), one_hot(spot, share))[0:1]
        if share < width:
            slots[s][4 * share :, share:] = jnp.zeros((small_rows, width - share), bf16)
        slots[s][4 * share :, :share] = jnp.concatenate(
            [vectors[0:6, s * share : (s + 1) * share], line, low[0 : small_rows - 7]], axis=0
        ).astype(bf16)


def joint_kernel(left, right, attend_out, output_out, bias_out, expand_out, vectors_out):
    place = own_place()
    total = left[0].astype(f32) + right[0].astype(f32)
    rows = attend_out.shape[1]
    for t in range(3):
        attend_out[t] = total[t * rows : (t + 1) * rows]
    send(attend_out)
    output_out[...] = total[3 * rows : 4 * rows].T
    small = total[4 * rows :]
    _, heads, part = bias_out.shape
    for t in range(2):
        for h in range(heads):
            bias_out[t, h : h + 1, :] = small[7 + t : 8 + t, h * part : (h + 1) * part]
    expand_out[...] = small[6:7, : expand_out.shape[1]]
    count, lanes = vectors_out.shape
    found = jnp.zeros((count, lanes), f32)
    for i in range(rows // lanes):
        found = found + jnp.where(place[1] == i, small[:count, i * lanes : (i + 1) * lanes], 0.0)
    vectors_out[...] = found


def tokens_grad_kernel(n_fs, n_dp, *refs):
    index = own_place()
    parts, (dh, out) = refs[:n_fs], refs[n_fs:]
    out[...] = from_slots(dh[...] + sum_blocks(parts), index[0], n_dp)


def segment_kernel(n_fs, lengths, owners, allowed, live):
    place = own_place()
    size = live.shape[0]
    slot = lax.broadcasted_iota(jnp.int32, (8, size), 1)
    blocks = [place[0] * n_fs + (place[1] ^ i) for i in range(n_fs)]

    def add(s, carry):
        result = []
        for block, (offset, found) in zip(blocks, carry):
            count = jnp.where(owners[s] == block, lengths[s], 0)
            found = jnp.where((slot >= offset) & (slot < offset + count), s, found)
            result.append((offset + count, found))
        return tuple(result)

    start = tuple((jnp.int32(0), jnp.full((8, size), -1, jnp.int32)) for _ in blocks)
    for i, (_, found) in enumerate(lax.fori_loop(0, lengths.shape[0], add, start)):
        along = jnp.broadcast_to(found[0:1].astype(f32), (size, size))
        down = along.T
        allowed[i] = jnp.where((along == down) & (down >= 0.0), 1.0, 0.0)
        if i == 0:
            live[...] = jnp.where(down[:, 0:1] >= 0.0, 1.0, 0.0)


def prepare_kernel(parity, *refs):
    for source in refs[:5]:
        if isinstance(source, Late):
            source.ready()

    @pl.when(own_place()[0] % 2 == parity)
    def _():
        inner, slope = refs[0], refs[-5]
        chunk = min(256, inner.shape[1])
        for c in range(0, inner.shape[1], chunk):
            value = inner[:, c : c + chunk]
            cdf = 0.5 * (1.0 + lax.erf(value * root_half))
            density = jnp.exp(-0.5 * value * value) * inverse_root_tau
            slope[:, c : c + chunk] = (cdf + value * density).astype(bf16)
        for source, target in zip(refs[1:5], refs[-4:]):
            target[...] = source[...].T


def on_device(
    tokens,
    attend_weight,
    attend_bias,
    output_weight,
    expand_weight,
    expand_bias,
    contract_weight,
    layer_vectors,
    sequence_lengths,
    sequence_owner,
    output_grad,
):
    size, width = tokens.shape
    n_fs = lax.axis_size("fs")
    n_dp = lax.axis_size("dp")
    many = n_fs * size
    share = width // n_dp
    heads_width = attend_weight.shape[2]
    hidden_width = expand_weight.shape[1]
    n_vectors, lanes = layer_vectors.shape
    bias_shape = attend_bias.shape

    def send_back(parts):
        return [parts[0]] + [swap(parts[j], "fs", j) for j in range(1, n_fs)]

    (attend_part,) = kernel_call(
        pack_kernel,
        hot([shape_of((4 * share + small_rows, heads_width), bf16)]),
        Far(attend_weight),
        Far(output_weight),
        Far(attend_bias),
        Far(layer_vectors),
        Far(expand_bias),
        extra=56,
    )
    (own_rows,) = kernel_call(
        functools.partial(slots_kernel, n_dp), hot([shape_of((size + small_rows, width), bf16)]), Far(tokens)
    )
    inputs = gather_fs(own_rows)
    allowed, live = kernel_call(
        functools.partial(segment_kernel, n_fs),
        hot([shape_of((n_fs, size, size), f32), shape_of((size, 1), f32)]),
        sequence_lengths,
        sequence_owner,
    )
    attend_lane = gather_lane(attend_part)
    attend_parts = gather_cores(attend_lane)
    (feed_part,) = kernel_call(
        pair_kernel,
        [shape_of((2 * share, hidden_width), bf16)],
        Far(after(expand_weight, allowed, *inputs[1:])),
        Far(contract_weight),
    )
    feed_lane = gather_lane(after(feed_part, *attend_lane.values()))
    half_shape = shape_of((many, heads_width), bf16)
    n_scores = n_fs * heads_width // head_size
    (
        queries,
        key_rows,
        values,
        mixed,
        chances,
        expand_row,
        x_all,
        w_all,
        mixing,
        *branch_parts,
    ) = kernel_call(
        functools.partial(attend_kernel, n_fs, n_dp, bias_shape, expand_bias.size),
        [half_shape] * 4
        + [shape_of((n_scores, size, size), f32), Hot(shape_of((1, hidden_width), f32))]
        + [
            shape_of((many, width), bf16),
            shape_of((3, width, heads_width), bf16),
            shape_of((width, heads_width), bf16),
        ]
        + block_shapes(n_fs, size + small_rows, width),
        *hot(attend_parts),
        *hot(inputs),
        Hot(allowed),
        extra=4,
    )
    vectors, middle, middle_low, unit_first, inverse_first = kernel_call(
        functools.partial(first_norm_kernel, n_fs),
        hot(
            [
                shape_of((n_vectors, width), f32),
                shape_of((size, width), f32),
                shape_of((size, width), bf16),
                shape_of((size, width), f32),
                shape_of((size, 1), f32),
            ]
        ),
        *hot(send_back(branch_parts)),
        Hot(after(own_rows, *list(feed_lane.values())[1:-1])),
    )
    middles = gather_fs(middle_low)
    last = list(feed_lane)[-1]
    feed_parts = gather_cores({**feed_lane, last: after(feed_lane[last], *middles[1:])})
    wide = shape_of((many, hidden_width), bf16)
    w1, w2, mid_all, hidden, inner, *result_parts = kernel_call(
        functools.partial(feed_kernel, n_fs, n_dp),
        [
            shape_of((width, hidden_width), bf16),
            shape_of((width, hidden_width), bf16),
            shape_of((many, width), bf16),
            wide,
            Hot(shape_of((many, hidden_width), f32)),
        ]
        + block_shapes(n_fs, size, width),
        *hot(middles),
        *hot(feed_parts),
        Hot(expand_row),
        extra=3,
    )
    turned = hot(
        [wide, shape_of((hidden_width, many), bf16)]
        + [shape_of((width, many), bf16)] * 2
        + [shape_of((hidden_width, width), bf16)]
    )
    ready = kernel_call(
        functools.partial(prepare_kernel, 0), turned, Hot(inner), hidden, mid_all, x_all, w1
    )
    result_parts = [after(part, ready[0]) for part in result_parts]
    layer_output, dh2, dffn, sums_second = kernel_call(
        functools.partial(second_norm_kernel, n_fs, n_dp),
        [
            Far(shape_of((size, width), bf16)),
            Hot(shape_of((size, width), f32)),
            Hot(shape_of((size, width), bf16)),
            Hot(shape_of((3, width), f32)),
        ],
        *hot(send_back(result_parts)),
        Hot(middle),
        Hot(vectors),
        Far(output_grad),
        Hot(live),
        extra=3,
    )
    dffns = gather_fs(dffn)
    slope, hidden_turned, mid_turned, x_turned, w1_turned = kernel_call(
        functools.partial(prepare_kernel, 1),
        turned,
        Hot(inner),
        hidden,
        mid_all,
        x_all,
        w1,
        *hot([after(ready[0], dffn), *ready[1:]]),
        aliases={5: 0, 6: 1, 7: 2, 8: 3, 9: 4},
    )
    contract_slots = kernel_call(
        functools.partial(contract_grad_kernel, n_fs),
        hot([shape_of((n_dp // 2, hidden_width, share), bf16)] * 2),
        Hot(hidden_turned),
        *hot(dffns),
        extra=2,
    )
    du, expand_sums, *middle_parts = kernel_call(
        functools.partial(feed_back_kernel, n_fs),
        [wide, Hot(shape_of((1, hidden_width), f32))]
        + block_shapes(n_fs, size, width),
        *hot(dffns),
        w2,
        Hot(after(slope, contract_slots[0])),
        Hot(w1_turned),
        extra=3,
    )
    back_parts = send_back(middle_parts)
    def last_sum(shape):
        return lambda keep, taken: kernel_call(
            last_kernel, [Far(shape_of(shape, f32))], keep, taken
        )[0]

    contract_pair = sum_cores(*contract_slots)
    contract_last, contract_rounds = sum_lanes(*contract_pair, lambda keep, taken: (keep, taken))
    expand_slots = kernel_call(
        expand_grad_kernel,
        hot([shape_of((n_dp // 2, share, hidden_width), bf16)] * 2),
        after(du, contract_pair[1]),
        Hot(mid_turned),
        extra=2,
    )

    expand_pair = sum_cores(*expand_slots)
    expand_grad, expand_rounds = sum_lanes(*expand_pair, last_sum(expand_weight.shape))
    dh1, dbranch = kernel_call(
        functools.partial(first_back_kernel, n_fs),
        hot([shape_of((size, width), f32), shape_of((size + small_rows, width), bf16)]),
        *hot(back_parts),
        Hot(after(dh2, expand_slots[0])),
        Hot(unit_first),
        Hot(inverse_first),
        Hot(vectors),
        Hot(sums_second),
    )
    branches = gather_fs(dbranch)
    dq, dk, dv = kernel_call(
        functools.partial(attend_back_kernel, n_fs),
        hot([half_shape] * 3),
        *hot(branches),
        after(mixing, expand_pair[1]),
        queries,
        key_rows,
        values,
        chances,
        extra=2.5,
    )
    attend_slots = kernel_call(
        functools.partial(attend_grad_kernel, n_fs, n_dp, bias_shape),
        hot([shape_of((n_dp // 2, 4 * share + small_rows, heads_width), bf16)] * 2),
        *hot(branches),
        Hot(after(x_turned, expand_rounds[-1], contract_last[1].array)),
        mixed,
        Hot(dq),
        Hot(dk),
        Hot(dv),
        Hot(expand_sums),
        extra=3,
    )
    keep, taken = (part.array for part in contract_last)
    contract_grad = last_sum(contract_weight.shape)(Hot(after(keep, attend_slots[0])), Hot(taken))
    attend_keep, attend_give = sum_cores(*attend_slots)
    input_parts = kernel_call(
        input_back_kernel,
        block_shapes(n_fs, size, width),
        after(w_all, attend_give),
        Hot(dq),
        Hot(dk),
        Hot(dv),
    )
    (tokens_grad,) = kernel_call(
        functools.partial(tokens_grad_kernel, n_fs, n_dp),
        [Far(shape_of((size, width), f32))],
        *hot(send_back(input_parts)),
        Hot(dh1),
    )
    small_outs = [
        shape_of(attend_bias.shape, f32),
        shape_of(expand_bias.shape, f32),
        shape_of(layer_vectors.shape, f32),
    ]
    sums, _ = sum_lanes(
        after(attend_keep, tokens_grad, expand_grad),
        attend_give,
        lambda keep, taken: kernel_call(
            joint_kernel,
            [Far(shape_of(attend_weight.shape, f32)), Far(shape_of(output_weight.shape, f32))]
            + hot(small_outs),
            keep,
            taken,
        ),
    )
    attend_grad, output_weight_grad, attend_bias_grad, expand_bias_grad, vector_grad = sums
    return (
        layer_output,
        tokens_grad,
        attend_grad,
        attend_bias_grad,
        output_weight_grad,
        expand_grad,
        expand_bias_grad,
        contract_grad,
        vector_grad,
    )


def solution(mesh):
    in_specs = (
        P(("dp", "fs"), None),
        P(None, "dp", "fs"),
        P(None, "fs", "dp"),
        P("fs", "dp"),
        P("dp", "fs"),
        P("fs", "dp"),
        P("fs", "dp"),
        P(None, ("dp", "fs")),
        P(),
        P(),
        P(("dp", "fs"), None),
    )
    out_specs = (
        P(("dp", "fs"), None),
        P(("dp", "fs"), None),
        P(None, "dp", "fs"),
        P(None, "fs", "dp"),
        P("fs", "dp"),
        P("dp", "fs"),
        P("fs", "dp"),
        P("fs", "dp"),
        P(None, ("dp", "fs")),
    )
    return jax.shard_map(
        on_device, mesh=mesh, in_specs=in_specs, out_specs=out_specs, check_vma=False
    )
```

```python
import functools

import jax
import jax.numpy as jnp
from jax import lax
from jax.experimental import pallas as pl
from jax.experimental.pallas import tpu as pltpu
from jax.sharding import PartitionSpec as P

masked_score = -1e30
norm_eps = 1e-12
root_half = 0.7071067811865476
inverse_root_tau = 0.3989422804014327
small_rows = 16
head_size = 64
f32 = jnp.float32
bf16 = jnp.bfloat16


def slot_order(count):
    order = [0]
    while len(order) < count:
        step = count // (2 * len(order))
        order = order + [entry | step for entry in order]
    bits = count.bit_length() - 1
    return [int(format(i, "b").zfill(bits)[::-1], 2) for i in range(count)]


def swap(part, axis_name, distance):
    count = lax.axis_size(axis_name)
    return lax.ppermute(part, axis_name, [(i, i ^ distance) for i in range(count)])


def gather_fs(part):
    return [part] + [swap(part, "fs", j) for j in range(1, lax.axis_size("fs"))]


def after(part, *earlier):
    return lax.optimization_barrier((part,) + earlier)[0]


def gather_lane(part, *earlier):
    held = {0: part}
    steps = []
    step = lax.axis_size("dp") // 2
    while step > 1:
        steps.append(step)
        held[step] = swap(part, "dp", step)
        step //= 2
    direct = list(held.values())[1:] + list(earlier)
    for i, step in enumerate(steps):
        for entry in [e for e in held if e % steps[i - 1] == 0 and e and i]:
            if entry | step not in held:
                held[entry | step] = swap(after(held[entry], *direct), "dp", step)
    return held


def gather_cores(held, *earlier):
    both = dict(held)
    for entry, piece in held.items():
        if earlier:
            piece = after(piece, *earlier)
        both[entry | 1] = swap(piece, "dp", 1)
    return [both[entry] for entry in slot_order(len(both))]


def sum_cores(keep, give):
    taken = swap(give, "dp", 1)
    half = Hot(shape_of((keep.shape[0] // 2,) + keep.shape[1:], bf16))
    return kernel_call(add_kernel, [half, half], Hot(keep), Hot(taken))


def sum_lanes(keep, give, done):
    step = 2
    rounds = []
    while True:
        taken = swap(give, "dp", step)
        step *= 2
        if step == lax.axis_size("dp"):
            return done(Hot(keep), Hot(taken)), rounds
        half = Hot(shape_of((keep.shape[0] // 2,) + keep.shape[1:], bf16))
        keep, give = kernel_call(add_kernel, [half, half], Hot(keep), Hot(taken))
        rounds.append(give)


class Late:
    def __init__(self, source, target, semaphore):
        self.target = target
        self.shape = target.shape
        self.dtype = target.dtype
        self.copy = pltpu.make_async_copy(source, target, semaphore)
        self.copy.start()
        self.waits = True

    def ready(self):
        if self.waits:
            self.copy.wait()
            self.waits = False

    def __getitem__(self, where):
        self.ready()
        return self.target[where]


class Leaving:
    def __init__(self, source, target, semaphore):
        self.source = source
        self.shape = source.shape
        self.dtype = source.dtype
        self.copy = pltpu.make_async_copy(source, target, semaphore)
        self.sent = False

    def send(self):
        if not self.sent:
            self.copy.start()
            self.sent = True

    def __getitem__(self, where):
        return self.source[where]

    def __setitem__(self, where, value):
        self.source[where] = value


class Far:
    def __init__(self, array):
        self.array = array


class Hot:
    def __init__(self, array):
        self.array = array


def hot(arrays):
    return [Hot(array) for array in arrays]


def kernel_call(body, outs, *args, extra=1.5, aliases=None):
    def far(a):
        return isinstance(a, Far)

    def bare(a):
        return a.array if isinstance(a, (Far, Hot)) else a

    late = [far(a) for a in args]
    leaving = [far(a) for a in outs]
    args = [bare(a) for a in args]
    outs = [bare(a) for a in outs]
    far_args = [a for a, b in zip(args, late) if b]
    far_outs = [a for a, b in zip(outs, leaving) if b]

    own = sum(a.size * a.dtype.itemsize for a in far_args + far_outs)
    limit = own + int(extra * 2**20) * max(1, lax.axis_size("fs") // 4)

    def whole(*refs):
        given, refs = refs[: len(args)], refs[len(args) :]
        out_refs, refs = refs[: len(outs)], refs[len(outs) :]
        items = []
        number = 0
        for ref, is_far in zip(given, late):
            if is_far:
                ref = Late(ref, refs[number], refs[-1].at[number])
                number += 1
            items.append(ref)
        targets = []
        for ref, is_far in zip(out_refs, leaving):
            if is_far:
                ref = Leaving(refs[number], ref, refs[-1].at[number])
                number += 1
            targets.append(ref)
        body(*items, *targets)
        for target in targets:
            if isinstance(target, Leaving):
                target.send()
        for item in items:
            if isinstance(item, Late):
                item.ready()
        for target in targets:
            if isinstance(target, Leaving):
                target.copy.wait()

    def place(a, is_far):
        if a.ndim == 1:
            return pltpu.SMEM
        return pltpu.HBM if is_far else pltpu.VMEM

    return pl.pallas_call(
        whole,
        out_shape=outs,
        in_specs=[pl.BlockSpec(memory_space=place(a, b)) for a, b in zip(args, late)],
        out_specs=[pl.BlockSpec(memory_space=place(a, b)) for a, b in zip(outs, leaving)],
        scratch_shapes=[pltpu.VMEM(a.shape, a.dtype) for a in far_args + far_outs]
        + [pltpu.SemaphoreType.DMA((max(1, len(far_args + far_outs)),))],
        compiler_params=pltpu.CompilerParams(vmem_limit_bytes=limit),
        cost_estimate=pl.CostEstimate(flops=0, bytes_accessed=0, transcendentals=0),
        input_output_aliases=aliases or {},
    )(*args)


def send(ref):
    if isinstance(ref, Leaving):
        ref.send()


def shape_of(shape, kind):
    return jax.ShapeDtypeStruct(shape, kind)


def dot(left, right):
    return jnp.dot(left, right, preferred_element_type=f32)


def dot_nt(left, right):
    return lax.dot_general(left, right, (((1,), (1,)), ((), ())), preferred_element_type=f32)


def dot_tn(left, right):
    return lax.dot_general(left, right, (((0,), (0,)), ((), ())), preferred_element_type=f32)


def flip_blocks(blocks, index):
    step = 1
    while step < len(blocks):
        chosen = (index // step) % 2 == 1
        blocks = [jnp.where(chosen, blocks[i ^ step], blocks[i]) for i in range(len(blocks))]
        step *= 2
    return blocks


def split_columns(rows, count):
    size = rows.shape[1] // count
    return [rows[:, i * size : (i + 1) * size] for i in range(count)]


def to_slots(rows, index, count):
    blocks = flip_blocks(split_columns(rows, count), index)
    return jnp.concatenate([blocks[entry] for entry in slot_order(count)], axis=1)


def from_slots(rows, index, count):
    slots = split_columns(rows, count)
    order = slot_order(count)
    blocks = [slots[order.index(i)] for i in range(count)]
    return jnp.concatenate(flip_blocks(blocks, index), axis=1)


def row_mean(rows):
    return jnp.mean(rows, axis=1, keepdims=True)


def normalize(rows):
    centred = rows - row_mean(rows)
    inverse = lax.rsqrt(row_mean(centred * centred) + norm_eps)
    return (centred * inverse, inverse)


def normalize_back(upstream, gain, unit, inverse):
    scaled = upstream * gain
    return inverse * (scaled - row_mean(scaled) - unit * row_mean(scaled * unit))


def column_sum(rows):
    return jnp.sum(rows, axis=0, keepdims=True)


def stacked(refs):
    return jnp.concatenate([ref[...] for ref in refs], axis=0)


def beside(refs):
    return jnp.concatenate([ref[...] for ref in refs], axis=1)


def sum_blocks(refs):
    total = refs[0][...]
    for ref in refs[1:]:
        total = total + ref[...].astype(f32)
    return total


def store_blocks(refs, total):
    size = refs[0].shape[0]
    for i, ref in enumerate(refs):
        ref[...] = total[i * size : (i + 1) * size].astype(ref.dtype)


def store_columns(refs, place, total):
    size = refs[0].shape[0]
    width = total.shape[1]
    for i, ref in enumerate(refs):
        part = total[i * size : (i + 1) * size].astype(ref.dtype)
        ref[:, place * width : (place + 1) * width] = part


def add_kernel(left, right, keep, give):
    half = keep.shape[0]
    for out, start in ((give, half), (keep, 0)):
        for i in range(half):
            total = left[start + i].astype(f32) + right[start + i].astype(f32)
            out[i] = total.astype(out.dtype)


def last_kernel(left, right, out):
    out[...] = left[0].astype(f32) + right[0].astype(f32)


def block_shapes(count, rows, width):
    return hot([shape_of((rows, width), f32)] + [shape_of((rows, width), bf16)] * (count - 1))


def one_hot(target, width):
    column = lax.broadcasted_iota(jnp.int32, (target.shape[0], width), 1)
    return jnp.where(column == target, 1.0, 0.0).astype(bf16)


def entries(count):
    return lax.broadcasted_iota(jnp.int32, (count, 1), 0)


def pack_kernel(weight, mixing, bias, vectors, expand_bias, out):
    place = own_place()
    rows, width = weight.shape[1:]
    for t in range(3):
        out[t * rows : (t + 1) * rows, :] = weight[t]
    out[3 * rows : 4 * rows, :] = mixing[...].T
    count, lanes = vectors.shape
    _, heads, part = bias.shape
    pads = small_rows // 2 - 2 * heads
    table = [
        dot(vectors[...], one_hot(entries(lanes) + place[1] * lanes, width)),
        dot(expand_bias[...], one_hot(entries(expand_bias.shape[1]), width)),
        jnp.zeros((small_rows // 2 - count - 1, width), f32),
    ]
    table = table + [dot(bias[t], one_hot(entries(part), width)) for t in range(2)]
    table = table + [jnp.zeros((pads, width), f32)]
    table = [rows for rows in table if rows.shape[0]]
    out[4 * rows :, :] = jnp.concatenate(table, axis=0).astype(bf16)


def slots_kernel(n_dp, tokens, out):
    size = tokens.shape[0]
    out[:size, :] = to_slots(tokens[...].astype(f32), own_place()[0], n_dp).astype(bf16)
    out[size:, :] = jnp.zeros((small_rows, out.shape[1]), bf16)


def pair_kernel(expand, contract, out):
    rows = expand.shape[0]
    out[:rows, :] = expand[...]
    out[rows:, :] = contract[...].T


def group_part(refs, t, count):
    rows = refs[0].shape[0] // count
    return jnp.concatenate([ref[t * rows : (t + 1) * rows, :] for ref in refs], axis=0)


def own_place():
    return (lax.axis_index("dp"), lax.axis_index("fs"))


def head_masks(width):
    lane = lax.broadcasted_iota(jnp.int32, (1, width), 1)
    return [lane // head_size == h for h in range(width // head_size)]


def attend_kernel(n_fs, n_dp, bias_shape, expand_share, *refs):
    place = own_place()
    w_refs, refs = refs[:n_dp], refs[n_dp:]
    x_refs, refs = refs[:n_fs], refs[n_fs:]
    allowed, q_out, k_out, v_out, o_out, p_out, expand_out = refs[:7]
    x_all, w_all, m_all = refs[7:10]
    outs = refs[10:]
    width = w_refs[0].shape[1]
    rows = (w_refs[0].shape[0] - small_rows) // 4
    order = slot_order(n_dp)
    size = x_refs[0].shape[0] - small_rows
    for b, ref in enumerate(x_refs):
        x_all[b * size : (b + 1) * size, :] = ref[:size, :]
    send(x_all)
    x = x_all[...]
    for t, ref in enumerate((w_all, w_all, w_all, m_all)):
        for s in range(n_dp):
            value = w_refs[s][t * rows : (t + 1) * rows, :]
            if t < 3:
                w_all[t, s * rows : (s + 1) * rows, :] = value
            else:
                m_all[s * rows : (s + 1) * rows, :] = value
    send(w_all)
    send(m_all)
    lows = [ref[4 * rows :, :] for ref in w_refs]
    _, heads, share = bias_shape
    taken = min(128, width)
    total = jnp.zeros((small_rows, width), f32)
    column = lax.broadcasted_iota(jnp.int32, (taken, width), 1)
    lane = entries(taken)
    for s in range(n_dp):
        target = jnp.where(lane < share, (place[0] ^ order[s]) * share + lane, -1)
        chosen = jnp.where(column % head_size == target, 1.0, 0.0).astype(bf16)
        total = total + dot(lows[s][:, :taken], chosen)
    row = entries(small_rows) - small_rows // 2
    head = lax.broadcasted_iota(jnp.int32, (small_rows, width), 1) // head_size
    biases = [column_sum(jnp.where(row == t * heads + head, total, 0.0)) for t in range(2)]
    if expand_share == rows:
        line = jnp.concatenate([low[6:7, :rows] for low in lows], axis=1).astype(f32)
        expand_out[...] = from_slots(line, place[0], n_dp)
    else:
        total = jnp.zeros((small_rows, expand_out.shape[1]), f32)
        for s in range(n_dp):
            owner = place[0] ^ order[s]
            target = jnp.where(lane < expand_share, lane + owner * expand_share, -1)
            total = total + dot(lows[s][:, :taken], one_hot(target, expand_out.shape[1]))
        expand_out[...] = total[6:7]
    parts = []
    for t, ref in enumerate((q_out, k_out, v_out)):
        part = dot(x, w_all[t])
        if t != 1:
            part = part + biases[t // 2]
        ref[...] = part.astype(bf16)
        send(ref)
    group = min(128, width)
    masks = head_masks(group)
    zero = jnp.zeros((), bf16)
    number = 0
    for b in range(n_fs):
        low, high = b * size, (b + 1) * size
        seen = allowed[b] > 0.0
        for g in range(0, width, group):
            q, k, v = (part[low:high, g : g + group] for part in (q_out, k_out, v_out))
            mixed = jnp.zeros((size, group), f32)
            for mask in masks:
                scores = dot_nt(jnp.where(mask, k, zero), q) * head_size**-0.5
                scores = jnp.where(seen, scores, masked_score)
                weights = jnp.exp(scores - jnp.max(scores, axis=0, keepdims=True))
                chances = weights * (1.0 / column_sum(weights))
                p_out[number] = chances
                number += 1
                mixed = mixed + dot_tn(chances.astype(bf16), jnp.where(mask, v, zero))
            o_out[low:high, g : g + group] = mixed.astype(bf16)
    send(p_out)
    send(o_out)
    total = dot_nt(o_out[...], m_all[...])
    small = jnp.concatenate([low[:, :rows] for low in lows], axis=1)
    for i, out in enumerate(outs):
        out[:size, :] = total[i * size : (i + 1) * size].astype(out.dtype)
        out[size:, :] = small.astype(out.dtype)


def first_norm_kernel(n_fs, *refs):
    parts, (x, vectors, mid, mid_low, unit_out, inverse_out) = refs[:n_fs], refs[n_fs:]
    total = sum_blocks(parts)
    size = x.shape[0] - small_rows
    small = total[size : size + vectors.shape[0]]
    vectors[...] = small
    rows = x[:size, :].astype(f32) + (total[:size] + small[0:1, :])
    unit, inverse = normalize(rows)
    middle = unit * small[1:2, :] + small[2:3, :]
    mid[...] = middle
    mid_low[...] = middle.astype(bf16)
    unit_out[...] = unit
    inverse_out[...] = inverse


def feed_kernel(n_fs, n_dp, *refs):
    mids, refs = refs[:n_fs], refs[n_fs:]
    weights, refs = refs[:n_dp], refs[n_dp:]
    bias, w1, w2, mid_all, hid_out, inner_out, outs = *refs[:6], refs[6:]
    size = mids[0].shape[0]
    for b, ref in enumerate(mids):
        mid_all[b * size : (b + 1) * size, :] = ref[...]
    rows = weights[0].shape[0] // 2
    for s, ref in enumerate(weights):
        w1[s * rows : (s + 1) * rows, :] = ref[:rows, :]
        w2[s * rows : (s + 1) * rows, :] = ref[rows:, :]
    send(mid_all)
    send(w1)
    send(w2)
    chunk = min(256, hid_out.shape[1])
    for c in range(0, hid_out.shape[1], chunk):
        value = dot(mid_all[...], w1[:, c : c + chunk]) + bias[:, c : c + chunk]
        inner_out[:, c : c + chunk] = value
        cdf = 0.5 * (1.0 + lax.erf(value * root_half))
        hid_out[:, c : c + chunk] = (value * cdf).astype(bf16)
    send(hid_out)
    chunk = min(256, w2.shape[0])
    for c in range(0, w2.shape[0], chunk):
        store_columns(outs, c // chunk, dot_nt(hid_out[...], w2[c : c + chunk, :]))


def second_norm_kernel(n_fs, n_dp, *refs):
    index = own_place()
    parts, refs = refs[:n_fs], refs[n_fs:]
    mid, vectors, grad, live, layer_out, dh, dh_low, sums = refs
    rows = mid[...] + (sum_blocks(parts) + vectors[3:4, :])
    unit, inverse = normalize(rows)
    alive = live[...]
    final = (unit * vectors[4:5, :] + vectors[5:6, :]) * alive
    layer_out[...] = from_slots(final, index[0], n_dp).astype(bf16)
    upstream = to_slots(grad[...].astype(f32), index[0], n_dp) * alive
    down = normalize_back(upstream, vectors[4:5, :], unit, inverse)
    low = down.astype(bf16)
    dh[...] = down
    dh_low[...] = low
    sums[0:1, :] = column_sum(low.astype(f32))
    sums[1:2, :] = column_sum(upstream * unit)
    sums[2:3, :] = column_sum(upstream)


def feed_back_kernel(n_fs, *refs):
    grads, refs = refs[:n_fs], refs[n_fs:]
    w2, slope, w1, du_out, bias_out, outs = *refs[:5], refs[5:]
    rows = stacked(grads)
    chunk = min(256, du_out.shape[1])
    for c in range(0, du_out.shape[1], chunk):
        du = dot(rows, w2[:, c : c + chunk]) * slope[:, c : c + chunk].astype(f32)
        du = du.astype(bf16)
        du_out[:, c : c + chunk] = du
        bias_out[:, c : c + chunk] = column_sum(du.astype(f32))
    send(du_out)
    chunk = min(256, w1.shape[1])
    for c in range(0, w1.shape[1], chunk):
        store_columns(outs, c // chunk, dot(du_out[...], w1[:, c : c + chunk]))


def slot_refs(keep, give):
    half = keep.shape[0]
    return [keep.at[s] for s in range(half)] + [give.at[s] for s in range(half)]


def contract_grad_kernel(n_fs, turned, *refs):
    grads, slots = stacked(refs[:n_fs]), slot_refs(*refs[n_fs:])
    left = turned[...]
    size = slots[0].shape[1]
    for s in reversed(range(0, len(slots), 2)):
        pair = dot(left, grads[:, s * size : (s + 2) * size])
        slots[s][...] = pair[:, :size].astype(bf16)
        slots[s + 1][...] = pair[:, size:].astype(bf16)


def expand_grad_kernel(du, turned, keep, give):
    left = turned[...]
    size = keep.shape[1]
    for s, slot in reversed(list(enumerate(slot_refs(keep, give)))):
        slot[...] = dot(left[s * size : (s + 1) * size], du[...]).astype(bf16)


def first_back_kernel(n_fs, *refs):
    parts, refs = refs[:n_fs], refs[n_fs:]
    dh2, unit, inverse, vectors, second, dh, out = refs
    upstream = dh2[...] + sum_blocks(parts)
    units = unit[...]
    down = normalize_back(upstream, vectors[1:2, :], units, inverse[...])
    low = down.astype(bf16)
    size = dh2.shape[0]
    dh[...] = down
    out[:size, :] = low
    out[size:, :] = jnp.concatenate(
        [
            column_sum(low.astype(f32)),
            column_sum(upstream * units),
            column_sum(upstream),
            second[...],
            jnp.zeros((small_rows - 3 - second.shape[0], upstream.shape[1]), f32),
        ],
        axis=0,
    ).astype(bf16)


def attend_back_kernel(n_fs, *refs):
    grads, refs = refs[:n_fs], refs[n_fs:]
    mixing, q_in, k_in, v_in, p_in, dq_out, dk_out, dv_out = refs
    width = q_in.shape[1]
    size = grads[0].shape[0] - small_rows
    group = min(128, width)
    masks = head_masks(group)
    zero = jnp.zeros((), bf16)
    rows = jnp.concatenate([ref[:size, :] for ref in grads], axis=0)
    grad_mixed = dot(rows, mixing[...]).astype(bf16)
    number = 0
    for b in range(n_fs):
        low, high = b * size, (b + 1) * size
        for g in range(0, width, group):
            q, k, v = (part[low:high, g : g + group] for part in (q_in, k_in, v_in))
            do = grad_mixed[low:high, g : g + group]
            dq = jnp.zeros((size, group), f32)
            dk = jnp.zeros((size, group), f32)
            dv = jnp.zeros((size, group), f32)
            for mask in masks:
                chances = p_in[number]
                number += 1
                masked_do = jnp.where(mask, do, zero)
                dp = dot_nt(v, masked_do)
                ds = chances * (dp - column_sum(dp * chances))
                ds = (ds * head_size**-0.5).astype(bf16)
                dv = dv + dot(chances.astype(bf16), masked_do)
                dq = dq + dot_tn(ds, jnp.where(mask, k, zero))
                dk = dk + dot(ds, jnp.where(mask, q, zero))
            dq_out[low:high, g : g + group] = dq.astype(bf16)
            dk_out[low:high, g : g + group] = dk.astype(bf16)
            dv_out[low:high, g : g + group] = dv.astype(bf16)


def input_back_kernel(weights, dq, dk, dv, *outs):
    width = weights.shape[1]
    chunk = min(256, width)
    for c in range(0, width, chunk):
        total = 0.0
        for t, part in enumerate((dq, dk, dv)):
            total = total + dot_nt(part[...], weights[t, c : c + chunk, :])
        store_columns(outs, c // chunk, total)


def attend_grad_kernel(n_fs, n_dp, bias_shape, *refs):
    place = own_place()
    grads, refs = refs[:n_fs], refs[n_fs:]
    x, mixed, dq, dk, dv, expand_sums = refs[:6]
    slots = slot_refs(*refs[6:])
    size = grads[0].shape[0] - small_rows
    width = slots[0].shape[1]
    branch = jnp.concatenate([ref[:size, :] for ref in grads], axis=0)
    left = branch.T
    share = left.shape[0] // n_dp
    inputs = x[...]
    for t, value in ((3, mixed), (0, dq), (1, dk), (2, dv)):
        result = dot(left if t == 3 else inputs, value[...]).astype(bf16)
        for s in range(n_dp):
            slots[s][t * share : (t + 1) * share, :] = result[s * share : (s + 1) * share]
    vectors = jnp.zeros((small_rows, x.shape[0]), f32)
    for ref in grads:
        vectors = vectors + ref[size:, :].astype(f32)
    _, heads, part = bias_shape
    padding = jnp.zeros((small_rows - 2, width), f32)
    sums = [column_sum(ref[...].astype(f32)) for ref in (dq, dv)]
    sums = jnp.concatenate(sums + [padding], axis=0).astype(bf16)
    expand = expand_sums[...]
    expand_part = expand.shape[1] // n_dp
    if expand_part == share:
        expand = to_slots(expand, place[0], n_dp)
    column = entries(width)
    order = slot_order(n_dp)
    for s in range(n_dp):
        owner = place[0] ^ order[s]
        inside = (column % head_size) // part == owner
        lane = jnp.where(inside, column // head_size * part + column % part, -1)
        low = dot(sums, one_hot(lane, share))
        if expand_part == share:
            line = expand[:, s * share : (s + 1) * share]
        else:
            spot = entries(expand.shape[1])
            spot = jnp.where(spot // expand_part == owner, spot % expand_part, -1)
            rows = jnp.concatenate([expand, jnp.zeros((7, expand.shape[1]), f32)], axis=0)
            line = dot(rows.astype(bf16), one_hot(spot, share))[0:1]
        if share < width:
            slots[s][4 * share :, share:] = jnp.zeros((small_rows, width - share), bf16)
        slots[s][4 * share :, :share] = jnp.concatenate(
            [vectors[0:6, s * share : (s + 1) * share], line, low[0 : small_rows - 7]], axis=0
        ).astype(bf16)


def joint_kernel(left, right, attend_out, output_out, bias_out, expand_out, vectors_out):
    place = own_place()
    total = left[0].astype(f32) + right[0].astype(f32)
    rows = attend_out.shape[1]
    for t in range(3):
        attend_out[t] = total[t * rows : (t + 1) * rows]
    send(attend_out)
    output_out[...] = total[3 * rows : 4 * rows].T
    small = total[4 * rows :]
    _, heads, part = bias_out.shape
    for t in range(2):
        for h in range(heads):
            bias_out[t, h : h + 1, :] = small[7 + t : 8 + t, h * part : (h + 1) * part]
    expand_out[...] = small[6:7, : expand_out.shape[1]]
    count, lanes = vectors_out.shape
    found = jnp.zeros((count, lanes), f32)
    for i in range(rows // lanes):
        found = found + jnp.where(place[1] == i, small[:count, i * lanes : (i + 1) * lanes], 0.0)
    vectors_out[...] = found


def tokens_grad_kernel(n_fs, n_dp, *refs):
    index = own_place()
    parts, (dh, out) = refs[:n_fs], refs[n_fs:]
    out[...] = from_slots(dh[...] + sum_blocks(parts), index[0], n_dp)


def segment_kernel(n_fs, lengths, owners, allowed, live):
    place = own_place()
    size = live.shape[0]
    slot = lax.broadcasted_iota(jnp.int32, (8, size), 1)
    blocks = [place[0] * n_fs + (place[1] ^ i) for i in range(n_fs)]

    def add(s, carry):
        result = []
        for block, (offset, found) in zip(blocks, carry):
            count = jnp.where(owners[s] == block, lengths[s], 0)
            found = jnp.where((slot >= offset) & (slot < offset + count), s, found)
            result.append((offset + count, found))
        return tuple(result)

    start = tuple((jnp.int32(0), jnp.full((8, size), -1, jnp.int32)) for _ in blocks)
    for i, (_, found) in enumerate(lax.fori_loop(0, lengths.shape[0], add, start)):
        along = jnp.broadcast_to(found[0:1].astype(f32), (size, size))
        down = along.T
        allowed[i] = jnp.where((along == down) & (down >= 0.0), 1.0, 0.0)
        if i == 0:
            live[...] = jnp.where(down[:, 0:1] >= 0.0, 1.0, 0.0)


def prepare_kernel(parity, *refs):
    for source in refs[:5]:
        if isinstance(source, Late):
            source.ready()

    @pl.when(own_place()[0] % 2 == parity)
    def _():
        inner, slope = refs[0], refs[-5]
        chunk = min(256, inner.shape[1])
        for c in range(0, inner.shape[1], chunk):
            value = inner[:, c : c + chunk]
            cdf = 0.5 * (1.0 + lax.erf(value * root_half))
            density = jnp.exp(-0.5 * value * value) * inverse_root_tau
            slope[:, c : c + chunk] = (cdf + value * density).astype(bf16)
        for source, target in zip(refs[1:5], refs[-4:]):
            target[...] = source[...].T


def on_device(
    tokens,
    attend_weight,
    attend_bias,
    output_weight,
    expand_weight,
    expand_bias,
    contract_weight,
    layer_vectors,
    sequence_lengths,
    sequence_owner,
    output_grad,
):
    size, width = tokens.shape
    n_fs = lax.axis_size("fs")
    n_dp = lax.axis_size("dp")
    many = n_fs * size
    share = width // n_dp
    heads_width = attend_weight.shape[2]
    hidden_width = expand_weight.shape[1]
    n_vectors, lanes = layer_vectors.shape
    bias_shape = attend_bias.shape

    def send_back(parts):
        return [parts[0]] + [swap(parts[j], "fs", j) for j in range(1, n_fs)]

    (attend_part,) = kernel_call(
        pack_kernel,
        hot([shape_of((4 * share + small_rows, heads_width), bf16)]),
        Far(attend_weight),
        Far(output_weight),
        Far(attend_bias),
        Far(layer_vectors),
        Far(expand_bias),
        extra=56,
    )
    (own_rows,) = kernel_call(
        functools.partial(slots_kernel, n_dp), hot([shape_of((size + small_rows, width), bf16)]), Far(tokens)
    )
    inputs = gather_fs(own_rows)
    allowed, live = kernel_call(
        functools.partial(segment_kernel, n_fs),
        hot([shape_of((n_fs, size, size), f32), shape_of((size, 1), f32)]),
        sequence_lengths,
        sequence_owner,
    )
    attend_lane = gather_lane(attend_part)
    attend_parts = gather_cores(attend_lane)
    (feed_part,) = kernel_call(
        pair_kernel,
        [shape_of((2 * share, hidden_width), bf16)],
        Far(after(expand_weight, allowed, *inputs[1:])),
        Far(contract_weight),
    )
    feed_lane = gather_lane(after(feed_part, *attend_lane.values()))
    half_shape = shape_of((many, heads_width), bf16)
    n_scores = n_fs * heads_width // head_size
    (
        queries,
        key_rows,
        values,
        mixed,
        chances,
        expand_row,
        x_all,
        w_all,
        mixing,
        *branch_parts,
    ) = kernel_call(
        functools.partial(attend_kernel, n_fs, n_dp, bias_shape, expand_bias.size),
        [half_shape] * 4
        + [shape_of((n_scores, size, size), f32), Hot(shape_of((1, hidden_width), f32))]
        + [
            shape_of((many, width), bf16),
            shape_of((3, width, heads_width), bf16),
            shape_of((width, heads_width), bf16),
        ]
        + block_shapes(n_fs, size + small_rows, width),
        *hot(attend_parts),
        *hot(inputs),
        Hot(allowed),
        extra=4,
    )
    vectors, middle, middle_low, unit_first, inverse_first = kernel_call(
        functools.partial(first_norm_kernel, n_fs),
        hot(
            [
                shape_of((n_vectors, width), f32),
                shape_of((size, width), f32),
                shape_of((size, width), bf16),
                shape_of((size, width), f32),
                shape_of((size, 1), f32),
            ]
        ),
        *hot(send_back(branch_parts)),
        Hot(after(own_rows, *list(feed_lane.values())[1:-1])),
    )
    middles = gather_fs(middle_low)
    last = list(feed_lane)[-1]
    feed_parts = gather_cores({**feed_lane, last: after(feed_lane[last], *middles[1:])})
    wide = shape_of((many, hidden_width), bf16)
    w1, w2, mid_all, hidden, inner, *result_parts = kernel_call(
        functools.partial(feed_kernel, n_fs, n_dp),
        [
            shape_of((width, hidden_width), bf16),
            shape_of((width, hidden_width), bf16),
            shape_of((many, width), bf16),
            wide,
            Hot(shape_of((many, hidden_width), f32)),
        ]
        + block_shapes(n_fs, size, width),
        *hot(middles),
        *hot(feed_parts),
        Hot(expand_row),
        extra=3,
    )
    turned = hot(
        [wide, shape_of((hidden_width, many), bf16)]
        + [shape_of((width, many), bf16)] * 2
        + [shape_of((hidden_width, width), bf16)]
    )
    ready = kernel_call(
        functools.partial(prepare_kernel, 0), turned, Hot(inner), hidden, mid_all, x_all, w1
    )
    result_parts = [after(part, ready[0]) for part in result_parts]
    layer_output, dh2, dffn, sums_second = kernel_call(
        functools.partial(second_norm_kernel, n_fs, n_dp),
        [
            Far(shape_of((size, width), bf16)),
            Hot(shape_of((size, width), f32)),
            Hot(shape_of((size, width), bf16)),
            Hot(shape_of((3, width), f32)),
        ],
        *hot(send_back(result_parts)),
        Hot(middle),
        Hot(vectors),
        Far(output_grad),
        Hot(live),
        extra=3,
    )
    dffns = gather_fs(dffn)
    slope, hidden_turned, mid_turned, x_turned, w1_turned = kernel_call(
        functools.partial(prepare_kernel, 1),
        turned,
        Hot(inner),
        hidden,
        mid_all,
        x_all,
        w1,
        *hot([after(ready[0], dffn), *ready[1:]]),
        aliases={5: 0, 6: 1, 7: 2, 8: 3, 9: 4},
    )
    contract_slots = kernel_call(
        functools.partial(contract_grad_kernel, n_fs),
        hot([shape_of((n_dp // 2, hidden_width, share), bf16)] * 2),
        Hot(hidden_turned),
        *hot(dffns),
        extra=2,
    )
    du, expand_sums, *middle_parts = kernel_call(
        functools.partial(feed_back_kernel, n_fs),
        [wide, Hot(shape_of((1, hidden_width), f32))]
        + block_shapes(n_fs, size, width),
        *hot(dffns),
        w2,
        Hot(after(slope, contract_slots[0])),
        Hot(w1_turned),
        extra=3,
    )
    back_parts = send_back(middle_parts)
    def last_sum(shape):
        return lambda keep, taken: kernel_call(
            last_kernel, [Far(shape_of(shape, f32))], keep, taken
        )[0]

    contract_pair = sum_cores(*contract_slots)
    contract_last, contract_rounds = sum_lanes(*contract_pair, lambda keep, taken: (keep, taken))
    expand_slots = kernel_call(
        expand_grad_kernel,
        hot([shape_of((n_dp // 2, share, hidden_width), bf16)] * 2),
        after(du, contract_pair[1]),
        Hot(mid_turned),
        extra=2,
    )

    expand_pair = sum_cores(*expand_slots)
    expand_last, expand_rounds = sum_lanes(*expand_pair, lambda keep, taken: (keep, taken))
    dh1, dbranch = kernel_call(
        functools.partial(first_back_kernel, n_fs),
        hot([shape_of((size, width), f32), shape_of((size + small_rows, width), bf16)]),
        *hot(back_parts),
        Hot(after(dh2, expand_slots[0])),
        Hot(unit_first),
        Hot(inverse_first),
        Hot(vectors),
        Hot(sums_second),
    )
    branches = gather_fs(dbranch)
    dq, dk, dv = kernel_call(
        functools.partial(attend_back_kernel, n_fs),
        hot([half_shape] * 3),
        *hot(branches),
        after(mixing, expand_pair[1]),
        queries,
        key_rows,
        values,
        chances,
        extra=2.5,
    )
    attend_slots = kernel_call(
        functools.partial(attend_grad_kernel, n_fs, n_dp, bias_shape),
        hot([shape_of((n_dp // 2, 4 * share + small_rows, heads_width), bf16)] * 2),
        *hot(branches),
        Hot(after(x_turned, expand_rounds[-1], contract_last[1].array)),
        mixed,
        Hot(dq),
        Hot(dk),
        Hot(dv),
        Hot(expand_sums),
        extra=3,
    )
    keep, taken = (part.array for part in contract_last)
    contract_grad = last_sum(contract_weight.shape)(Hot(after(keep, attend_slots[0])), Hot(taken))
    attend_keep, attend_give = sum_cores(*attend_slots)
    input_parts = kernel_call(
        input_back_kernel,
        block_shapes(n_fs, size, width),
        after(w_all, attend_give),
        Hot(dq),
        Hot(dk),
        Hot(dv),
    )
    received = send_back(input_parts)
    small_outs = [
        shape_of(attend_bias.shape, f32),
        shape_of(expand_bias.shape, f32),
        shape_of(layer_vectors.shape, f32),
    ]
    sums, attend_rounds = sum_lanes(
        after(attend_keep, expand_last[1].array, *received[1:]),
        attend_give,
        lambda keep, taken: kernel_call(
            joint_kernel,
            [Far(shape_of(attend_weight.shape, f32)), Far(shape_of(output_weight.shape, f32))]
            + hot(small_outs),
            keep,
            taken,
        ),
    )
    attend_grad, output_weight_grad, attend_bias_grad, expand_bias_grad, vector_grad = sums
    keep, taken = (part.array for part in expand_last)
    expand_grad = last_sum(expand_weight.shape)(Hot(after(keep, attend_rounds[0])), Hot(taken))
    (tokens_grad,) = kernel_call(
        functools.partial(tokens_grad_kernel, n_fs, n_dp),
        [Far(shape_of((size, width), f32))],
        *hot(received),
        Hot(after(dh1, attend_rounds[0])),
    )
    return (
        layer_output,
        tokens_grad,
        attend_grad,
        attend_bias_grad,
        output_weight_grad,
        expand_grad,
        expand_bias_grad,
        contract_grad,
        vector_grad,
    )


def solution(mesh):
    in_specs = (
        P(("dp", "fs"), None),
        P(None, "dp", "fs"),
        P(None, "fs", "dp"),
        P("fs", "dp"),
        P("dp", "fs"),
        P("fs", "dp"),
        P("fs", "dp"),
        P(None, ("dp", "fs")),
        P(),
        P(),
        P(("dp", "fs"), None),
    )
    out_specs = (
        P(("dp", "fs"), None),
        P(("dp", "fs"), None),
        P(None, "dp", "fs"),
        P(None, "fs", "dp"),
        P("fs", "dp"),
        P("dp", "fs"),
        P("fs", "dp"),
        P("fs", "dp"),
        P(None, ("dp", "fs")),
    )
    return jax.shard_map(
        on_device, mesh=mesh, in_specs=in_specs, out_specs=out_specs, check_vma=False
    )
```
